128 devices in a mesh: gx: 8 (over z, core), gy: 16 (over x, y).
Axes of the slice: x: 4, y: 4, z: 4, core: 2. Of those that a mesh axis runs over, the one named last changes fastest.
Arguments:
- u_now: float32 [3, 40, 272, 256], P(None, 'gx', 'gy'), as said below
- load: float32 [3, 40, 272, 256], P(None, 'gx', 'gy'), may hold values from -6 to 6
- mass: float32 [40, 272, 256], P('gx', 'gy'), may hold values from 0.2 to 2
- modulus: float32 [32, 256, 256], P('gx', 'gy'), may hold values from 0.3 to 3
- plastic_ids: int32 [8, 16, 1024], P('gx', 'gy'), may hold values from 0 to 16383, as said below
- plastic_count: int32 [8, 16], P('gx', 'gy'), may hold values from 128 to 1024, as said below
- w_in: float32 [6, 512], replicated, may hold values from -2.5 to 2.5
- w_hidden: float32 [3, 512, 512], replicated, may hold values from -0.25 to 0.25
- w_head: float32 [512, 42], replicated, may hold values from -0.5 to 0.5
Outputs:
- increment: float32 [3, 40, 272, 256], P(None, 'gx', 'gy')
- cg_residual: float32 [3, 40, 272, 256], P(None, 'gx', 'gy')
The draws below stay inside these ranges and needn't reach their ends.
Inputs may be any that keep to these rules, and one draw needn't show every extreme that they name: `u_now`: copies of one node in neighbouring blocks are equal, and nodes of the planes I = 32 and J = 256 are zero. `plastic_ids`: the entries of one block are distinct element indices of that block. `plastic_count`: some block holds 1024 live points in every draw.
All inputs are finite; a program needn't handle non-finite values.
Results may differ from the reference program's by a relative error of at most 0.0003.
Values sent between devices are 32-bit elements; how exact they have to be, the bound alone decides.
A program may use at most 128 MiB of HBM per device.

```python
import math
import jax
import jax.numpy as jnp
from jax import lax

EX = 4
EY = 16
EZ = 256
PMAX = 1024
HID = 512
LAYERS = 4
ITERS = 6
NX = 32
NY = 256
NXD = 40
NYD = 272
ELEMS = 16384
BLOCKS_X = 8
BLOCKS_Y = 16
N_GX = 8
N_GY = 16


def draw_u_now(key, part):
    key = jax.random.fold_in(key, 11)
    shape = (3, NX + 1, NY + 1, EZ)
    unique = 0.5 * jax.random.normal(key, shape, jnp.float32)
    keep_x = (jnp.arange(NX + 1) < NX).astype(jnp.float32)
    keep_y = (jnp.arange(NY + 1) < NY).astype(jnp.float32)
    unique = unique * keep_x[None, :, None, None] * keep_y[None, None, :, None]
    dup_x = jnp.arange((EX + 1) * BLOCKS_X, dtype=jnp.int32)
    glob_x = dup_x // (EX + 1) * EX + dup_x % (EX + 1)
    dup_y = jnp.arange((EY + 1) * BLOCKS_Y, dtype=jnp.int32)
    glob_y = dup_y // (EY + 1) * EY + dup_y % (EY + 1)
    return jnp.take(jnp.take(unique, glob_x, axis=1), glob_y, axis=2).astype(jnp.float32)


def draw_plastic_ids(key, part):
    key = jax.random.fold_in(key, 37)
    keys = jax.random.split(key, BLOCKS_X * BLOCKS_Y)
    picks = jax.vmap(lambda single: jax.random.permutation(single, ELEMS)[:PMAX])(keys)
    return picks.reshape(BLOCKS_X, BLOCKS_Y, PMAX).astype(jnp.int32)


def draw_plastic_count(key, part):
    key = jax.random.fold_in(key, 23)
    first, second = jax.random.split(key)
    counts = jax.random.randint(first, (BLOCKS_X * BLOCKS_Y,), PMAX // 8, PMAX // 2 + 1)
    busiest = jax.random.randint(second, (), 0, BLOCKS_X * BLOCKS_Y)
    counts = jnp.where(jnp.arange(BLOCKS_X * BLOCKS_Y) == busiest, PMAX, counts)
    return counts.reshape(BLOCKS_X, BLOCKS_Y).astype(jnp.int32)


def block_levels(stream_key, shape, cuts, least, top_value):
    loudness = 1.0
    for axis_at, blocks in cuts:
        heights = jax.random.uniform(jax.random.fold_in(jax.random.fold_in(stream_key, 6), axis_at), (blocks,), jnp.float32, least / len(cuts), top_value / len(cuts))
        loudness = loudness * jnp.repeat(jnp.exp(heights), shape[axis_at] // blocks).reshape((-1,) + (1,) * (len(shape) - 1 - axis_at))
    return loudness


def gaussian(own_key, shape, scale, bound, cuts=(), held_as=jnp.bfloat16):
    drawn = scale * jax.random.normal(own_key, shape, jnp.float32)
    if cuts:
        drawn = drawn * block_levels(own_key, shape, cuts, -0.22, 0.18)
    return jnp.clip(drawn, -bound, bound).astype(held_as)


def setup_inputs(seed: int = 0) -> dict:
    arg_keys = jax.random.split(jax.random.key(seed), 10)
    return {
        "u_now": draw_u_now(jax.random.fold_in(arg_keys[9], 71), 0),
        "load": gaussian(arg_keys[1], (3, NXD, NYD, EZ), 1.0, 6.0, ((1, 8), (2, 16)), jnp.float32),
        "mass": jnp.clip(jnp.exp(math.log(2.0) - 2.3025851 * jax.random.uniform(arg_keys[2], (NXD, NYD, EZ), jnp.float32) ** block_levels(arg_keys[2], (NXD, NYD, EZ), ((0, 8), (1, 16)), -0.2, 0.2)), 0.2, 2.0),
        "modulus": jnp.clip(jnp.exp(math.log(3.0) - 2.3025851 * jax.random.uniform(arg_keys[3], (NX, NY, EZ), jnp.float32) ** block_levels(arg_keys[3], (NX, NY, EZ), ((0, 8), (1, 16)), -0.2, 0.2)), 0.3, 3.0),
        "plastic_ids": draw_plastic_ids(jax.random.fold_in(arg_keys[9], 71), 0),
        "plastic_count": draw_plastic_count(jax.random.fold_in(arg_keys[9], 71), 0),
        "w_in": gaussian(arg_keys[6], (6, HID), 6 ** -0.5, 2.5, (), jnp.float32),
        "w_hidden": gaussian(arg_keys[7], (LAYERS - 1, HID, HID), HID ** -0.5, 0.25, (), jnp.float32),
        "w_head": gaussian(arg_keys[8], (HID, 42), (HID // 4) ** -0.5, 0.5, (), jnp.float32),
    }


lame_first = 0.3 / (1.3 * 0.4)
lame_second = 1.0 / 2.6
highest = lax.Precision.HIGHEST

def pair_mean(values, dim):
    length = values.shape[dim]
    return 0.5 * (lax.slice_in_dim(values, 0, length - 1, axis=dim) + lax.slice_in_dim(values, 1, length, axis=dim))

def pair_diff(values, dim):
    length = values.shape[dim]
    return lax.slice_in_dim(values, 1, length, axis=dim) - lax.slice_in_dim(values, 0, length - 1, axis=dim)

def strain_of(field):
    padded = jnp.pad(field, ((0, 0), (0, 0), (0, 0), (0, 1)))
    grad_x = pair_mean(pair_mean(pair_diff(padded, 1), 2), 3)
    grad_y = pair_mean(pair_mean(pair_diff(padded, 2), 1), 3)
    grad_z = pair_mean(pair_mean(pair_diff(padded, 3), 1), 2)
    parts = [grad_x[0], grad_y[1], grad_z[2], grad_z[1] + grad_y[2], grad_z[0] + grad_x[2], grad_y[0] + grad_x[1]]
    return jnp.stack(parts).reshape(6, -1)

def iso_matrix():
    upper = lame_first * jnp.ones((3, 3), jnp.float32) + 2.0 * lame_second * jnp.eye(3, dtype=jnp.float32)
    lower = lame_second * jnp.eye(3, dtype=jnp.float32)
    zeros = jnp.zeros((3, 3), jnp.float32)
    return jnp.concatenate([jnp.concatenate([upper, zeros], 1), jnp.concatenate([zeros, lower], 1)], 0)

def elastic_stress(strain, moduli):
    trace = strain[0] + strain[1] + strain[2]
    normal = lame_first * trace[None] + 2.0 * lame_second * strain[:3]
    shear = lame_second * strain[3:]
    return moduli[None] * jnp.concatenate([normal, shear], 0)

def contract(weights, values):
    return lax.dot_general(weights, values, (((0,), (0,)), ((), ())), precision=highest, preferred_element_type=jnp.float32)

def surrogate(inputs, w_in, w_hidden, w_head):
    hidden = jnp.tanh(contract(w_in, inputs))
    for layer in range(w_hidden.shape[0]):
        hidden = jnp.tanh(contract(w_hidden[layer], hidden))
    return contract(w_head, hidden)

def plastic_laws(outputs, eps_plastic, modulus_plastic):
    iso = iso_matrix()
    stress_plastic = modulus_plastic[None] * (0.25 * jnp.dot(iso, eps_plastic, precision=highest) + outputs[:6])
    factor = outputs[6:].reshape(6, 6, -1)
    outer = jnp.einsum('ikp,jkp->ijp', factor, factor, precision=highest)
    tangent = modulus_plastic[None, None] * (0.25 * iso[:, :, None] + outer / 6.0)
    return (stress_plastic, tangent)

def reference(u_now, load, mass, modulus, plastic_ids, plastic_count, w_in, w_hidden, w_head):
    dup_x = jnp.arange((EX + 1) * N_GX, dtype=jnp.int32)
    glob_x = (dup_x // (EX + 1) * EX + dup_x % (EX + 1)).astype(jnp.int32)
    dup_y = jnp.arange((EY + 1) * N_GY, dtype=jnp.int32)
    glob_y = (dup_y // (EY + 1) * EY + dup_y % (EY + 1)).astype(jnp.int32)
    uniq_x = jnp.arange(NX + 1, dtype=jnp.int32)
    block_x = jnp.minimum(uniq_x // EX, N_GX - 1)
    pick_x = (block_x * (EX + 1) + uniq_x - block_x * EX).astype(jnp.int32)
    uniq_y = jnp.arange(NY + 1, dtype=jnp.int32)
    block_y = jnp.minimum(uniq_y // EY, N_GY - 1)
    pick_y = (block_y * (EY + 1) + uniq_y - block_y * EY).astype(jnp.int32)

    def to_unique(field):
        return jnp.take(jnp.take(field, pick_x, axis=1), pick_y, axis=2)

    def add_copies(field):
        summed = jax.ops.segment_sum(jnp.moveaxis(field, 1, 0), glob_x, num_segments=NX + 1)
        summed = jnp.moveaxis(summed, 0, 1)
        summed = jax.ops.segment_sum(jnp.moveaxis(summed, 2, 0), glob_y, num_segments=NY + 1)
        return jnp.moveaxis(summed, 0, 2)

    def to_blocks(field):
        return jnp.take(jnp.take(field, glob_x, axis=1), glob_y, axis=2)
    keep = ((uniq_x < NX)[:, None] & (uniq_y < NY)[None, :]).astype(jnp.float32)[None, :, :, None]
    load_u = add_copies(load)
    mass_u = add_copies(mass[None])
    moduli = modulus.reshape(-1)
    local_i = plastic_ids // (EY * EZ)
    local_j = plastic_ids // EZ % EY
    local_k = plastic_ids % EZ
    index_bx = jnp.arange(N_GX, dtype=jnp.int32)[:, None, None]
    index_by = jnp.arange(N_GY, dtype=jnp.int32)[None, :, None]
    gid = (((index_bx * EX + local_i) * NY + index_by * EY + local_j) * EZ + local_k).reshape(-1).astype(jnp.int32)
    live = (jnp.arange(PMAX, dtype=jnp.int32)[None, None, :] < plastic_count[:, :, None]).reshape(-1).astype(jnp.float32)
    u_unique = to_unique(u_now)
    strain_now = strain_of(u_unique)
    eps_plastic = jnp.take(strain_now, gid, axis=1)
    modulus_plastic = jnp.take(moduli, gid)
    blocks = eps_plastic.reshape(6, N_GX * N_GY, PMAX).transpose(1, 0, 2)
    answers = lax.map(lambda single: surrogate(single, w_in, w_hidden, w_head), blocks)
    outputs = answers.transpose(1, 0, 2).reshape(42, -1)
    stress_plastic, tangent = plastic_laws(outputs, eps_plastic, modulus_plastic)

    def stress_of(strain, plastic_value):
        base = elastic_stress(strain, moduli)
        change = live[None] * (plastic_value - jnp.take(base, gid, axis=1))
        return base.at[:, gid].add(change)
    _, pull_back = jax.vjp(strain_of, u_unique)

    def forces(stress):
        return pull_back(stress)[0]
    residual = keep * (load_u - forces(stress_of(strain_now, stress_plastic)))

    def apply(direction):
        strain = strain_of(direction)
        local = jnp.einsum('ijp,jp->ip', tangent, jnp.take(strain, gid, axis=1), precision=highest)
        return keep * (forces(stress_of(strain, local)) + mass_u * direction)
    increment = jnp.zeros_like(residual)
    direction = residual
    norm_now = jnp.sum(residual * residual)
    for step in range(ITERS):
        image = apply(direction)
        alpha = norm_now / jnp.sum(direction * image)
        increment = increment + alpha * direction
        residual = residual - alpha * image
        norm_next = jnp.sum(residual * residual)
        direction = residual + norm_next / norm_now * direction
        norm_now = norm_next
    return (to_blocks(increment), to_blocks(residual))
```

```python
import jax
import jax.numpy as jnp
from jax import lax
from jax.experimental import pallas as pl
from jax.experimental.pallas import tpu as pltpu
from jax.sharding import PartitionSpec as P

MESH = pl.DeviceIdType.MESH
F32, BF16 = jnp.float32, jnp.bfloat16
LAME_FIRST = 0.3 / (1.3 * 0.4)
LAME_SECOND = 1.0 / 2.6

BX, BY, NZ = 4, 16, 256
NODES_X, NODES_Y = BX + 1, BY + 1
ROWS = BY + 3
SUB = 8
SLOTS, HID, HIDDEN_LAYERS = 1024, 512, 3
COLUMNS = BY * BX
OUTER = 3
CHUNK = 256
GROUP = 7

PAIRS = [(a, b) for a in range(6) for b in range(a, 6)]
PAIR_OF = {}
for _at, (_a, _b) in enumerate(PAIRS):
    PAIR_OF[_a, _b] = PAIR_OF[_b, _a] = _at
N_PAIRS = len(PAIRS)
N_SCATTER = 28

DIRECTIONS = [(dx, dy) for dx in (-1, 0, 1) for dy in (-1, 0, 1) if (dx, dy) != (0, 0)]


def iso(a, b):
    if a < 3 and b < 3:
        return LAME_FIRST + (2.0 * LAME_SECOND if a == b else 0.0)
    return LAME_SECOND if a == b else 0.0


def z_next(values):
    lane = lax.broadcasted_iota(jnp.int32, values.shape, 1)
    return jnp.where(lane == NZ - 1, 0.0, pltpu.roll(values, NZ - 1, 1))


def z_prev(values):
    lane = lax.broadcasted_iota(jnp.int32, values.shape, 1)
    return jnp.where(lane == 0, 0.0, pltpu.roll(values, 1, 1))


def x_pairs(values):
    upper = pltpu.roll(values, SUB - 1, 0)
    return upper + values, upper - values


def strain_row(low, high):
    a = [low[m][1] + high[m][1] for m in range(3)]
    b = [high[m][0] - low[m][0] for m in range(3)]
    c = [high[m][0] + low[m][0] for m in range(3)]
    yz, xz, xy = c[1] + b[2], c[0] + a[2], b[0] + a[1]
    return [
        z_next(a[0]) + a[0],
        z_next(b[1]) + b[1],
        z_next(c[2]) - c[2],
        z_next(yz) + (b[2] - c[1]),
        z_next(xz) + (a[2] - c[0]),
        z_next(xy) + xy,
    ]


def force_parts(stress):
    before = [z_prev(s) for s in stress]
    total = {n: stress[n] + before[n] for n in (0, 1, 3, 4, 5)}
    differ = {n: before[n] - stress[n] for n in (2, 3, 4)}
    parts = []
    for along_x, along_y, along_z in ((0, 5, 4), (5, 1, 3), (4, 3, 2)):
        parts.append(
            (
                total[along_x],
                differ[along_z] - total[along_y],
                differ[along_z] + total[along_y],
            )
        )
    return parts


def force_of(along_x, other):
    return pltpu.roll(along_x + other, 1, 0) + (other - along_x)


def split(values):
    high = values.astype(BF16)
    return high, (values - high.astype(F32)).astype(BF16)


def mm(a, b):
    return jnp.dot(a, b, preferred_element_type=F32)


def face(dx, dy, depth):
    if depth == 2:
        sx = {-1: slice(1, 3), 0: slice(1, 6), 1: slice(4, 6)}[dx]
        tx = {-1: slice(5, 7), 0: slice(1, 6), 1: slice(0, 2)}[dx]
        sy = {-1: slice(1, 3), 0: slice(1, 18), 1: slice(16, 18)}[dy]
        ty = {-1: slice(17, 19), 0: slice(1, 18), 1: slice(0, 2)}[dy]
    else:
        sx = {-1: slice(2, 3), 0: slice(1, 6), 1: slice(4, 5)}[dx]
        tx = {-1: slice(6, 7), 0: slice(1, 6), 1: slice(0, 1)}[dx]
        sy = {-1: slice(2, 3), 0: slice(1, 18), 1: slice(16, 17)}[dy]
        ty = {-1: slice(18, 19), 0: slice(1, 18), 1: slice(0, 1)}[dy]
    return sy, sx, ty, tx


def element_face(dx, dy):
    sx = {-1: slice(1, 2), 0: slice(1, 5), 1: slice(4, 5)}[dx]
    tx = {-1: slice(5, 6), 0: slice(1, 5), 1: slice(0, 1)}[dx]
    sy = {-1: slice(0, 1), 0: slice(0, 16), 1: slice(15, 16)}[dy]
    ty = {-1: slice(17, 18), 0: slice(1, 17), 1: slice(0, 1)}[dy]
    return sy, sx, ty, tx


def kernel(
    size_x, size_y,
    u_hbm, load_hbm, mass_hbm, modulus_hbm, ids_ref, count_ref, w_in_ref, w_hidden_hbm, w_head_ref,
    increment_hbm, residual_hbm,
    ux, lx, mass_part, mass_full, mass_rx, modulus, weights,
    strain_now, onehot_k, onehot_kt, onehot_r, onehot_r8, inputs_t, out_t, values, lhs, scattered,
    own_tangent, tangent, tangent_rx,
    v0, v1, v2, q1, q0, d1, x, sum_rx, copy_rx, gathered,
    load_sem, out_sem, mass_send, mass_recv, tan_send, tan_recv,
    sum_send, sum_recv, copy_send, copy_recv, all_send, all_recv,
):
    index_x, index_y = lax.axis_index("gx"), lax.axis_index("gy")
    me = index_x * size_y + index_y
    peers = size_x * size_y
    neighbours = [
        (lax.rem(index_x + dx + size_x, size_x), lax.rem(index_y + dy + size_y, size_y))
        for dx, dy in DIRECTIONS
    ]

    def peer(step):
        other = lax.rem(me + step, peers)
        return (other // size_y, lax.rem(other, size_y))

    barrier = pltpu.get_barrier_semaphore()

    def greet(step, carry):
        pl.semaphore_signal(barrier, inc=1, device_id=peer(step), device_id_type=MESH)
        return carry

    lax.fori_loop(1, peers, greet, 0)

    for ref in (ux, lx, mass_part, modulus):
        ref[...] = jnp.zeros_like(ref)
    loads = []
    for i in range(NODES_X):
        loads.append(pltpu.make_async_copy(u_hbm.at[:, i], ux.at[:, 1:18, i + 1], load_sem.at[0, i]))
    for i in range(BX):
        loads.append(pltpu.make_async_copy(modulus_hbm.at[i], modulus.at[:, i + 1], load_sem.at[1, i]))
    for i in range(NODES_X):
        loads.append(pltpu.make_async_copy(mass_hbm.at[i], mass_part.at[1:18, i + 1], load_sem.at[2, i]))
        loads.append(pltpu.make_async_copy(load_hbm.at[:, i], lx.at[:, 1:18, i + 1], load_sem.at[3, i]))
    for layer in range(HIDDEN_LAYERS):
        loads.append(pltpu.make_async_copy(w_hidden_hbm.at[layer], weights.at[layer], load_sem.at[4, layer]))
    for copy in loads:
        copy.start()
    for ref in (q1, q0, d1, x):
        ref[...] = jnp.zeros_like(ref)

    ids = ids_ref[...]
    slot = lax.broadcasted_iota(jnp.int32, (1, SLOTS), 1)
    live = jnp.where(slot < count_ref[0, 0], 1.0, 0.0)
    at_k = ids & (NZ - 1)
    at_j = (ids >> 8) & (BY - 1)
    at_i = ids >> 12
    onehot_k[...] = jnp.where(
        lax.broadcasted_iota(jnp.int32, (NZ, SLOTS), 0) == at_k, 1.0, 0.0
    ).astype(BF16)
    onehot_r[...] = jnp.where(
        lax.broadcasted_iota(jnp.int32, (COLUMNS, SLOTS), 0) == at_j * BX + at_i, live, 0.0
    ).astype(BF16)
    onehot_r8[...] = jnp.where(
        lax.broadcasted_iota(jnp.int32, (BY * SUB, SLOTS), 0) == at_j * SUB + at_i + 1, 1.0, 0.0
    )
    k_column = jnp.broadcast_to(at_k.astype(F32), (128, SLOTS)).T
    lane_k = lax.broadcasted_iota(jnp.int32, (SLOTS, 128), 1).astype(F32)
    onehot_kt[:, 0:128] = jnp.where(k_column == lane_k, 1.0, 0.0).astype(BF16)
    onehot_kt[:, 128:256] = jnp.where(k_column == lane_k + 128.0, 1.0, 0.0).astype(BF16)

    for copy in loads:
        copy.wait()

    def pairs_of(ref, row):
        return [x_pairs(ref[m, row]) for m in range(3)]

    def strain_step(row, low):
        high = pairs_of(ux, row + 1)
        for n, value in enumerate(strain_row(low, high)):
            strain_now[n, row - 1] = 0.25 * value
        return high

    lax.fori_loop(1, 1 + BY, strain_step, pairs_of(ux, 1))

    picked = []
    for n in range(6):
        high, low = split(strain_now[n].reshape(BY * SUB, NZ))
        rows = mm(high, onehot_k[...]) + mm(low, onehot_k[...])
        picked.append(jnp.sum(rows * onehot_r8[...], axis=0, keepdims=True))
    eps = jnp.concatenate(picked + [jnp.zeros((2, SLOTS), F32)], axis=0)
    eps_high = eps.astype(BF16).astype(F32)
    stacked = jnp.concatenate(
        [eps_high, eps - eps_high, eps_high, jnp.zeros((104, SLOTS), F32)], axis=0
    )
    inputs_t[...] = stacked.T.astype(BF16)

    w_in = jnp.concatenate([w_in_ref[...], jnp.zeros((2, HID), F32)], axis=0)
    w_in_high = w_in.astype(BF16).astype(F32)
    w_first = jnp.concatenate(
        [w_in_high, w_in_high, w_in - w_in_high, jnp.zeros((104, HID), F32)], axis=0
    ).astype(BF16)
    from_out = lax.broadcasted_iota(jnp.int32, (42, 128), 0)
    to_lane = lax.broadcasted_iota(jnp.int32, (42, 128), 1)
    place = jnp.where(
        (from_out == (to_lane // 8) * 6 + to_lane % 8) & (to_lane % 8 < 6) & (to_lane < 56), 1.0, 0.0
    ).astype(BF16)
    head_high, head_low = split(w_head_ref[...])
    head_high = mm(head_high, place).astype(BF16)
    head_low = mm(head_low, place).astype(BF16)
    halves = [split(weights[layer]) for layer in range(HIDDEN_LAYERS)]

    def surrogate_chunk(at, carry):
        start = pl.multiple_of(at * CHUNK, CHUNK)
        hidden = jnp.tanh(mm(inputs_t[pl.ds(start, CHUNK)], w_first))
        for w_high, w_low in halves:
            high, low = split(hidden)
            hidden = jnp.tanh(mm(high, w_high) + (mm(low, w_high) + mm(high, w_low)))
        high, low = split(hidden)
        out = mm(high, head_high) + (mm(low, head_high) + mm(high, head_low))
        out_t[:, pl.ds(start, CHUNK)] = out.T
        return carry

    lax.fori_loop(0, SLOTS // CHUNK, surrogate_chunk, 0)

    pl.semaphore_wait(barrier, peers - 1)
    mass_copies = []
    for q, ((dx, dy), device) in enumerate(zip(DIRECTIONS, neighbours)):
        sy, sx, ty, tx = face(dx, dy, 2)
        kind = 0 if dy == 0 else (1 if dx == 0 else 2)
        copy = pltpu.make_async_remote_copy(
            mass_part.at[sy, sx], mass_rx.at[kind, ty, tx], mass_send.at[q], mass_recv.at[q],
            device_id=device, device_id_type=MESH,
        )
        copy.start()
        mass_copies.append(copy)

    factor = [out_t[8 * (a + 1) : 8 * (a + 2)] for a in range(6)]
    for at, (a, b) in enumerate(PAIRS):
        values[at : at + 1] = jnp.sum(factor[a] * factor[b], axis=0, keepdims=True) * (1.0 / 6.0)
    values[N_PAIRS : N_PAIRS + 6] = out_t[0:6]
    values[N_SCATTER - 1 : N_SCATTER] = jnp.ones((1, SLOTS), F32)

    def scatter_group(at, carry):
        for n in range(GROUP):
            high, low = split(values[pl.ds(at * GROUP + n, 1)])
            rows = onehot_r[...]
            lhs[n * COLUMNS : (n + 1) * COLUMNS] = rows * high
            lhs[(GROUP + n) * COLUMNS : (GROUP + n + 1) * COLUMNS] = rows * low
        spread = mm(lhs[...], onehot_kt[...])
        spread = spread[: GROUP * COLUMNS] + spread[GROUP * COLUMNS :]
        sub = lax.broadcasted_iota(jnp.int32, (SUB, NZ), 0)
        inside = (sub >= 1) & (sub <= BX)
        for n in range(GROUP):
            for g in range(BY // 2):
                start = n * COLUMNS + g * SUB
                both = spread[start : start + SUB]
                scattered[at * GROUP + n, 2 * g] = jnp.where(inside, pltpu.roll(both, 1, 0), 0.0)
                scattered[at * GROUP + n, 2 * g + 1] = jnp.where(inside, pltpu.roll(both, 5, 0), 0.0)
        return carry

    lax.fori_loop(0, N_SCATTER // GROUP, scatter_group, 0)

    def tangent_row(row, carry):
        scale = modulus[row]
        base = scale * (1.0 - 0.75 * scattered[N_SCATTER - 1, row])
        for at, (a, b) in enumerate(PAIRS):
            entry = scale * scattered[at, row]
            if iso(a, b):
                entry = entry + base * iso(a, b)
            own_tangent[at, row] = entry * (1.0 / 16.0)
        return carry

    lax.fori_loop(0, BY, tangent_row, 0)

    tangent_copies = []
    for q, ((dx, dy), device) in enumerate(zip(DIRECTIONS, neighbours)):
        sy, sx, ty, tx = element_face(dx, dy)
        copy = pltpu.make_async_remote_copy(
            own_tangent.at[:, sy, sx], tangent_rx.at[:, ty, tx], tan_send.at[q], tan_recv.at[q],
            device_id=device, device_id_type=MESH,
        )
        copy.start()
        tangent_copies.append(copy)

    def sum_copies(parity):
        copies = []
        for q, ((dx, dy), device) in enumerate(zip(DIRECTIONS, neighbours)):
            sy, sx, ty, tx = face(dx, dy, 2)
            kind = 0 if dy == 0 else (1 if dx == 0 else 2)
            copies.append(
                pltpu.make_async_remote_copy(
                    v2.at[:, sy, sx], sum_rx.at[parity, kind, :, ty, tx],
                    sum_send.at[parity, q], sum_recv.at[parity, q],
                    device_id=device, device_id_type=MESH,
                )
            )
        return copies

    def exact_copies(parity):
        copies = []
        for q, ((dx, dy), device) in enumerate(zip(DIRECTIONS, neighbours)):
            sy, sx, ty, tx = face(dx, dy, 1)
            copies.append(
                pltpu.make_async_remote_copy(
                    v1.at[:, sy, sx], copy_rx.at[parity, :, ty, tx],
                    copy_send.at[parity, q], copy_recv.at[parity, q],
                    device_id=device, device_id_type=MESH,
                )
            )
        return copies

    sub = lax.broadcasted_iota(jnp.int32, (SUB, NZ), 0)
    global_x = index_x * BX + sub - 1
    keep_x = jnp.where(
        (global_x >= 0) & (global_x < size_x * BX) & (sub < SUB - 1), 1.0, 0.0
    )
    own_planes = (sub >= 1) & (sub <= NODES_X)
    rim_planes = ((sub <= 1) & (index_x > 0)) | ((sub >= NODES_X) & (sub <= NODES_X + 1))
    all_planes = sub <= NODES_X + 1

    def keep_of(row):
        global_y = index_y * BY + row - 1
        inside = jnp.where((global_y >= 0) & (global_y < size_y * BY), 1.0, 0.0)
        return keep_x * inside

    def assembled(part, side, flank, corner, row):
        own_row = (row >= 1) & (row <= NODES_Y)
        rim_row = ((row <= 1) & (index_y > 0)) | (row >= NODES_Y)
        total = jnp.where(own_planes & own_row, part, 0.0)
        total = total + jnp.where(rim_planes & own_row, side, 0.0)
        total = total + jnp.where(own_planes & rim_row, flank, 0.0)
        return total + jnp.where(rim_planes & rim_row, corner, 0.0)

    def stress_now(row):
        scale = 0.25 * modulus[row]
        base = scale * (1.0 - 0.75 * scattered[N_SCATTER - 1, row])
        eps_row = [strain_now[n, row] for n in range(6)]
        trace = LAME_FIRST * (eps_row[0] + eps_row[1] + eps_row[2])
        elastic = [trace + 2.0 * LAME_SECOND * eps_row[n] for n in range(3)]
        elastic += [LAME_SECOND * eps_row[n] for n in range(3, 6)]
        return [base * elastic[n] + scale * scattered[N_PAIRS + n, row] for n in range(6)]

    zero = jnp.zeros((SUB, NZ), F32)
    no_parts = [(zero, zero)] * 3

    def residual_step(row, before):
        parts = force_parts(stress_now(row - 1))
        for m in range(3):
            force = force_of(parts[m][0] + before[m][0], parts[m][1] + before[m][1])
            v2[m, row] = lx[m, row] - force
        return [(parts[m][0], parts[m][2]) for m in range(3)]

    last = lax.fori_loop(1, 1 + BY, residual_step, no_parts)
    for m in range(3):
        v2[m, NODES_Y] = lx[m, NODES_Y] - force_of(*last[m])

    first_copies = sum_copies(0)
    for copy in first_copies:
        copy.start()
    for copy in mass_copies:
        copy.wait()

    def mass_row(row, carry):
        mass_full[row] = assembled(
            mass_part[row], mass_rx[0, row], mass_rx[1, row], mass_rx[2, row], row
        )
        return carry

    lax.fori_loop(0, ROWS, mass_row, 0)
    for copy in first_copies:
        copy.wait()

    def start_row(row, carry):
        keep = keep_of(row)
        for m in range(3):
            v0[m, row] = keep * assembled(
                v2[m, row], sum_rx[0, 0, m, row], sum_rx[0, 1, m, row], sum_rx[0, 2, m, row], row
            )
        return carry

    lax.fori_loop(0, ROWS, start_row, 0)
    for copy in tangent_copies:
        copy.wait()

    def merge_row(row, carry):
        own_row = (row >= 1) & (row <= BY)
        own = (sub >= 1) & (sub <= BX) & own_row
        inside = (global_x >= 0) & (sub <= BX + 1) & (index_y * BY + row - 1 >= 0)
        from_row = jnp.clip(row - 1, 0, BY - 1)
        for at in range(N_PAIRS):
            entry = jnp.where(own, own_tangent[at, from_row], tangent_rx[at, row])
            tangent[at, row] = jnp.where(inside, entry, 0.0)
        return carry

    lax.fori_loop(0, BY + 2, merge_row, 0)

    def stress_row(ref, row, strain):
        entries = [ref[at, row] for at in range(N_PAIRS)]
        result = []
        for a in range(6):
            total = entries[PAIR_OF[a, 0]] * strain[0]
            for b in range(1, 6):
                total = total + entries[PAIR_OF[a, b]] * strain[b]
            result.append(total)
        return result

    def first_image(row, carry):
        low, before = carry
        high = pairs_of(v0, row + 1)
        parts = force_parts(stress_row(tangent, row, strain_row(low, high)))

        @pl.when(row > 0)
        def _():
            keep = keep_of(row)
            for m in range(3):
                force = force_of(parts[m][0] + before[m][0], parts[m][1] + before[m][1])
                v1[m, row] = keep * (force + mass_full[row] * v0[m, row])

        return high, [(parts[m][0], parts[m][2]) for m in range(3)]

    def second_image(row, carry):
        low, before, sums = carry
        high = pairs_of(v1, row + 1)
        parts = force_parts(stress_row(own_tangent, row - 1, strain_row(low, high)))
        rr, r_ar, ar_ar, ar_aar = sums
        for m in range(3):
            here, image = v0[m, row], v1[m, row]
            force = force_of(parts[m][0] + before[m][0], parts[m][1] + before[m][1])
            force = force + mass_part[row] * image
            v2[m, row] = force
            rr = rr + here * here
            r_ar = r_ar + here * image
            ar_ar = ar_ar + image * image
            ar_aar = ar_aar + image * force
        return high, [(parts[m][0], parts[m][2]) for m in range(3)], (rr, r_ar, ar_ar, ar_aar)

    unique_planes = (sub >= 1) & (sub <= BX)
    lane = lax.broadcasted_iota(jnp.int32, (1, 128), 1)

    def outer(step, carry):
        be0, ia1, ia0, rr_before = carry
        parity = lax.rem(step, 2)
        sum_parity = lax.rem(step + 1, 2)
        lax.fori_loop(0, BY + 2, first_image, (pairs_of(v0, 0), no_parts))
        exact = exact_copies(parity)
        for copy in exact:
            copy.start()
        _, before, sums = lax.fori_loop(
            1, 1 + BY, second_image, (pairs_of(v1, 1), no_parts, (zero,) * 4)
        )
        ar_aar = sums[3]
        for m in range(3):
            image = v1[m, NODES_Y]
            force = force_of(*before[m]) + mass_part[NODES_Y] * image
            v2[m, NODES_Y] = force
            ar_aar = ar_aar + jnp.where(own_planes, image * force, 0.0)
        summed = sum_copies(sum_parity)
        for copy in summed:
            copy.start()

        message = jnp.zeros((1, 128), F32)
        for at, (value, mask) in enumerate(
            ((sums[0], unique_planes), (sums[1], unique_planes), (sums[2], unique_planes), (ar_aar, own_planes))
        ):
            total = jnp.sum(jnp.where(mask, value, 0.0), axis=0, keepdims=True)
            total = jnp.sum(total, axis=1, keepdims=True)
            message = message + jnp.where(lane == at, total, 0.0)
        gathered[parity, me] = message

        def tell(other, unused):
            pltpu.make_async_remote_copy(
                gathered.at[parity, me], gathered.at[parity, me],
                all_send.at[parity], all_recv.at[parity],
                device_id=peer(other), device_id_type=MESH,
            ).start()
            return unused

        lax.fori_loop(1, peers, tell, 0)
        for copy in exact + summed:
            copy.wait()
        rest = gathered.at[parity, 0 : peers - 1]
        pltpu.make_async_copy(rest, rest, all_recv.at[parity]).wait()
        totals = jnp.sum(gathered[parity], axis=0)
        rr2, m1, m2, m3 = [
            jnp.sum(jnp.where(lane == at, totals, 0.0), axis=1, keepdims=True) for at in range(4)
        ]
        be1 = jnp.where(step == 0, 0.0, rr2 / rr_before)
        r_q1 = -rr2 * ia1
        ar_q1 = (r_q1 - m1) * ia1
        q1_q1 = (rr_before + rr2) * ia1 * ia1
        ar_q0 = rr2 * ia1 * ia0
        q1_q0 = -rr_before * ia1 * ia0
        q1_aar = ia1 * (ar_q1 - be0 * ar_q0 - m2)
        q1_aq1 = ia1 * (q1_q1 - be0 * q1_q0 - ar_q1)
        q2_q2 = m2 + 2.0 * be1 * ar_q1 + be1 * be1 * q1_q1
        ar_q2 = m2 + be1 * ar_q1
        q2_aq2 = m3 + 2.0 * be1 * q1_aar + be1 * be1 * q1_aq1
        a2 = rr2 / (m1 + be1 * r_q1)
        rr3 = a2 * a2 * q2_q2 - rr2
        be2 = rr3 / rr2
        a3 = rr3 / (m1 - 2.0 * a2 * ar_q2 + a2 * a2 * q2_aq2 - be2 * rr3 / a2)

        def update_row(row, unused):
            keep = keep_of(row)
            own_row = (row >= 1) & (row <= NODES_Y)
            for m in range(3):
                r2 = v0[m, row]
                ar2 = jnp.where(own_planes & own_row, v1[m, row], copy_rx[parity, m, row])
                ar2 = jnp.where(all_planes, keep * ar2, 0.0)
                aar2 = keep * assembled(
                    v2[m, row],
                    sum_rx[sum_parity, 0, m, row],
                    sum_rx[sum_parity, 1, m, row],
                    sum_rx[sum_parity, 2, m, row],
                    row,
                )
                old1, old0 = q1[m, row], q0[m, row]
                q2 = ar2 + be1 * old1
                aq1 = (old1 - be0 * old0 - ar2) * ia1
                r3 = r2 - a2 * q2
                q3 = ar2 - a2 * (aar2 + be1 * aq1) + be2 * q2
                d2 = r2 + be1 * d1[m, row]
                d3 = r3 + be2 * d2
                x[m, row] = x[m, row] + (a2 * d2 + a3 * d3)
                v0[m, row] = r3 - a3 * q3
                q1[m, row] = q3
                q0[m, row] = q2
                d1[m, row] = d3
            return unused

        lax.fori_loop(0, ROWS, update_row, 0)
        pltpu.make_async_copy(rest, rest, all_send.at[parity]).wait()
        return be2, 1.0 / a3, 1.0 / a2, rr3

    none = jnp.zeros((1, 1), F32)
    lax.fori_loop(0, OUTER, outer, (none, none, none, none + 1.0))

    stores = []
    for i in range(NODES_X):
        stores.append(pltpu.make_async_copy(x.at[:, 1:18, i + 1], increment_hbm.at[:, i], out_sem.at[0, i]))
        stores.append(pltpu.make_async_copy(v0.at[:, 1:18, i + 1], residual_hbm.at[:, i], out_sem.at[1, i]))
    for copy in stores:
        copy.start()
    for copy in stores:
        copy.wait()


def solution(mesh):
    size_x, size_y = mesh.shape["gx"], mesh.shape["gy"]
    peers = size_x * size_y
    field = jax.ShapeDtypeStruct((3, NODES_X, NODES_Y, NZ), F32)

    def vmem(*shape, dtype=F32):
        return pltpu.VMEM(shape, dtype)

    def node(*lead):
        return vmem(*lead, ROWS, SUB, NZ)

    dma = pltpu.SemaphoreType.DMA
    scratch = [
        node(3), node(3), node(), node(), node(3), vmem(BY, SUB, NZ), vmem(HIDDEN_LAYERS, HID, HID),
        vmem(6, BY, SUB, NZ), vmem(NZ, SLOTS, dtype=BF16), vmem(SLOTS, NZ, dtype=BF16),
        vmem(COLUMNS, SLOTS, dtype=BF16), vmem(BY * SUB, SLOTS), vmem(SLOTS, 128, dtype=BF16),
        vmem(128, SLOTS), vmem(32, SLOTS), vmem(2 * GROUP * COLUMNS, SLOTS, dtype=BF16),
        vmem(N_SCATTER, BY, SUB, NZ),
        vmem(N_PAIRS, BY, SUB, NZ), vmem(N_PAIRS, BY + 2, SUB, NZ), vmem(N_PAIRS, BY + 2, SUB, NZ),
        node(3), node(3), node(3), node(3), node(3), node(3), node(3),
        node(2, 3, 3), node(2, 3), vmem(2, peers, 1, 128),
        dma((5, 5)), dma((2, 5)), dma((8,)), dma((8,)), dma((8,)), dma((8,)),
        dma((2, 8)), dma((2, 8)), dma((2, 8)), dma((2, 8)), dma((2,)), dma((2,)),
    ]

    def body(u_now, load, mass, modulus, plastic_ids, plastic_count, w_in, w_hidden, w_head):
        hbm = pl.BlockSpec(memory_space=pl.ANY)
        local = pl.BlockSpec(memory_space=pltpu.VMEM)
        return pl.pallas_call(
            lambda *refs: kernel(size_x, size_y, *refs),
            out_shape=(field, field),
            in_specs=[
                hbm, hbm, hbm, hbm, local, pl.BlockSpec(memory_space=pltpu.SMEM), local, hbm, local,
            ],
            out_specs=(hbm, hbm),
            scratch_shapes=scratch,
            compiler_params=pltpu.CompilerParams(
                collective_id=0, has_side_effects=True, vmem_limit_bytes=60 * 2**20
            ),
        )(u_now, load, mass, modulus, plastic_ids.reshape(1, SLOTS), plastic_count, w_in, w_hidden, w_head)

    split_field = P(None, "gx", "gy", None)
    split_block = P("gx", "gy", None)
    return jax.shard_map(
        body,
        mesh=mesh,
        in_specs=(
            split_field, split_field, split_block, split_block, split_block, P("gx", "gy"), P(), P(), P(),
        ),
        out_specs=(split_field, split_field),
        check_vma=False,
    )
```

```python
import jax
import jax.numpy as jnp
from jax import lax
from jax.experimental import pallas as pl
from jax.experimental.pallas import tpu as pltpu
from jax.sharding import PartitionSpec as P

MESH = pl.DeviceIdType.MESH
F32, BF16 = jnp.float32, jnp.bfloat16
LAME_FIRST = 0.3 / (1.3 * 0.4)
LAME_SECOND = 1.0 / 2.6

BX, BY, NZ = 4, 16, 256
NODES_X, NODES_Y = BX + 1, BY + 1
ROWS = BY + 3
SUB = 8
SLOTS, HID, HIDDEN_LAYERS = 1024, 512, 3
COLUMNS = BY * BX
OUTER = 3
GROUP = 7
RINGS = 4

PAIRS = [(a, b) for a in range(6) for b in range(a, 6)]
PAIR_OF = {}
for _at, (_a, _b) in enumerate(PAIRS):
    PAIR_OF[_a, _b] = PAIR_OF[_b, _a] = _at
N_PAIRS = len(PAIRS)
N_SCATTER = 28
LIVE, FIRST_PAIR = 6, 7

DIRECTIONS = [(dx, dy) for dx in (-1, 0, 1) for dy in (-1, 0, 1) if (dx, dy) != (0, 0)]


def iso(a, b):
    if a < 3 and b < 3:
        return LAME_FIRST + (2.0 * LAME_SECOND if a == b else 0.0)
    return LAME_SECOND if a == b else 0.0


def z_next(values):
    lane = lax.broadcasted_iota(jnp.int32, values.shape, 1)
    return jnp.where(lane == NZ - 1, 0.0, pltpu.roll(values, NZ - 1, 1))


def z_prev(values):
    lane = lax.broadcasted_iota(jnp.int32, values.shape, 1)
    return jnp.where(lane == 0, 0.0, pltpu.roll(values, 1, 1))


def x_pairs(values):
    upper = pltpu.roll(values, SUB - 1, 0)
    return upper + values, upper - values


def strain_row(low, high):
    a = [low[m][1] + high[m][1] for m in range(3)]
    b = [high[m][0] - low[m][0] for m in range(3)]
    c = [high[m][0] + low[m][0] for m in range(3)]
    yz, xz, xy = c[1] + b[2], c[0] + a[2], b[0] + a[1]
    return [
        z_next(a[0]) + a[0],
        z_next(b[1]) + b[1],
        z_next(c[2]) - c[2],
        z_next(yz) + (b[2] - c[1]),
        z_next(xz) + (a[2] - c[0]),
        z_next(xy) + xy,
    ]


def force_parts(stress):
    before = [z_prev(s) for s in stress]
    total = {n: stress[n] + before[n] for n in (0, 1, 3, 4, 5)}
    differ = {n: before[n] - stress[n] for n in (2, 3, 4)}
    parts = []
    for along_x, along_y, along_z in ((0, 5, 4), (5, 1, 3), (4, 3, 2)):
        parts.append(
            (
                total[along_x],
                differ[along_z] - total[along_y],
                differ[along_z] + total[along_y],
            )
        )
    return parts


def force_of(along_x, other):
    return pltpu.roll(along_x + other, 1, 0) + (other - along_x)


def split(values):
    high = values.astype(BF16)
    return high, (values - high.astype(F32)).astype(BF16)


def mm(a, b):
    return jnp.dot(a, b, preferred_element_type=F32)


def face(dx, dy, depth):
    if depth == 2:
        sx = {-1: slice(1, 3), 0: slice(1, 6), 1: slice(4, 6)}[dx]
        tx = {-1: slice(5, 7), 0: slice(1, 6), 1: slice(0, 2)}[dx]
        sy = {-1: slice(1, 3), 0: slice(1, 18), 1: slice(16, 18)}[dy]
        ty = {-1: slice(17, 19), 0: slice(1, 18), 1: slice(0, 2)}[dy]
    else:
        sx = {-1: slice(2, 3), 0: slice(1, 6), 1: slice(4, 5)}[dx]
        tx = {-1: slice(6, 7), 0: slice(1, 6), 1: slice(0, 1)}[dx]
        sy = {-1: slice(2, 3), 0: slice(1, 18), 1: slice(16, 17)}[dy]
        ty = {-1: slice(18, 19), 0: slice(1, 18), 1: slice(0, 1)}[dy]
    return sy, sx, ty, tx


def element_face(dx, dy):
    sx = {-1: slice(1, 2), 0: slice(1, 5), 1: slice(4, 5)}[dx]
    tx = {-1: slice(5, 6), 0: slice(1, 5), 1: slice(0, 1)}[dx]
    sy = {-1: slice(1, 2), 0: slice(1, 17), 1: slice(16, 17)}[dy]
    ty = {-1: slice(17, 18), 0: slice(1, 17), 1: slice(0, 1)}[dy]
    return sy, sx, ty, tx


def all_offsets(size_x, size_y):
    offsets = [
        (z, core, x, y)
        for z in range(size_x // 2)
        for core in range(2)
        for x in range(size_y // RINGS)
        for y in range(RINGS)
    ][1:]

    def hops(offset):
        z, core, x, y = offset
        return sum(min(d, RINGS - d) for d in (z, x, y)) * 2 + core

    return sorted(offsets, key=hops, reverse=True)


def by_rows(first, last, width, body, carry):
    assert (last - first) % width == 0

    def block(at, carry):
        for n in range(width):
            carry = body(first + at * width + n, carry)
        return carry

    return lax.fori_loop(0, (last - first) // width, block, carry)


def kernel(
    size_x, size_y,
    u_hbm, load_hbm, mass_hbm, modulus_hbm, ids_ref, count_ref, w_in_ref, w_hidden_hbm, w_head_ref,
    increment_hbm, residual_hbm,
    ux, lx, mass_part, mass_full, mass_rx, modulus, weights,
    strain_now, onehot_k, onehot_kt, onehot_r, onehot_r8, inputs_t, out_t, values, lhs, scattered,
    tangent,
    v0, v1, v2, q1, q0, d1, x, sum_rx, copy_rx, gathered,
    load_sem, out_sem, mass_send, mass_recv, tan_send, tan_recv,
    sum_send, sum_recv, copy_send, copy_recv, all_send, all_recv,
):
    index_x, index_y = lax.axis_index("gx"), lax.axis_index("gy")
    me = index_x * size_y + index_y
    peers = size_x * size_y
    neighbours = [
        (lax.rem(index_x + dx + size_x, size_x), lax.rem(index_y + dy + size_y, size_y))
        for dx, dy in DIRECTIONS
    ]

    ring_x, ring_y = index_y // RINGS, lax.rem(index_y, RINGS)
    ring_z, core = index_x // 2, lax.rem(index_x, 2)
    at_z = [lax.rem(ring_z + d, RINGS) * 2 for d in range(size_x // 2)]
    at_core = [core, 1 - core]
    at_ring_x = [lax.rem(ring_x + d, RINGS) * RINGS for d in range(size_y // RINGS)]
    at_ring_y = [lax.rem(ring_y + d, RINGS) for d in range(RINGS)]
    along_gx = [[z + c for c in at_core] for z in at_z]
    along_gy = [[a + b for b in at_ring_y] for a in at_ring_x]
    others = [
        (along_gx[z][c], along_gy[a][b]) for z, c, a, b in all_offsets(size_x, size_y)
    ]

    for ref in (mass_part, modulus):
        ref[...] = jnp.zeros_like(ref)
    u_loads, modulus_loads, mass_loads, load_loads, weight_loads = [], [], [], [], []
    for i in range(NODES_X):
        for m in range(3):
            u_loads.append(pltpu.make_async_copy(u_hbm.at[i, :, m : m + 1], ux.at[m, 1:18, i + 1 : i + 2], load_sem.at[m, i]))
    for layer in range(HIDDEN_LAYERS):
        weight_loads.append(pltpu.make_async_copy(w_hidden_hbm.at[layer], weights.at[layer], load_sem.at[8, layer]))
    for i in range(BX):
        modulus_loads.append(pltpu.make_async_copy(modulus_hbm.at[i], modulus.at[:, i + 1], load_sem.at[6, i]))
    for i in range(NODES_X):
        mass_loads.append(pltpu.make_async_copy(mass_hbm.at[i], mass_part.at[1:18, i + 1], load_sem.at[7, i]))
        for m in range(3):
            load_loads.append(pltpu.make_async_copy(load_hbm.at[i, :, m : m + 1], lx.at[m, 1:18, i + 1 : i + 2], load_sem.at[3 + m, i]))
    loads = u_loads + weight_loads + modulus_loads + mass_loads + load_loads
    for copy in loads:
        copy.start()

    tangent[...] = jnp.zeros_like(tangent)
    barrier = pltpu.get_barrier_semaphore()
    for device in others:
        pl.semaphore_signal(barrier, inc=1, device_id=device, device_id_type=MESH)
    for ref in (q1, q0, d1, x):
        ref[...] = jnp.zeros_like(ref)

    ids = ids_ref[...]
    slot = lax.broadcasted_iota(jnp.int32, (1, SLOTS), 1)
    live = jnp.where(slot < count_ref[0, 0], 1.0, 0.0)
    at_k = ids & (NZ - 1)
    at_j = (ids >> 8) & (BY - 1)
    at_i = ids >> 12
    onehot_k[...] = jnp.where(
        lax.broadcasted_iota(jnp.int32, (NZ, SLOTS), 0) == at_k, 1.0, 0.0
    ).astype(BF16)
    onehot_r[...] = jnp.where(
        lax.broadcasted_iota(jnp.int32, (COLUMNS, SLOTS), 0) == at_j * BX + at_i, live, 0.0
    ).astype(BF16)
    onehot_r8[...] = jnp.where(
        lax.broadcasted_iota(jnp.int32, (BY * SUB, SLOTS), 0) == at_j * SUB + at_i + 1, 1.0, 0.0
    )
    k_column = jnp.broadcast_to(at_k.astype(F32), (128, SLOTS)).T
    lane_k = lax.broadcasted_iota(jnp.int32, (SLOTS, 128), 1).astype(F32)
    onehot_kt[:, 0:128] = jnp.where(k_column == lane_k, 1.0, 0.0).astype(BF16)
    onehot_kt[:, 128:256] = jnp.where(k_column == lane_k + 128.0, 1.0, 0.0).astype(BF16)

    sub = lax.broadcasted_iota(jnp.int32, (SUB, NZ), 0)
    own_elements = (sub >= 1) & (sub <= BX)
    for copy in u_loads:
        copy.wait()

    def pairs_of(ref, row):
        return [x_pairs(ref[m, row]) for m in range(3)]

    def strain_step(row, low):
        high = pairs_of(ux, row + 1)
        for n, value in enumerate(strain_row(low, high)):
            strain_now[n, row - 1] = jnp.where(own_elements, 0.25 * value, 0.0)
        return high

    by_rows(1, 1 + BY, 8, strain_step, pairs_of(ux, 1))

    picked = []
    for n in range(6):
        high, low = split(strain_now[n].reshape(BY * SUB, NZ))
        rows = mm(high, onehot_k[...]) + mm(low, onehot_k[...])
        picked.append(jnp.sum(rows * onehot_r8[...], axis=0, keepdims=True))
    eps = jnp.concatenate(picked + [jnp.zeros((2, SLOTS), F32)], axis=0)
    eps_high = eps.astype(BF16).astype(F32)
    stacked = jnp.concatenate(
        [eps_high, eps - eps_high, eps_high, jnp.zeros((104, SLOTS), F32)], axis=0
    )
    inputs_t[...] = stacked.T.astype(BF16)

    w_in = jnp.concatenate([w_in_ref[...], jnp.zeros((2, HID), F32)], axis=0)
    w_in_high = w_in.astype(BF16).astype(F32)
    w_first = jnp.concatenate(
        [w_in_high, w_in_high, w_in - w_in_high, jnp.zeros((104, HID), F32)], axis=0
    ).astype(BF16)
    to_row = lax.broadcasted_iota(jnp.int32, (128, 42), 0)
    from_out = lax.broadcasted_iota(jnp.int32, (128, 42), 1)
    place = jnp.where(
        (from_out == (to_row // 8) * 6 + to_row % 8) & (to_row % 8 < 6) & (to_row < 56), 1.0, 0.0
    ).astype(BF16)
    head_high, head_low = split(w_head_ref[...])
    head_high = mm(place, head_high).T.astype(BF16)
    head_low = mm(place, head_low).T.astype(BF16)
    for copy in weight_loads:
        copy.wait()
    halves = [split(weights[layer]) for layer in range(HIDDEN_LAYERS)]

    def product(hidden, parts):
        high, low = split(hidden)
        return mm(high, parts[0]) + (mm(low, parts[0]) + mm(high, parts[1]))

    half = SLOTS // 2
    left, right = mm(inputs_t[0:half], w_first), mm(inputs_t[half:SLOTS], w_first)
    for parts in halves + [(head_high, head_low)]:
        left = product(jnp.tanh(left), parts)
        right = product(jnp.tanh(right), parts)
    out_t[:, 0:half] = left.T
    out_t[:, half:SLOTS] = right.T

    for copy in mass_loads:
        copy.wait()
    pl.semaphore_wait(barrier, peers - 1)
    mass_copies = []
    for q, ((dx, dy), device) in enumerate(zip(DIRECTIONS, neighbours)):
        sy, sx, ty, tx = face(dx, dy, 2)
        kind = 0 if dy == 0 else (1 if dx == 0 else 2)
        copy = pltpu.make_async_remote_copy(
            mass_part.at[sy, sx], mass_rx.at[kind, ty, tx], mass_send.at[q], mass_recv.at[q],
            device_id=device, device_id_type=MESH,
        )
        copy.start()
        mass_copies.append(copy)

    values[0:6] = out_t[0:6]
    values[LIVE : LIVE + 1] = jnp.ones((1, SLOTS), F32)
    factor = [out_t[8 * (a + 1) : 8 * (a + 2)] for a in range(6)]
    for at, (a, b) in enumerate(PAIRS):
        values[FIRST_PAIR + at : FIRST_PAIR + at + 1] = jnp.sum(
            factor[a] * factor[b], axis=0, keepdims=True
        ) * (1.0 / 6.0)

    def scatter_group(at):
        for n in range(GROUP):
            high, low = split(values[at * GROUP + n : at * GROUP + n + 1])
            rows = onehot_r[...]
            lhs[n * COLUMNS : (n + 1) * COLUMNS] = rows * high
            lhs[(GROUP + n) * COLUMNS : (GROUP + n + 1) * COLUMNS] = rows * low
        spread = mm(lhs[...], onehot_kt[...])
        spread = spread[: GROUP * COLUMNS] + spread[GROUP * COLUMNS :]
        for n in range(GROUP):
            for g in range(BY // 2):
                start = n * COLUMNS + g * SUB
                both = spread[start : start + SUB]
                scattered[at * GROUP + n, 2 * g] = jnp.where(own_elements, pltpu.roll(both, 1, 0), 0.0)
                scattered[at * GROUP + n, 2 * g + 1] = jnp.where(own_elements, pltpu.roll(both, 5, 0), 0.0)

    def sum_copies(parity):
        copies = []
        for q, ((dx, dy), device) in enumerate(zip(DIRECTIONS, neighbours)):
            sy, sx, ty, tx = face(dx, dy, 2)
            kind = 0 if dy == 0 else (1 if dx == 0 else 2)
            copies.append(
                pltpu.make_async_remote_copy(
                    v2.at[:, sy, sx], sum_rx.at[parity, kind, :, ty, tx],
                    sum_send.at[parity, q], sum_recv.at[parity, q],
                    device_id=device, device_id_type=MESH,
                )
            )
        return copies

    def exact_copies(parity):
        copies = []
        for q, ((dx, dy), device) in enumerate(zip(DIRECTIONS, neighbours)):
            sy, sx, ty, tx = face(dx, dy, 1)
            copies.append(
                pltpu.make_async_remote_copy(
                    v1.at[:, sy, sx], copy_rx.at[parity, :, ty, tx],
                    copy_send.at[parity, q], copy_recv.at[parity, q],
                    device_id=device, device_id_type=MESH,
                )
            )
        return copies

    global_x = index_x * BX + sub - 1
    keep_x = jnp.where(
        (global_x >= 0) & (global_x < size_x * BX) & (sub < SUB - 1), 1.0, 0.0
    )
    own_planes = (sub >= 1) & (sub <= NODES_X)
    rim_planes = ((sub <= 1) & (index_x > 0)) | ((sub >= NODES_X) & (sub <= NODES_X + 1))
    halo_planes = (sub == 0) | (sub == NODES_X + 1)
    flank_low, corner_low = own_planes & (index_y > 0), rim_planes & (index_y > 0)
    valid_elements = (sub <= BX + 1) & ((sub >= 1) | (index_x > 0))

    def keep_of(row):
        global_y = index_y * BY + row - 1
        inside = jnp.where((global_y >= 0) & (global_y < size_y * BY), 1.0, 0.0)
        return keep_x * inside

    def assembled(part, received, row):
        at_rim = isinstance(row, int)
        total = jnp.zeros((SUB, NZ), F32)
        if not at_rim or 1 <= row <= NODES_Y:
            total = part + jnp.where(rim_planes, received(0), 0.0)
        if at_rim:
            flank, corner = (flank_low, corner_low) if row <= 1 else (own_planes, rim_planes)
            total = total + jnp.where(flank, received(1), 0.0) + jnp.where(corner, received(2), 0.0)
        return total

    def all_rows(body):
        for row in (0, 1, NODES_Y, NODES_Y + 1):
            body(row)

        def inner(row, carry):
            body(row)
            return carry

        by_rows(2, NODES_Y, 5, inner, 0)

    def stress_now(row):
        scale = 0.25 * modulus[row]
        base = scale * (1.0 - 0.75 * scattered[LIVE, row])
        eps_row = [strain_now[n, row] for n in range(6)]
        trace = LAME_FIRST * (eps_row[0] + eps_row[1] + eps_row[2])
        elastic = [trace + 2.0 * LAME_SECOND * eps_row[n] for n in range(3)]
        elastic += [LAME_SECOND * eps_row[n] for n in range(3, 6)]
        return [base * elastic[n] + scale * scattered[n, row] for n in range(6)]

    zero = jnp.zeros((SUB, NZ), F32)
    no_parts = [(zero, zero)] * 3

    def residual_step(row, before):
        parts = force_parts(stress_now(row - 1))
        for m in range(3):
            force = force_of(parts[m][0] + before[m][0], parts[m][1] + before[m][1])
            v2[m, row] = jnp.where(own_planes, lx[m, row] - force, 0.0)
        return [(parts[m][0], parts[m][2]) for m in range(3)]

    scatter_group(0)
    for copy in modulus_loads + load_loads:
        copy.wait()
    last = by_rows(1, 1 + BY, 8, residual_step, no_parts)
    for m in range(3):
        v2[m, NODES_Y] = jnp.where(own_planes, lx[m, NODES_Y] - force_of(*last[m]), 0.0)

    first_copies = sum_copies(0)
    for copy in first_copies:
        copy.start()

    tangent_copies = []
    for group in range(N_PAIRS // GROUP):
        scatter_group(group + 1)

        def tangent_row(row, carry):
            scale = modulus[row] * (1.0 / 16.0)
            base = scale * (1.0 - 0.75 * scattered[LIVE, row])
            for at in range(group * GROUP, (group + 1) * GROUP):
                entry = scale * scattered[FIRST_PAIR + at, row]
                if iso(*PAIRS[at]):
                    entry = entry + base * iso(*PAIRS[at])
                tangent[at, row + 1, 1 : 1 + BX] = entry[1 : 1 + BX]
            return carry

        by_rows(0, BY, 4, tangent_row, 0)
        entries = pl.ds(group * GROUP, GROUP)
        for q, ((dx, dy), device) in enumerate(zip(DIRECTIONS, neighbours)):
            sy, sx, ty, tx = element_face(dx, dy)
            copy = pltpu.make_async_remote_copy(
                tangent.at[entries, sy, sx], tangent.at[entries, ty, tx],
                tan_send.at[group, q], tan_recv.at[group, q],
                device_id=device, device_id_type=MESH,
            )
            copy.start()
            tangent_copies.append(copy)

    for copy in mass_copies:
        copy.wait()

    def mass_row(row):
        mass_full[row] = assembled(mass_part[row], lambda kind: mass_rx[kind, row], row)

    all_rows(mass_row)
    for copy in first_copies:
        copy.wait()

    def start_row(row):
        keep = keep_of(row)
        for m in range(3):
            part = None if isinstance(row, int) and row in (0, NODES_Y + 1) else v2[m, row]
            v0[m, row] = keep * assembled(part, lambda kind: sum_rx[0, kind, m, row], row)

    all_rows(start_row)
    for copy in tangent_copies:
        copy.wait()

    def stress_row(row, strain):
        entries = [tangent[at, row] for at in range(N_PAIRS)]
        result = []
        for a in range(6):
            total = entries[PAIR_OF[a, 0]] * strain[0]
            for b in range(1, 6):
                total = total + entries[PAIR_OF[a, b]] * strain[b]
            result.append(total)
        return result

    def first_image(row, carry):
        low, before = carry
        high = pairs_of(v0, row + 1)
        present = valid_elements & (row + index_y > 0)
        strain = [jnp.where(present, value, 0.0) for value in strain_row(low, high)]
        parts = force_parts(stress_row(row, strain))
        keep = keep_of(row)
        for m in range(3):
            force = force_of(parts[m][0] + before[m][0], parts[m][1] + before[m][1])
            v1[m, row] = keep * (force + mass_full[row] * v0[m, row])
        return high, [(parts[m][0], parts[m][2]) for m in range(3)]

    def second_image(row, carry):
        low, before, sums = carry
        high = pairs_of(v1, row + 1)
        strain = [jnp.where(own_elements, value, 0.0) for value in strain_row(low, high)]
        parts = force_parts(stress_row(row, strain))
        rr, r_ar, ar_ar, ar_aar = sums
        for m in range(3):
            here, image = v0[m, row], v1[m, row]
            force = force_of(parts[m][0] + before[m][0], parts[m][1] + before[m][1])
            force = force + mass_part[row] * image
            v2[m, row] = force
            rr = rr + here * here
            r_ar = r_ar + here * image
            ar_ar = ar_ar + image * image
            ar_aar = ar_aar + image * force
        return high, [(parts[m][0], parts[m][2]) for m in range(3)], (rr, r_ar, ar_ar, ar_aar)

    lane = lax.broadcasted_iota(jnp.int32, (1, 128), 1)

    def outer(step, carry):
        be0, ia1, ia0, rr_before = carry
        parity = lax.rem(step, 2)
        sum_parity = lax.rem(step + 1, 2)
        by_rows(0, BY + 2, 6, first_image, (pairs_of(v0, 0), no_parts))
        exact = exact_copies(parity)
        for copy in exact:
            copy.start()
        _, before, sums = by_rows(
            1, 1 + BY, 8, second_image, (pairs_of(v1, 1), no_parts, (zero,) * 4)
        )
        ar_aar = sums[3]
        for m in range(3):
            image = v1[m, NODES_Y]
            force = force_of(*before[m]) + mass_part[NODES_Y] * image
            v2[m, NODES_Y] = force
            ar_aar = ar_aar + jnp.where(own_planes, image * force, 0.0)
        summed = sum_copies(sum_parity)
        for copy in summed:
            copy.start()

        message = jnp.zeros((1, 128), F32)
        for at, (value, mask) in enumerate(
            ((sums[0], own_elements), (sums[1], own_elements), (sums[2], own_elements), (ar_aar, own_planes))
        ):
            total = jnp.sum(jnp.where(mask, value, 0.0), axis=0, keepdims=True)
            total = jnp.sum(total, axis=1, keepdims=True)
            message = message + jnp.where(lane == at, total, 0.0)
        gathered[parity, me] = message

        for device in others:
            pltpu.make_async_remote_copy(
                gathered.at[parity, me], gathered.at[parity, me],
                all_send.at[parity], all_recv.at[parity],
                device_id=device, device_id_type=MESH,
            ).start()
        for copy in exact + summed:
            copy.wait()

        def image_row(row):
            keep = keep_of(row)
            outside = isinstance(row, int) and row in (0, NODES_Y + 1)
            for m in range(3):
                rim = copy_rx[parity, m, row]
                if outside:
                    ar2 = jnp.where(sub <= NODES_X + 1, rim, 0.0)
                else:
                    ar2 = jnp.where(halo_planes, rim, v1[m, row])
                ar2 = keep * ar2
                part = None if outside else v2[m, row]
                v2[m, row] = keep * assembled(part, lambda kind: sum_rx[sum_parity, kind, m, row], row)
                v1[m, row] = ar2
                q0[m, row] = (q1[m, row] - be0 * q0[m, row] - ar2) * ia1

        all_rows(image_row)
        rest = gathered.at[parity, 0 : peers - 1]
        pltpu.make_async_copy(rest, rest, all_recv.at[parity]).wait()
        totals = jnp.sum(gathered[parity], axis=0)
        rr2, m1, m2, m3 = [
            jnp.sum(jnp.where(lane == at, totals, 0.0), axis=1, keepdims=True) for at in range(4)
        ]
        be1 = jnp.where(step == 0, 0.0, rr2 / rr_before)
        r_q1 = -rr2 * ia1
        ar_q1 = (r_q1 - m1) * ia1
        q1_q1 = (rr_before + rr2) * ia1 * ia1
        ar_q0 = rr2 * ia1 * ia0
        q1_q0 = -rr_before * ia1 * ia0
        q1_aar = ia1 * (ar_q1 - be0 * ar_q0 - m2)
        q1_aq1 = ia1 * (q1_q1 - be0 * q1_q0 - ar_q1)
        q2_q2 = m2 + 2.0 * be1 * ar_q1 + be1 * be1 * q1_q1
        ar_q2 = m2 + be1 * ar_q1
        q2_aq2 = m3 + 2.0 * be1 * q1_aar + be1 * be1 * q1_aq1
        a2 = rr2 / (m1 + be1 * r_q1)
        rr3 = a2 * a2 * q2_q2 - rr2
        be2 = rr3 / rr2
        a3 = rr3 / (m1 - 2.0 * a2 * ar_q2 + a2 * a2 * q2_aq2 - be2 * rr3 / a2)

        def update_row(row, unused):
            for m in range(3):
                ar2, old = v1[m, row], q1[m, row]
                q2 = ar2 + be1 * old
                r3 = v0[m, row] - a2 * q2
                q3 = ar2 - a2 * (v2[m, row] + be1 * q0[m, row]) + be2 * q2
                d2 = v0[m, row] + be1 * d1[m, row]
                d3 = r3 + be2 * d2
                x[m, row] = x[m, row] + (a2 * d2 + a3 * d3)
                v0[m, row] = r3 - a3 * q3
                q1[m, row] = q3
                q0[m, row] = q2
                d1[m, row] = d3
            return unused

        by_rows(0, ROWS - 1, 6, update_row, 0)
        update_row(ROWS - 1, 0)
        pltpu.make_async_copy(rest, rest, all_send.at[parity]).wait()
        return be2, 1.0 / a3, 1.0 / a2, rr3

    none = jnp.zeros((1, 1), F32)
    lax.fori_loop(0, OUTER, outer, (none, none, none, none + 1.0))

    stores = []
    for i in range(NODES_X):
        for m in range(3):
            stores.append(pltpu.make_async_copy(x.at[m, 1:18, i + 1 : i + 2], increment_hbm.at[i, :, m : m + 1], out_sem.at[0, m, i]))
            stores.append(pltpu.make_async_copy(v0.at[m, 1:18, i + 1 : i + 2], residual_hbm.at[i, :, m : m + 1], out_sem.at[1, m, i]))
    for copy in stores:
        copy.start()
    for copy in stores:
        copy.wait()


def solution(mesh):
    size_x, size_y = mesh.shape["gx"], mesh.shape["gy"]
    peers = size_x * size_y
    field = jax.ShapeDtypeStruct((NODES_X, NODES_Y, 3, NZ), F32)

    def vmem(*shape, dtype=F32):
        return pltpu.VMEM(shape, dtype)

    def node(*lead):
        return vmem(*lead, ROWS, SUB, NZ)

    dma = pltpu.SemaphoreType.DMA
    scratch = [
        node(3), node(3), node(), node(), node(3), vmem(BY, SUB, NZ), vmem(HIDDEN_LAYERS, HID, HID),
        vmem(6, BY, SUB, NZ), vmem(NZ, SLOTS, dtype=BF16), vmem(SLOTS, NZ, dtype=BF16),
        vmem(COLUMNS, SLOTS, dtype=BF16), vmem(BY * SUB, SLOTS), vmem(SLOTS, 128, dtype=BF16),
        vmem(128, SLOTS), vmem(32, SLOTS), vmem(2 * GROUP * COLUMNS, SLOTS, dtype=BF16),
        vmem(N_SCATTER, BY, SUB, NZ),
        vmem(N_PAIRS, BY + 2, SUB, NZ),
        node(3), node(3), node(3), node(3), node(3), node(3), node(3),
        node(2, 3, 3), node(2, 3), vmem(2, peers, 1, 128),
        dma((9, 5)), dma((2, 3, 5)), dma((8,)), dma((8,)), dma((3, 8)), dma((3, 8)),
        dma((2, 8)), dma((2, 8)), dma((2, 8)), dma((2, 8)), dma((2,)), dma((2,)),
    ]

    def body(u_now, load, mass, modulus, plastic_ids, plastic_count, w_in, w_hidden, w_head):
        hbm = pl.BlockSpec(memory_space=pl.ANY)
        local = pl.BlockSpec(memory_space=pltpu.VMEM)
        increment, residual = pl.pallas_call(
            lambda *refs: kernel(size_x, size_y, *refs),
            out_shape=(field, field),
            in_specs=[
                hbm, hbm, hbm, hbm, local, pl.BlockSpec(memory_space=pltpu.SMEM), local, hbm, local,
            ],
            out_specs=(hbm, hbm),
            scratch_shapes=scratch,
            compiler_params=pltpu.CompilerParams(
                collective_id=0, has_side_effects=True, vmem_limit_bytes=60 * 2**20
            ),
        )(
            u_now.transpose(1, 2, 0, 3), load.transpose(1, 2, 0, 3), mass, modulus,
            plastic_ids.reshape(1, SLOTS), plastic_count, w_in, w_hidden, w_head.T,
        )
        return increment.transpose(2, 0, 1, 3), residual.transpose(2, 0, 1, 3)

    split_field = P(None, "gx", "gy", None)
    split_block = P("gx", "gy", None)
    return jax.shard_map(
        body,
        mesh=mesh,
        in_specs=(
            split_field, split_field, split_block, split_block, split_block, P("gx", "gy"), P(), P(), P(),
        ),
        out_specs=(split_field, split_field),
        check_vma=False,
    )
```

```python
import jax
import jax.numpy as jnp
from jax import lax
from jax.experimental import pallas as pl
from jax.experimental.pallas import tpu as pltpu
from jax.sharding import PartitionSpec as P

MESH = pl.DeviceIdType.MESH
F32, BF16 = jnp.float32, jnp.bfloat16
LAME_FIRST = 0.3 / (1.3 * 0.4)
LAME_SECOND = 1.0 / 2.6

BX, BY, NZ = 4, 16, 256
NODES_X, NODES_Y = BX + 1, BY + 1
ROWS = BY + 3
SUB = 8
SLOTS, HID, HIDDEN_LAYERS = 1024, 512, 3
COLUMNS = BY * BX
OUTER = 3
GROUP = 7
RINGS = 4

PAIRS = [(a, b) for a in range(6) for b in range(a, 6)]
PAIR_OF = {}
for _at, (_a, _b) in enumerate(PAIRS):
    PAIR_OF[_a, _b] = PAIR_OF[_b, _a] = _at
N_PAIRS = len(PAIRS)
N_SCATTER = 28
LIVE, FIRST_PAIR = 6, 7

DIRECTIONS = [(dx, dy) for dx in (-1, 0, 1) for dy in (-1, 0, 1) if (dx, dy) != (0, 0)]


def iso(a, b):
    if a < 3 and b < 3:
        return LAME_FIRST + (2.0 * LAME_SECOND if a == b else 0.0)
    return LAME_SECOND if a == b else 0.0


def z_next(values):
    lane = lax.broadcasted_iota(jnp.int32, values.shape, 1)
    return jnp.where(lane == NZ - 1, 0.0, pltpu.roll(values, NZ - 1, 1))


def z_prev(values):
    lane = lax.broadcasted_iota(jnp.int32, values.shape, 1)
    return jnp.where(lane == 0, 0.0, pltpu.roll(values, 1, 1))


def x_pairs(values):
    upper = pltpu.roll(values, SUB - 1, 0)
    return upper + values, upper - values


def strain_row(low, high):
    a = [low[m][1] + high[m][1] for m in range(3)]
    b = [high[m][0] - low[m][0] for m in range(3)]
    c = [high[m][0] + low[m][0] for m in range(3)]
    yz, xz, xy = c[1] + b[2], c[0] + a[2], b[0] + a[1]
    return [
        z_next(a[0]) + a[0],
        z_next(b[1]) + b[1],
        z_next(c[2]) - c[2],
        z_next(yz) + (b[2] - c[1]),
        z_next(xz) + (a[2] - c[0]),
        z_next(xy) + xy,
    ]


def force_parts(stress):
    before = [z_prev(s) for s in stress]
    total = {n: stress[n] + before[n] for n in (0, 1, 3, 4, 5)}
    differ = {n: before[n] - stress[n] for n in (2, 3, 4)}
    parts = []
    for along_x, along_y, along_z in ((0, 5, 4), (5, 1, 3), (4, 3, 2)):
        parts.append(
            (
                total[along_x],
                differ[along_z] - total[along_y],
                differ[along_z] + total[along_y],
            )
        )
    return parts


def force_of(along_x, other):
    return pltpu.roll(along_x + other, 1, 0) + (other - along_x)


def split(values):
    high = values.astype(BF16)
    return high, (values - high.astype(F32)).astype(BF16)


def mm(a, b):
    return jnp.dot(a, b, preferred_element_type=F32)


def face(dx, dy, depth):
    if depth == 2:
        sx = {-1: slice(1, 3), 0: slice(1, 6), 1: slice(4, 6)}[dx]
        tx = {-1: slice(5, 7), 0: slice(1, 6), 1: slice(0, 2)}[dx]
        sy = {-1: slice(1, 3), 0: slice(1, 18), 1: slice(16, 18)}[dy]
        ty = {-1: slice(17, 19), 0: slice(1, 18), 1: slice(0, 2)}[dy]
    else:
        sx = {-1: slice(2, 3), 0: slice(1, 6), 1: slice(4, 5)}[dx]
        tx = {-1: slice(6, 7), 0: slice(1, 6), 1: slice(0, 1)}[dx]
        sy = {-1: slice(2, 3), 0: slice(1, 18), 1: slice(16, 17)}[dy]
        ty = {-1: slice(18, 19), 0: slice(1, 18), 1: slice(0, 1)}[dy]
    return sy, sx, ty, tx


def element_face(dx, dy):
    sx = {-1: slice(1, 2), 0: slice(1, 5), 1: slice(4, 5)}[dx]
    tx = {-1: slice(5, 6), 0: slice(1, 5), 1: slice(0, 1)}[dx]
    sy = {-1: slice(1, 2), 0: slice(1, 17), 1: slice(16, 17)}[dy]
    ty = {-1: slice(17, 18), 0: slice(1, 17), 1: slice(0, 1)}[dy]
    return sy, sx, ty, tx


def all_offsets(size_x, size_y):
    offsets = [
        (z, core, x, y)
        for z in range(size_x // 2)
        for core in range(2)
        for x in range(size_y // RINGS)
        for y in range(RINGS)
    ][1:]

    def hops(offset):
        z, core, x, y = offset
        return sum(min(d, RINGS - d) for d in (z, x, y)) * 2 + core

    return sorted(offsets, key=hops, reverse=True)


def by_rows(first, last, width, body, carry):
    assert (last - first) % width == 0

    def block(at, carry):
        for n in range(width):
            carry = body(first + at * width + n, carry)
        return carry

    return lax.fori_loop(0, (last - first) // width, block, carry)


def kernel(
    size_x, size_y,
    u_hbm, load_hbm, mass_hbm, modulus_hbm, ids_hbm, count_hbm, w_in_hbm, w_hidden_hbm, w_head_hbm,
    increment_hbm, residual_hbm,
    ids_ref, count_ref, w_in_ref, w_head_ref, ux, lx, mass_part, mass_full, mass_rx, modulus, weights,
    strain_now, onehot_k, onehot_kt, onehot_r, onehot_r8, inputs_t, out_t, values, lhs, scattered,
    tangent,
    v0, v1, v2, q1, q0, d1, x, sum_rx, copy_rx, gathered,
    load_sem, out_sem, mass_send, mass_recv, tan_send, tan_recv,
    sum_send, sum_recv, copy_send, copy_recv, all_send, all_recv,
):
    index_x, index_y = lax.axis_index("gx"), lax.axis_index("gy")
    me = index_x * size_y + index_y
    peers = size_x * size_y
    neighbours = [
        (lax.rem(index_x + dx + size_x, size_x), lax.rem(index_y + dy + size_y, size_y))
        for dx, dy in DIRECTIONS
    ]

    ring_x, ring_y = index_y // RINGS, lax.rem(index_y, RINGS)
    ring_z, core = index_x // 2, lax.rem(index_x, 2)
    at_z = [lax.rem(ring_z + d, RINGS) * 2 for d in range(size_x // 2)]
    at_core = [core, 1 - core]
    at_ring_x = [lax.rem(ring_x + d, RINGS) * RINGS for d in range(size_y // RINGS)]
    at_ring_y = [lax.rem(ring_y + d, RINGS) for d in range(RINGS)]
    along_gx = [[z + c for c in at_core] for z in at_z]
    along_gy = [[a + b for b in at_ring_y] for a in at_ring_x]
    others = [
        (along_gx[z][c], along_gy[a][b]) for z, c, a, b in all_offsets(size_x, size_y)
    ]

    for ref in (mass_part, modulus):
        ref[...] = jnp.zeros_like(ref)
    small = ((ids_hbm, ids_ref), (count_hbm, count_ref), (w_in_hbm, w_in_ref), (w_head_hbm, w_head_ref))
    small_loads = [
        pltpu.make_async_copy(source, target, load_sem.at[9, at])
        for at, (source, target) in enumerate(small)
    ]
    u_loads, modulus_loads, mass_loads, load_loads, weight_loads = [], [], [], [], []
    for i in range(NODES_X):
        for m in range(3):
            u_loads.append(pltpu.make_async_copy(u_hbm.at[i, :, m : m + 1], ux.at[m, 1:18, i + 1 : i + 2], load_sem.at[m, i]))
    for layer in range(HIDDEN_LAYERS):
        weight_loads.append(pltpu.make_async_copy(w_hidden_hbm.at[layer], weights.at[layer], load_sem.at[8, layer]))
    for i in range(BX):
        modulus_loads.append(pltpu.make_async_copy(modulus_hbm.at[i], modulus.at[:, i + 1], load_sem.at[6, i]))
    for i in range(NODES_X):
        mass_loads.append(pltpu.make_async_copy(mass_hbm.at[i], mass_part.at[1:18, i + 1], load_sem.at[7, i]))
        for m in range(3):
            load_loads.append(pltpu.make_async_copy(load_hbm.at[i, :, m : m + 1], lx.at[m, 1:18, i + 1 : i + 2], load_sem.at[3 + m, i]))
    loads = small_loads + u_loads + weight_loads + modulus_loads + mass_loads + load_loads
    for copy in loads:
        copy.start()

    barrier = pltpu.get_barrier_semaphore()
    for device in others:
        pl.semaphore_signal(barrier, inc=1, device_id=device, device_id_type=MESH)
    for copy in small_loads:
        copy.wait()

    ids = ids_ref[...]
    slot = lax.broadcasted_iota(jnp.int32, (1, SLOTS), 1)
    live = jnp.where(slot < count_ref[...], 1.0, 0.0)
    at_k = ids & (NZ - 1)
    at_j = (ids >> 8) & (BY - 1)
    at_i = ids >> 12
    onehot_k[...] = jnp.where(
        lax.broadcasted_iota(jnp.int32, (NZ, SLOTS), 0) == at_k, 1.0, 0.0
    ).astype(BF16)
    onehot_r[...] = jnp.where(
        lax.broadcasted_iota(jnp.int32, (COLUMNS, SLOTS), 0) == at_j * BX + at_i, live, 0.0
    ).astype(BF16)
    onehot_r8[...] = jnp.where(
        lax.broadcasted_iota(jnp.int32, (BY * SUB, SLOTS), 0) == at_j * SUB + at_i + 1, 1.0, 0.0
    )
    k_column = jnp.broadcast_to(at_k.astype(F32), (128, SLOTS)).T
    lane_k = lax.broadcasted_iota(jnp.int32, (SLOTS, 128), 1).astype(F32)
    onehot_kt[:, 0:128] = jnp.where(k_column == lane_k, 1.0, 0.0).astype(BF16)
    onehot_kt[:, 128:256] = jnp.where(k_column == lane_k + 128.0, 1.0, 0.0).astype(BF16)

    sub = lax.broadcasted_iota(jnp.int32, (SUB, NZ), 0)
    own_elements = (sub >= 1) & (sub <= BX)
    for copy in u_loads:
        copy.wait()

    def pairs_of(ref, row):
        return [x_pairs(ref[m, row]) for m in range(3)]

    def strain_step(row, low):
        high = pairs_of(ux, row + 1)
        for n, value in enumerate(strain_row(low, high)):
            strain_now[n, row - 1] = jnp.where(own_elements, 0.25 * value, 0.0)
        return high

    by_rows(1, 1 + BY, 8, strain_step, pairs_of(ux, 1))

    picked = []
    for n in range(6):
        high, low = split(strain_now[n].reshape(BY * SUB, NZ))
        rows = mm(high, onehot_k[...]) + mm(low, onehot_k[...])
        picked.append(jnp.sum(rows * onehot_r8[...], axis=0, keepdims=True))
    eps = jnp.concatenate(picked + [jnp.zeros((2, SLOTS), F32)], axis=0)
    eps_high = eps.astype(BF16).astype(F32)
    stacked = jnp.concatenate(
        [eps_high, eps - eps_high, eps_high, jnp.zeros((104, SLOTS), F32)], axis=0
    )
    inputs_t[...] = stacked.T.astype(BF16)

    w_in = jnp.concatenate([w_in_ref[...], jnp.zeros((2, HID), F32)], axis=0)
    w_in_high = w_in.astype(BF16).astype(F32)
    w_first = jnp.concatenate(
        [w_in_high, w_in_high, w_in - w_in_high, jnp.zeros((104, HID), F32)], axis=0
    ).astype(BF16)
    to_row = lax.broadcasted_iota(jnp.int32, (128, 42), 0)
    from_out = lax.broadcasted_iota(jnp.int32, (128, 42), 1)
    place = jnp.where(
        (from_out == (to_row // 8) * 6 + to_row % 8) & (to_row % 8 < 6) & (to_row < 56), 1.0, 0.0
    ).astype(BF16)
    head_high, head_low = split(w_head_ref[...])
    head_high = mm(place, head_high).T.astype(BF16)
    head_low = mm(place, head_low).T.astype(BF16)
    halves = []
    for layer in range(HIDDEN_LAYERS):
        weight_loads[layer].wait()
        halves.append(split(weights[layer]))

    def product(hidden, parts):
        high, low = split(hidden)
        return mm(high, parts[0]) + (mm(low, parts[0]) + mm(high, parts[1]))

    half = SLOTS // 2
    left, right = mm(inputs_t[0:half], w_first), mm(inputs_t[half:SLOTS], w_first)
    for parts in halves + [(head_high, head_low)]:
        left = product(jnp.tanh(left), parts)
        right = product(jnp.tanh(right), parts)
    out_t[:, 0:half] = left.T
    out_t[:, half:SLOTS] = right.T

    for copy in mass_loads:
        copy.wait()
    pl.semaphore_wait(barrier, peers - 1)
    mass_copies = []
    for q, ((dx, dy), device) in enumerate(zip(DIRECTIONS, neighbours)):
        sy, sx, ty, tx = face(dx, dy, 2)
        kind = 0 if dy == 0 else (1 if dx == 0 else 2)
        copy = pltpu.make_async_remote_copy(
            mass_part.at[sy, sx], mass_rx.at[kind, ty, tx], mass_send.at[q], mass_recv.at[q],
            device_id=device, device_id_type=MESH,
        )
        copy.start()
        mass_copies.append(copy)

    values[0:6] = out_t[0:6]
    values[LIVE : LIVE + 1] = jnp.ones((1, SLOTS), F32)
    factor = [out_t[8 * (a + 1) : 8 * (a + 2)] for a in range(6)]
    for at, (a, b) in enumerate(PAIRS):
        values[FIRST_PAIR + at : FIRST_PAIR + at + 1] = jnp.sum(
            factor[a] * factor[b], axis=0, keepdims=True
        ) * (1.0 / 6.0)

    def scatter_group(at):
        for n in range(GROUP):
            high, low = split(values[at * GROUP + n : at * GROUP + n + 1])
            rows = onehot_r[...]
            lhs[n * COLUMNS : (n + 1) * COLUMNS] = rows * high
            lhs[(GROUP + n) * COLUMNS : (GROUP + n + 1) * COLUMNS] = rows * low
        if at == 0:
            spread = mm(lhs[...], onehot_kt[...])
            return spread[: GROUP * COLUMNS] + spread[GROUP * COLUMNS :]
        return mm(lhs[: GROUP * COLUMNS], onehot_kt[...]) + mm(lhs[GROUP * COLUMNS :], onehot_kt[...])

    def element_rows(spread, n, g):
        start = n * COLUMNS + g * SUB
        both = spread[start : start + SUB]
        return pltpu.roll(both, 1, 0), pltpu.roll(both, 5, 0)

    def sum_copies(parity):
        copies = []
        for q, ((dx, dy), device) in enumerate(zip(DIRECTIONS, neighbours)):
            sy, sx, ty, tx = face(dx, dy, 2)
            kind = 0 if dy == 0 else (1 if dx == 0 else 2)
            copies.append(
                pltpu.make_async_remote_copy(
                    v2.at[:, sy, sx], sum_rx.at[parity, kind, :, ty, tx],
                    sum_send.at[parity, q], sum_recv.at[parity, q],
                    device_id=device, device_id_type=MESH,
                )
            )
        return copies

    def exact_copies(parity):
        copies = []
        for q, ((dx, dy), device) in enumerate(zip(DIRECTIONS, neighbours)):
            sy, sx, ty, tx = face(dx, dy, 1)
            copies.append(
                pltpu.make_async_remote_copy(
                    v1.at[:, sy, sx], copy_rx.at[parity, :, ty, tx],
                    copy_send.at[parity, q], copy_recv.at[parity, q],
                    device_id=device, device_id_type=MESH,
                )
            )
        return copies

    global_x = index_x * BX + sub - 1
    keep_x = jnp.where(
        (global_x >= 0) & (global_x < size_x * BX) & (sub < SUB - 1), 1.0, 0.0
    )
    own_planes = (sub >= 1) & (sub <= NODES_X)
    rim_planes = ((sub <= 1) & (index_x > 0)) | ((sub >= NODES_X) & (sub <= NODES_X + 1))
    halo_planes = (sub == 0) | (sub == NODES_X + 1)
    flank_low, corner_low = own_planes & (index_y > 0), rim_planes & (index_y > 0)
    valid_elements = (sub <= BX + 1) & ((sub >= 1) | (index_x > 0))

    def keep_of(row):
        global_y = index_y * BY + row - 1
        inside = jnp.where((global_y >= 0) & (global_y < size_y * BY), 1.0, 0.0)
        return keep_x * inside

    def assembled(part, received, row):
        at_rim = isinstance(row, int)
        total = jnp.zeros((SUB, NZ), F32)
        if not at_rim or 1 <= row <= NODES_Y:
            total = part + jnp.where(rim_planes, received(0), 0.0)
        if at_rim:
            flank, corner = (flank_low, corner_low) if row <= 1 else (own_planes, rim_planes)
            total = total + jnp.where(flank, received(1), 0.0) + jnp.where(corner, received(2), 0.0)
        return total

    def all_rows(body):
        for row in (0, 1, NODES_Y, NODES_Y + 1):
            body(row)

        def inner(row, carry):
            body(row)
            return carry

        by_rows(2, NODES_Y, 5, inner, 0)

    def stress_now(row):
        scale = 0.25 * modulus[row]
        base = scale * (1.0 - 0.75 * scattered[LIVE, row])
        eps_row = [strain_now[n, row] for n in range(6)]
        trace = LAME_FIRST * (eps_row[0] + eps_row[1] + eps_row[2])
        elastic = [trace + 2.0 * LAME_SECOND * eps_row[n] for n in range(3)]
        elastic += [LAME_SECOND * eps_row[n] for n in range(3, 6)]
        return [base * elastic[n] + scale * scattered[n, row] for n in range(6)]

    zero = jnp.zeros((SUB, NZ), F32)
    no_parts = [(zero, zero)] * 3

    def residual_step(row, before):
        parts = force_parts(stress_now(row - 1))
        for m in range(3):
            force = force_of(parts[m][0] + before[m][0], parts[m][1] + before[m][1])
            v2[m, row] = jnp.where(own_planes, lx[m, row] - force, 0.0)
        return [(parts[m][0], parts[m][2]) for m in range(3)]

    spread = scatter_group(0)
    for n in range(GROUP):
        for g in range(BY // 2):
            for odd, entry in enumerate(element_rows(spread, n, g)):
                scattered[n, 2 * g + odd] = jnp.where(own_elements, entry, 0.0)
    for copy in modulus_loads + load_loads:
        copy.wait()
    last = by_rows(1, 1 + BY, 8, residual_step, no_parts)
    for m in range(3):
        v2[m, NODES_Y] = jnp.where(own_planes, lx[m, NODES_Y] - force_of(*last[m]), 0.0)

    first_copies = sum_copies(0)
    for copy in first_copies:
        copy.start()

    tangent_copies = []
    planes = slice(1, 1 + BX)
    for group in range(N_PAIRS // GROUP):
        spread = scatter_group(group + 1)
        for g in range(BY // 2):
            scales = [modulus[2 * g + odd] * (1.0 / 16.0) for odd in range(2)]
            bases = [scales[odd] * (1.0 - 0.75 * scattered[LIVE, 2 * g + odd]) for odd in range(2)]
            for n in range(GROUP):
                at = group * GROUP + n
                for odd, entry in enumerate(element_rows(spread, n, g)):
                    entry = scales[odd] * entry
                    if iso(*PAIRS[at]):
                        entry = entry + bases[odd] * iso(*PAIRS[at])
                    tangent[at, 2 * g + odd + 1, planes] = entry[planes]
        entries = pl.ds(group * GROUP, GROUP)
        for q, ((dx, dy), device) in enumerate(zip(DIRECTIONS, neighbours)):
            sy, sx, ty, tx = element_face(dx, dy)
            copy = pltpu.make_async_remote_copy(
                tangent.at[entries, sy, sx], tangent.at[entries, ty, tx],
                tan_send.at[group, q], tan_recv.at[group, q],
                device_id=device, device_id_type=MESH,
            )
            copy.start()
            tangent_copies.append(copy)

    for ref in (q1, q0, d1, x):
        ref[...] = jnp.zeros_like(ref)
    for copy in mass_copies:
        copy.wait()

    def mass_row(row):
        mass_full[row] = assembled(mass_part[row], lambda kind: mass_rx[kind, row], row)

    all_rows(mass_row)
    for copy in first_copies:
        copy.wait()

    def start_row(row):
        keep = keep_of(row)
        for m in range(3):
            part = None if isinstance(row, int) and row in (0, NODES_Y + 1) else v2[m, row]
            v0[m, row] = keep * assembled(part, lambda kind: sum_rx[0, kind, m, row], row)

    all_rows(start_row)
    for copy in tangent_copies:
        copy.wait()

    def stress_row(row, strain, present):
        entries = [tangent[at, row] for at in range(N_PAIRS)]
        result = []
        for a in range(6):
            total = entries[PAIR_OF[a, 0]] * strain[0]
            for b in range(1, 6):
                total = total + entries[PAIR_OF[a, b]] * strain[b]
            result.append(jnp.where(present, total, 0.0))
        return result

    def first_image(row, carry):
        low, before = carry
        high = pairs_of(v0, row + 1)
        present = valid_elements & (row + index_y > 0)
        parts = force_parts(stress_row(row, strain_row(low, high), present))
        keep = keep_of(row)
        for m in range(3):
            force = force_of(parts[m][0] + before[m][0], parts[m][1] + before[m][1])
            v1[m, row] = keep * (force + mass_full[row] * v0[m, row])
        return high, [(parts[m][0], parts[m][2]) for m in range(3)]

    def second_image(row, carry):
        low, before, sums = carry
        high = pairs_of(v1, row + 1)
        parts = force_parts(stress_row(row, strain_row(low, high), own_elements))
        rr, r_ar, ar_ar, ar_aar = sums
        for m in range(3):
            here, image = v0[m, row], v1[m, row]
            force = force_of(parts[m][0] + before[m][0], parts[m][1] + before[m][1])
            force = force + mass_part[row] * image
            v2[m, row] = force
            rr = rr + here * here
            r_ar = r_ar + here * image
            ar_ar = ar_ar + image * image
            ar_aar = ar_aar + image * force
        return high, [(parts[m][0], parts[m][2]) for m in range(3)], (rr, r_ar, ar_ar, ar_aar)

    lane = lax.broadcasted_iota(jnp.int32, (1, 128), 1)

    def outer(step, carry):
        be0, ia1, ia0, rr_before = carry
        parity = lax.rem(step, 2)
        sum_parity = lax.rem(step + 1, 2)
        by_rows(0, BY + 2, 6, first_image, (pairs_of(v0, 0), no_parts))
        exact = exact_copies(parity)
        for copy in exact:
            copy.start()
        _, before, sums = by_rows(
            1, 1 + BY, 8, second_image, (pairs_of(v1, 1), no_parts, (zero,) * 4)
        )
        ar_aar = sums[3]
        for m in range(3):
            image = v1[m, NODES_Y]
            force = force_of(*before[m]) + mass_part[NODES_Y] * image
            v2[m, NODES_Y] = force
            ar_aar = ar_aar + jnp.where(own_planes, image * force, 0.0)
        summed = sum_copies(sum_parity)
        for copy in summed:
            copy.start()

        message = jnp.zeros((1, 128), F32)
        for at, (value, mask) in enumerate(
            ((sums[0], own_elements), (sums[1], own_elements), (sums[2], own_elements), (ar_aar, own_planes))
        ):
            total = jnp.sum(jnp.where(mask, value, 0.0), axis=0, keepdims=True)
            total = jnp.sum(total, axis=1, keepdims=True)
            message = message + jnp.where(lane == at, total, 0.0)
        gathered[parity, me] = message

        for device in others:
            pltpu.make_async_remote_copy(
                gathered.at[parity, me], gathered.at[parity, me],
                all_send.at[parity], all_recv.at[parity],
                device_id=device, device_id_type=MESH,
            ).start()
        for copy in exact + summed:
            copy.wait()

        def image_row(row):
            keep = keep_of(row)
            outside = isinstance(row, int) and row in (0, NODES_Y + 1)
            for m in range(3):
                rim = copy_rx[parity, m, row]
                if outside:
                    ar2 = jnp.where(sub <= NODES_X + 1, rim, 0.0)
                else:
                    ar2 = jnp.where(halo_planes, rim, v1[m, row])
                ar2 = keep * ar2
                part = None if outside else v2[m, row]
                v2[m, row] = keep * assembled(part, lambda kind: sum_rx[sum_parity, kind, m, row], row)
                v1[m, row] = ar2
                q0[m, row] = (q1[m, row] - be0 * q0[m, row] - ar2) * ia1

        all_rows(image_row)
        rest = gathered.at[parity, 0 : peers - 1]
        pltpu.make_async_copy(rest, rest, all_recv.at[parity]).wait()
        totals = [jnp.sum(gathered[parity, at : at + 16], axis=0) for at in range(0, peers, 16)]
        while len(totals) > 1:
            totals = [a + b for a, b in zip(totals[0::2], totals[1::2])]
        totals = totals[0]
        rr2, m1, m2, m3 = [
            jnp.sum(jnp.where(lane == at, totals, 0.0), axis=1, keepdims=True) for at in range(4)
        ]
        be1 = jnp.where(step == 0, 0.0, rr2 / rr_before)
        r_q1 = -rr2 * ia1
        ar_q1 = (r_q1 - m1) * ia1
        q1_q1 = (rr_before + rr2) * ia1 * ia1
        ar_q0 = rr2 * ia1 * ia0
        q1_q0 = -rr_before * ia1 * ia0
        q1_aar = ia1 * (ar_q1 - be0 * ar_q0 - m2)
        q1_aq1 = ia1 * (q1_q1 - be0 * q1_q0 - ar_q1)
        q2_q2 = m2 + 2.0 * be1 * ar_q1 + be1 * be1 * q1_q1
        ar_q2 = m2 + be1 * ar_q1
        q2_aq2 = m3 + 2.0 * be1 * q1_aar + be1 * be1 * q1_aq1
        a2 = rr2 / (m1 + be1 * r_q1)
        rr3 = a2 * a2 * q2_q2 - rr2
        be2 = rr3 / rr2
        a3 = rr3 / (m1 - 2.0 * a2 * ar_q2 + a2 * a2 * q2_aq2 - be2 * rr3 / a2)

        def update_row(row, unused):
            for m in range(3):
                ar2, old = v1[m, row], q1[m, row]
                q2 = ar2 + be1 * old
                r3 = v0[m, row] - a2 * q2
                q3 = ar2 - a2 * (v2[m, row] + be1 * q0[m, row]) + be2 * q2
                d2 = v0[m, row] + be1 * d1[m, row]
                d3 = r3 + be2 * d2
                x[m, row] = x[m, row] + (a2 * d2 + a3 * d3)
                v0[m, row] = r3 - a3 * q3
                q1[m, row] = q3
                q0[m, row] = q2
                d1[m, row] = d3
            return unused

        by_rows(0, ROWS - 1, 6, update_row, 0)
        update_row(ROWS - 1, 0)
        pltpu.make_async_copy(rest, rest, all_send.at[parity]).wait()
        return be2, 1.0 / a3, 1.0 / a2, rr3

    none = jnp.zeros((1, 1), F32)
    lax.fori_loop(0, OUTER, outer, (none, none, none, none + 1.0))

    stores = [
        pltpu.make_async_copy(x, increment_hbm, out_sem.at[0]),
        pltpu.make_async_copy(v0, residual_hbm, out_sem.at[1]),
    ]
    for copy in stores:
        copy.start()
    for copy in stores:
        copy.wait()


def place_kernel(increment_in, residual_in, increment_out, residual_out, sem):
    copies = []
    for at, (source, target) in enumerate(((increment_in, increment_out), (residual_in, residual_out))):
        for i in range(NODES_X):
            for m in range(3):
                copies.append(
                    pltpu.make_async_copy(
                        source.at[m, 1:18, i + 1 : i + 2], target.at[i, :, m : m + 1], sem.at[at, m, i]
                    )
                )
    for copy in copies:
        copy.start()
    for copy in copies:
        copy.wait()


def solution(mesh):
    size_x, size_y = mesh.shape["gx"], mesh.shape["gy"]
    peers = size_x * size_y
    held = jax.ShapeDtypeStruct((3, ROWS, SUB, NZ), F32)
    field = jax.ShapeDtypeStruct((NODES_X, NODES_Y, 3, NZ), F32)

    def vmem(*shape, dtype=F32):
        return pltpu.VMEM(shape, dtype)

    def node(*lead):
        return vmem(*lead, ROWS, SUB, NZ)

    dma = pltpu.SemaphoreType.DMA
    scratch = [
        vmem(1, SLOTS, dtype=jnp.int32), vmem(1, 1, dtype=jnp.int32), vmem(6, HID), vmem(42, HID),
        node(3), node(3), node(), node(), node(3), vmem(BY, SUB, NZ), vmem(HIDDEN_LAYERS, HID, HID),
        vmem(6, BY, SUB, NZ), vmem(NZ, SLOTS, dtype=BF16), vmem(SLOTS, NZ, dtype=BF16),
        vmem(COLUMNS, SLOTS, dtype=BF16), vmem(BY * SUB, SLOTS), vmem(SLOTS, 128, dtype=BF16),
        vmem(128, SLOTS), vmem(32, SLOTS), vmem(2 * GROUP * COLUMNS, SLOTS, dtype=BF16),
        vmem(GROUP, BY, SUB, NZ),
        vmem(N_PAIRS, BY + 2, SUB, NZ),
        node(3), node(3), node(3), node(3), node(3), node(3), node(3),
        node(2, 3, 3), node(2, 3), vmem(2, peers, 1, 128),
        dma((10, 5)), dma((2,)), dma((8,)), dma((8,)), dma((3, 8)), dma((3, 8)),
        dma((2, 8)), dma((2, 8)), dma((2, 8)), dma((2, 8)), dma((2,)), dma((2,)),
    ]

    def body(u_now, load, mass, modulus, plastic_ids, plastic_count, w_in, w_hidden, w_head):
        hbm = pl.BlockSpec(memory_space=pl.ANY)
        increment, residual = pl.pallas_call(
            lambda *refs: kernel(size_x, size_y, *refs),
            out_shape=(held, held),
            in_specs=[hbm] * 9,
            out_specs=(hbm, hbm),
            scratch_shapes=scratch,
            compiler_params=pltpu.CompilerParams(
                collective_id=0, has_side_effects=True, vmem_limit_bytes=60 * 2**20
            ),
        )(
            u_now.transpose(1, 2, 0, 3), load.transpose(1, 2, 0, 3), mass, modulus,
            plastic_ids.reshape(1, SLOTS), plastic_count, w_in, w_hidden, w_head.T,
        )
        increment, residual = pl.pallas_call(
            place_kernel,
            out_shape=(field, field),
            in_specs=[pl.BlockSpec(memory_space=pltpu.VMEM)] * 2,
            out_specs=(hbm, hbm),
            scratch_shapes=[dma((2, 3, 5))],
        )(increment, residual)
        return increment.transpose(2, 0, 1, 3), residual.transpose(2, 0, 1, 3)

    split_field = P(None, "gx", "gy", None)
    split_block = P("gx", "gy", None)
    return jax.shard_map(
        body,
        mesh=mesh,
        in_specs=(
            split_field, split_field, split_block, split_block, split_block, P("gx", "gy"), P(), P(), P(),
        ),
        out_specs=(split_field, split_field),
        check_vma=False,
    )
```

```python
import jax
import jax.numpy as jnp
from jax import lax
from jax.experimental import pallas as pl
from jax.experimental.pallas import tpu as pltpu
from jax.sharding import PartitionSpec as P

MESH = pl.DeviceIdType.MESH
F32, BF16 = jnp.float32, jnp.bfloat16
LAME_FIRST = 0.3 / (1.3 * 0.4)
LAME_SECOND = 1.0 / 2.6

BX, BY, NZ = 4, 16, 256
NODES_X, NODES_Y = BX + 1, BY + 1
ROWS = BY + 3
SUB = 8
SLOTS, HID, HIDDEN_LAYERS = 1024, 512, 3
COLUMNS = BY * BX
OUTER = 3
GROUP = 7
RINGS = 4

PAIRS = [(a, b) for a in range(6) for b in range(a, 6)]
PAIR_OF = {}
for _at, (_a, _b) in enumerate(PAIRS):
    PAIR_OF[_a, _b] = PAIR_OF[_b, _a] = _at
N_PAIRS = len(PAIRS)
N_SCATTER = 28
LIVE, FIRST_PAIR = 6, 7

DIRECTIONS = [(dx, dy) for dx in (-1, 1) for dy in (-1, 1)] + [(0, -1), (0, 1), (-1, 0), (1, 0)]
FACES = 2


def iso(a, b):
    if a < 3 and b < 3:
        return LAME_FIRST + (2.0 * LAME_SECOND if a == b else 0.0)
    return LAME_SECOND if a == b else 0.0


def z_next(values):
    lane = lax.broadcasted_iota(jnp.int32, values.shape, 1)
    return jnp.where(lane == NZ - 1, 0.0, pltpu.roll(values, NZ - 1, 1))


def z_prev(values):
    lane = lax.broadcasted_iota(jnp.int32, values.shape, 1)
    return jnp.where(lane == 0, 0.0, pltpu.roll(values, 1, 1))


def x_pairs(values):
    upper = pltpu.roll(values, SUB - 1, 0)
    return upper + values, upper - values


def strain_row(low, high):
    a = [low[m][1] + high[m][1] for m in range(3)]
    b = [high[m][0] - low[m][0] for m in range(3)]
    c = [high[m][0] + low[m][0] for m in range(3)]
    yz, xz, xy = c[1] + b[2], c[0] + a[2], b[0] + a[1]
    return [
        z_next(a[0]) + a[0],
        z_next(b[1]) + b[1],
        z_next(c[2]) - c[2],
        z_next(yz) + (b[2] - c[1]),
        z_next(xz) + (a[2] - c[0]),
        z_next(xy) + xy,
    ]


def force_parts(stress):
    before = [z_prev(s) for s in stress]
    total = {n: stress[n] + before[n] for n in (0, 1, 3, 4, 5)}
    differ = {n: before[n] - stress[n] for n in (2, 3, 4)}
    parts = []
    for along_x, along_y, along_z in ((0, 5, 4), (5, 1, 3), (4, 3, 2)):
        parts.append(
            (
                total[along_x],
                differ[along_z] - total[along_y],
                differ[along_z] + total[along_y],
            )
        )
    return parts


def force_of(along_x, other):
    return pltpu.roll(along_x + other, 1, 0) + (other - along_x)


def split(values):
    high = values.astype(BF16)
    return high, (values - high.astype(F32)).astype(BF16)


def mm(a, b):
    return jnp.dot(a, b, preferred_element_type=F32)


def face(dx, dy, depth):
    if depth == 2:
        sx = {-1: slice(1, 3), 0: slice(1, 6), 1: slice(4, 6)}[dx]
        tx = {-1: slice(5, 7), 0: slice(1, 6), 1: slice(0, 2)}[dx]
        sy = {-1: slice(1, 3), 0: slice(1, 18), 1: slice(16, 18)}[dy]
        ty = {-1: slice(17, 19), 0: slice(1, 18), 1: slice(0, 2)}[dy]
    else:
        sx = {-1: slice(2, 3), 0: slice(1, 6), 1: slice(4, 5)}[dx]
        tx = {-1: slice(6, 7), 0: slice(1, 6), 1: slice(0, 1)}[dx]
        sy = {-1: slice(2, 3), 0: slice(1, 18), 1: slice(16, 17)}[dy]
        ty = {-1: slice(18, 19), 0: slice(1, 18), 1: slice(0, 1)}[dy]
    return sy, sx, ty, tx


def element_face(dx, dy):
    sx = {-1: slice(1, 2), 0: slice(1, 5), 1: slice(4, 5)}[dx]
    tx = {-1: slice(5, 6), 0: slice(1, 5), 1: slice(0, 1)}[dx]
    sy = {-1: slice(1, 2), 0: slice(1, 17), 1: slice(16, 17)}[dy]
    ty = {-1: slice(17, 18), 0: slice(1, 17), 1: slice(0, 1)}[dy]
    return sy, sx, ty, tx


def all_offsets(size_x, size_y):
    offsets = [
        (z, core, x, y)
        for z in range(size_x // 2)
        for core in range(2)
        for x in range(size_y // RINGS)
        for y in range(RINGS)
    ][1:]

    def hops(offset):
        z, core, x, y = offset
        return sum(min(d, RINGS - d) for d in (z, x, y)) * 2 + core

    return sorted(offsets, key=hops, reverse=True)


def by_rows(first, last, width, body, carry):
    assert (last - first) % width == 0

    def block(at, carry):
        for n in range(width):
            carry = body(first + at * width + n, carry)
        return carry

    return lax.fori_loop(0, (last - first) // width, block, carry)


def kernel(
    size_x, size_y,
    u_hbm, load_hbm, mass_hbm, modulus_hbm, ids_hbm, count_hbm, w_in_hbm, w_hidden_hbm, w_head_hbm,
    increment_hbm, residual_hbm,
    ids_ref, count_ref, w_in_ref, w_head_ref, ux, lx, mass_part, mass_full, mass_rx, modulus, weights,
    strain_now, packed, onehot_k, onehot_kt, onehot_r, inputs_t, out_t, values, lhs, scattered,
    tangent,
    v0, v1, v2, q1, q0, d1, x, sum_rx, copy_rx, gathered,
    load_sem, out_sem, mass_send, mass_recv, tan_send, tan_recv,
    sum_send, sum_recv, copy_send, copy_recv, all_send, all_recv,
):
    index_x, index_y = lax.axis_index("gx"), lax.axis_index("gy")
    me = index_x * size_y + index_y
    peers = size_x * size_y
    neighbours = [
        (lax.rem(index_x + dx + size_x, size_x), lax.rem(index_y + dy + size_y, size_y))
        for dx, dy in DIRECTIONS
    ]

    ring_x, ring_y = index_y // RINGS, lax.rem(index_y, RINGS)
    ring_z, core = index_x // 2, lax.rem(index_x, 2)
    at_z = [lax.rem(ring_z + d, RINGS) * 2 for d in range(size_x // 2)]
    at_core = [core, 1 - core]
    at_ring_x = [lax.rem(ring_x + d, RINGS) * RINGS for d in range(size_y // RINGS)]
    at_ring_y = [lax.rem(ring_y + d, RINGS) for d in range(RINGS)]
    along_gx = [[z + c for c in at_core] for z in at_z]
    along_gy = [[a + b for b in at_ring_y] for a in at_ring_x]
    others = [
        (along_gx[z][c], along_gy[a][b]) for z, c, a, b in all_offsets(size_x, size_y)
    ]

    for ref in (mass_part, modulus):
        ref[...] = jnp.zeros_like(ref)
    small = ((ids_hbm, ids_ref), (count_hbm, count_ref), (w_in_hbm, w_in_ref), (w_head_hbm, w_head_ref))
    small_loads = [
        pltpu.make_async_copy(source, target, load_sem.at[9, at])
        for at, (source, target) in enumerate(small)
    ]
    u_loads, modulus_loads, mass_loads, load_loads, weight_loads = [], [], [], [], []
    for i in range(NODES_X):
        for m in range(3):
            u_loads.append(pltpu.make_async_copy(u_hbm.at[i, :, m : m + 1], ux.at[m, 1:18, i + 1 : i + 2], load_sem.at[m, i]))
    for layer in range(HIDDEN_LAYERS):
        weight_loads.append(pltpu.make_async_copy(w_hidden_hbm.at[layer], weights.at[layer], load_sem.at[8, layer]))
    for i in range(BX):
        modulus_loads.append(pltpu.make_async_copy(modulus_hbm.at[i], modulus.at[:, i + 1], load_sem.at[6, i]))
    for i in range(NODES_X):
        mass_loads.append(pltpu.make_async_copy(mass_hbm.at[i], mass_part.at[1:18, i + 1], load_sem.at[7, i]))
        for m in range(3):
            load_loads.append(pltpu.make_async_copy(load_hbm.at[i, :, m : m + 1], lx.at[m, 1:18, i + 1 : i + 2], load_sem.at[3 + m, i]))
    loads = small_loads + u_loads + weight_loads + modulus_loads + mass_loads + load_loads
    for copy in loads:
        copy.start()

    barrier = pltpu.get_barrier_semaphore()
    for device in others:
        pl.semaphore_signal(barrier, inc=1, device_id=device, device_id_type=MESH)
    for copy in small_loads:
        copy.wait()

    ids = ids_ref[...]
    slot = lax.broadcasted_iota(jnp.int32, (1, SLOTS), 1)
    live = jnp.where(slot < count_ref[...], 1.0, 0.0)
    at_k = ids & (NZ - 1)
    at_j = (ids >> 8) & (BY - 1)
    at_i = ids >> 12
    onehot_k[...] = jnp.where(
        lax.broadcasted_iota(jnp.int32, (NZ, SLOTS), 0) == at_k, 1.0, 0.0
    ).astype(BF16)
    onehot_r[...] = jnp.where(
        lax.broadcasted_iota(jnp.int32, (COLUMNS, SLOTS), 0) == at_j * BX + at_i, live, 0.0
    ).astype(BF16)
    k_column = jnp.broadcast_to(at_k.astype(F32), (128, SLOTS)).T
    lane_k = lax.broadcasted_iota(jnp.int32, (SLOTS, 128), 1).astype(F32)
    onehot_kt[:, 0:128] = jnp.where(k_column == lane_k, 1.0, 0.0).astype(BF16)
    onehot_kt[:, 128:256] = jnp.where(k_column == lane_k + 128.0, 1.0, 0.0).astype(BF16)

    sub = lax.broadcasted_iota(jnp.int32, (SUB, NZ), 0)
    own_elements = (sub >= 1) & (sub <= BX)
    for copy in u_loads:
        copy.wait()

    def pairs_of(ref, row):
        return [x_pairs(ref[m, row]) for m in range(3)]

    def strain_step(row, low):
        high = pairs_of(ux, row + 1)
        for n, value in enumerate(strain_row(low, high)):
            strain_now[n, row - 1] = jnp.where(own_elements, 0.25 * value, 0.0)
        return high

    by_rows(1, 1 + BY, 8, strain_step, pairs_of(ux, 1))

    picked = []
    for n in range(6):
        for g in range(BY // 2):
            pair = jnp.where(
                sub < BX,
                pltpu.roll(strain_now[n, 2 * g], SUB - 1, 0),
                pltpu.roll(strain_now[n, 2 * g + 1], BX - 1, 0),
            )
            high = pair.astype(BF16).astype(F32)
            packed[n * COLUMNS + g * SUB : n * COLUMNS + (g + 1) * SUB] = high
            packed[(6 + n) * COLUMNS + g * SUB : (6 + n) * COLUMNS + (g + 1) * SUB] = pair - high
    at_slots = mm(packed[...].astype(BF16), onehot_k[...])
    for n in range(6):
        rows = at_slots[n * COLUMNS : (n + 1) * COLUMNS] + at_slots[(6 + n) * COLUMNS : (7 + n) * COLUMNS]
        picked.append(jnp.sum(rows * onehot_r[...].astype(F32), axis=0, keepdims=True))
    eps = jnp.concatenate(picked + [jnp.zeros((2, SLOTS), F32)], axis=0)
    eps_high = eps.astype(BF16).astype(F32)
    stacked = jnp.concatenate(
        [eps_high, eps - eps_high, eps_high, jnp.zeros((104, SLOTS), F32)], axis=0
    )
    inputs_t[...] = stacked.T.astype(BF16)

    w_in = jnp.concatenate([w_in_ref[...], jnp.zeros((2, HID), F32)], axis=0)
    w_in_high = w_in.astype(BF16).astype(F32)
    w_first = jnp.concatenate(
        [w_in_high, w_in_high, w_in - w_in_high, jnp.zeros((104, HID), F32)], axis=0
    ).astype(BF16)
    to_row = lax.broadcasted_iota(jnp.int32, (128, 42), 0)
    from_out = lax.broadcasted_iota(jnp.int32, (128, 42), 1)
    place = jnp.where(
        (from_out == (to_row // 8) * 6 + to_row % 8) & (to_row % 8 < 6) & (to_row < 56), 1.0, 0.0
    ).astype(BF16)
    head_high, head_low = split(w_head_ref[...])
    head_high = mm(place, head_high).T.astype(BF16)
    head_low = mm(place, head_low).T.astype(BF16)
    halves = []
    for layer in range(HIDDEN_LAYERS):
        weight_loads[layer].wait()
        halves.append(split(weights[layer]))

    def product(hidden, parts):
        high, low = split(hidden)
        return mm(high, parts[0]) + (mm(low, parts[0]) + mm(high, parts[1]))

    half = SLOTS // 2
    left, right = mm(inputs_t[0:half], w_first), mm(inputs_t[half:SLOTS], w_first)
    for parts in halves + [(head_high, head_low)]:
        left = product(jnp.tanh(left), parts)
        right = product(jnp.tanh(right), parts)
    out_t[:, 0:half] = left.T
    out_t[:, half:SLOTS] = right.T

    for copy in mass_loads:
        copy.wait()
    pl.semaphore_wait(barrier, peers - 1)
    mass_copies = []
    for q, ((dx, dy), device) in enumerate(zip(DIRECTIONS, neighbours)):
        sy, sx, ty, tx = face(dx, dy, 2)
        kind = 0 if dy == 0 else (1 if dx == 0 else 2)
        copy = pltpu.make_async_remote_copy(
            mass_part.at[sy, sx], mass_rx.at[kind, ty, tx], mass_send.at[q], mass_recv.at[q],
            device_id=device, device_id_type=MESH,
        )
        copy.start()
        mass_copies.append(copy)

    values[0:6] = out_t[0:6]
    values[LIVE : LIVE + 1] = jnp.ones((1, SLOTS), F32)
    factor = [out_t[8 * (a + 1) : 8 * (a + 2)] for a in range(6)]
    for at, (a, b) in enumerate(PAIRS):
        values[FIRST_PAIR + at : FIRST_PAIR + at + 1] = jnp.sum(
            factor[a] * factor[b], axis=0, keepdims=True
        ) * (1.0 / 6.0)

    def scatter_group(at):
        for n in range(GROUP):
            high, low = split(values[at * GROUP + n : at * GROUP + n + 1])
            rows = onehot_r[...]
            lhs[n * COLUMNS : (n + 1) * COLUMNS] = rows * high
            lhs[(GROUP + n) * COLUMNS : (GROUP + n + 1) * COLUMNS] = rows * low
        if at == 0:
            spread = mm(lhs[...], onehot_kt[...])
            return spread[: GROUP * COLUMNS] + spread[GROUP * COLUMNS :]
        return mm(lhs[: GROUP * COLUMNS], onehot_kt[...]) + mm(lhs[GROUP * COLUMNS :], onehot_kt[...])

    def element_rows(spread, n, g):
        start = n * COLUMNS + g * SUB
        both = spread[start : start + SUB]
        return pltpu.roll(both, 1, 0), pltpu.roll(both, 5, 0)

    def sum_copies(parity):
        copies = []
        for q, ((dx, dy), device) in enumerate(zip(DIRECTIONS, neighbours)):
            sy, sx, ty, tx = face(dx, dy, 2)
            kind = 0 if dy == 0 else (1 if dx == 0 else 2)
            copies.append(
                pltpu.make_async_remote_copy(
                    v2.at[:, sy, sx], sum_rx.at[parity, kind, :, ty, tx],
                    sum_send.at[parity, q], sum_recv.at[parity, q],
                    device_id=device, device_id_type=MESH,
                )
            )
        return copies

    def exact_copies(parity):
        copies = []
        for q, ((dx, dy), device) in enumerate(zip(DIRECTIONS, neighbours)):
            sy, sx, ty, tx = face(dx, dy, 1)
            copies.append(
                pltpu.make_async_remote_copy(
                    v1.at[:, sy, sx], copy_rx.at[parity, :, ty, tx],
                    copy_send.at[parity, q], copy_recv.at[parity, q],
                    device_id=device, device_id_type=MESH,
                )
            )
        return copies

    global_x = index_x * BX + sub - 1
    keep_x = jnp.where(
        (global_x >= 0) & (global_x < size_x * BX) & (sub < SUB - 1), 1.0, 0.0
    )
    own_planes = (sub >= 1) & (sub <= NODES_X)
    rim_planes = ((sub <= 1) & (index_x > 0)) | ((sub >= NODES_X) & (sub <= NODES_X + 1))
    halo_planes = (sub == 0) | (sub == NODES_X + 1)
    flank_low, corner_low = own_planes & (index_y > 0), rim_planes & (index_y > 0)
    valid_elements = (sub <= BX + 1) & ((sub >= 1) | (index_x > 0))

    def keep_of(row):
        global_y = index_y * BY + row - 1
        inside = jnp.where((global_y >= 0) & (global_y < size_y * BY), 1.0, 0.0)
        return keep_x * inside

    def assembled(part, received, row):
        at_rim = isinstance(row, int)
        total = jnp.zeros((SUB, NZ), F32)
        if not at_rim or 1 <= row <= NODES_Y:
            total = part + jnp.where(rim_planes, received(0), 0.0)
        if at_rim:
            flank, corner = (flank_low, corner_low) if row <= 1 else (own_planes, rim_planes)
            total = total + jnp.where(flank, received(1), 0.0) + jnp.where(corner, received(2), 0.0)
        return total

    def all_rows(body):
        for row in (0, 1, NODES_Y, NODES_Y + 1):
            body(row)

        def inner(row, carry):
            body(row)
            return carry

        by_rows(2, NODES_Y, 5, inner, 0)

    def stress_now(row):
        scale = 0.25 * modulus[row]
        base = scale * (1.0 - 0.75 * scattered[LIVE, row])
        eps_row = [strain_now[n, row] for n in range(6)]
        trace = LAME_FIRST * (eps_row[0] + eps_row[1] + eps_row[2])
        elastic = [trace + 2.0 * LAME_SECOND * eps_row[n] for n in range(3)]
        elastic += [LAME_SECOND * eps_row[n] for n in range(3, 6)]
        return [base * elastic[n] + scale * scattered[n, row] for n in range(6)]

    zero = jnp.zeros((SUB, NZ), F32)
    no_parts = [(zero, zero)] * 3

    def residual_step(row, before):
        parts = force_parts(stress_now(row - 1))
        for m in range(3):
            force = force_of(parts[m][0] + before[m][0], parts[m][1] + before[m][1])
            v2[m, row] = jnp.where(own_planes, lx[m, row] - force, 0.0)
        return [(parts[m][0], parts[m][2]) for m in range(3)]

    spread = scatter_group(0)
    for n in range(GROUP):
        for g in range(BY // 2):
            for odd, entry in enumerate(element_rows(spread, n, g)):
                scattered[n, 2 * g + odd] = jnp.where(own_elements, entry, 0.0)
    for copy in modulus_loads + load_loads:
        copy.wait()
    last = by_rows(1, 1 + BY, 8, residual_step, no_parts)
    for m in range(3):
        v2[m, NODES_Y] = jnp.where(own_planes, lx[m, NODES_Y] - force_of(*last[m]), 0.0)

    first_copies = sum_copies(0)
    for copy in first_copies:
        copy.start()

    tangent_copies = []
    planes = slice(1, 1 + BX)
    for group in range(N_PAIRS // GROUP):
        spread = scatter_group(group + 1)
        for g in range(BY // 2):
            scales = [modulus[2 * g + odd] * (1.0 / 16.0) for odd in range(2)]
            bases = [scales[odd] * (1.0 - 0.75 * scattered[LIVE, 2 * g + odd]) for odd in range(2)]
            for n in range(GROUP):
                at = group * GROUP + n
                for odd, entry in enumerate(element_rows(spread, n, g)):
                    entry = scales[odd] * entry
                    if iso(*PAIRS[at]):
                        entry = entry + bases[odd] * iso(*PAIRS[at])
                    tangent[at, 2 * g + odd + 1, planes] = entry[planes]
        entries = pl.ds(group * GROUP, GROUP)
        for q, ((dx, dy), device) in enumerate(zip(DIRECTIONS, neighbours)):
            sy, sx, ty, tx = element_face(dx, dy)
            copy = pltpu.make_async_remote_copy(
                tangent.at[entries, sy, sx], tangent.at[entries, ty, tx],
                tan_send.at[group, q], tan_recv.at[group, q],
                device_id=device, device_id_type=MESH,
            )
            copy.start()
            tangent_copies.append(copy)

    for ref in (q1, q0, d1, x):
        ref[...] = jnp.zeros_like(ref)
    for copy in mass_copies:
        copy.wait()

    def mass_row(row):
        mass_full[row] = assembled(mass_part[row], lambda kind: mass_rx[kind, row], row)

    all_rows(mass_row)
    for copy in first_copies:
        copy.wait()

    def start_row(row):
        keep = keep_of(row)
        for m in range(3):
            part = None if isinstance(row, int) and row in (0, NODES_Y + 1) else v2[m, row]
            v0[m, row] = keep * assembled(part, lambda kind: sum_rx[0, kind, m, row], row)

    all_rows(start_row)
    for copy in tangent_copies:
        copy.wait()

    def stress_row(row, strain, present):
        entries = [tangent[at, row] for at in range(N_PAIRS)]
        result = []
        for a in range(6):
            total = entries[PAIR_OF[a, 0]] * strain[0]
            for b in range(1, 6):
                total = total + entries[PAIR_OF[a, b]] * strain[b]
            result.append(jnp.where(present, total, 0.0))
        return result

    def first_image(row, carry):
        low, before = carry
        high = pairs_of(v0, row + 1)
        present = valid_elements & (row + index_y > 0)
        parts = force_parts(stress_row(row, strain_row(low, high), present))
        keep = keep_of(row)
        for m in range(3):
            force = force_of(parts[m][0] + before[m][0], parts[m][1] + before[m][1])
            v1[m, row] = keep * (force + mass_full[row] * v0[m, row])
        return high, [(parts[m][0], parts[m][2]) for m in range(3)]

    def second_image(row, carry):
        low, before, sums = carry
        high = pairs_of(v1, row + 1)
        parts = force_parts(stress_row(row, strain_row(low, high), own_elements))
        rr, r_ar, ar_ar, ar_aar = sums
        for m in range(3):
            here, image = v0[m, row], v1[m, row]
            force = force_of(parts[m][0] + before[m][0], parts[m][1] + before[m][1])
            force = force + mass_part[row] * image
            v2[m, row] = force
            rr = rr + here * here
            r_ar = r_ar + here * image
            ar_ar = ar_ar + image * image
            ar_aar = ar_aar + image * force
        return high, [(parts[m][0], parts[m][2]) for m in range(3)], (rr, r_ar, ar_ar, ar_aar)

    lane = lax.broadcasted_iota(jnp.int32, (1, 128), 1)

    def outer(step, carry):
        be0, ia1, ia0, rr_before = carry
        parity = lax.rem(step, 2)
        sum_parity = lax.rem(step + 1, 2)
        by_rows(0, BY + 2, 6, first_image, (pairs_of(v0, 0), no_parts))
        exact = exact_copies(parity)
        for copy in exact:
            copy.start()
        _, before, sums = by_rows(
            1, 1 + BY, 8, second_image, (pairs_of(v1, 1), no_parts, (zero,) * 4)
        )
        ar_aar = sums[3]
        for m in range(3):
            image = v1[m, NODES_Y]
            force = force_of(*before[m]) + mass_part[NODES_Y] * image
            v2[m, NODES_Y] = force
            ar_aar = ar_aar + jnp.where(own_planes, image * force, 0.0)
        summed = sum_copies(sum_parity)
        for copy in summed[:-FACES]:
            copy.start()

        message = jnp.zeros((1, 128), F32)
        for at, (value, mask) in enumerate(
            ((sums[0], own_elements), (sums[1], own_elements), (sums[2], own_elements), (ar_aar, own_planes))
        ):
            total = jnp.sum(jnp.where(mask, value, 0.0), axis=0, keepdims=True)
            total = jnp.sum(total, axis=1, keepdims=True)
            message = message + jnp.where(lane == at, total, 0.0)
        gathered[parity, me] = message

        for device in others:
            pltpu.make_async_remote_copy(
                gathered.at[parity, me], gathered.at[parity, me],
                all_send.at[parity], all_recv.at[parity],
                device_id=device, device_id_type=MESH,
            ).start()
        for copy in summed[-FACES:]:
            copy.start()
        for copy in exact + summed:
            copy.wait()

        def image_row(row):
            keep = keep_of(row)
            outside = isinstance(row, int) and row in (0, NODES_Y + 1)
            for m in range(3):
                rim = copy_rx[parity, m, row]
                if outside:
                    ar2 = jnp.where(sub <= NODES_X + 1, rim, 0.0)
                else:
                    ar2 = jnp.where(halo_planes, rim, v1[m, row])
                ar2 = keep * ar2
                part = None if outside else v2[m, row]
                v2[m, row] = keep * assembled(part, lambda kind: sum_rx[sum_parity, kind, m, row], row)
                v1[m, row] = ar2
                q0[m, row] = (q1[m, row] - be0 * q0[m, row] - ar2) * ia1

        all_rows(image_row)
        rest = gathered.at[parity, 0 : peers - 1]
        pltpu.make_async_copy(rest, rest, all_recv.at[parity]).wait()
        totals = [jnp.sum(gathered[parity, at : at + 16], axis=0) for at in range(0, peers, 16)]
        while len(totals) > 1:
            totals = [a + b for a, b in zip(totals[0::2], totals[1::2])]
        totals = totals[0]
        rr2, m1, m2, m3 = [
            jnp.sum(jnp.where(lane == at, totals, 0.0), axis=1, keepdims=True) for at in range(4)
        ]
        be1 = jnp.where(step == 0, 0.0, rr2 / rr_before)
        r_q1 = -rr2 * ia1
        ar_q1 = (r_q1 - m1) * ia1
        q1_q1 = (rr_before + rr2) * ia1 * ia1
        ar_q0 = rr2 * ia1 * ia0
        q1_q0 = -rr_before * ia1 * ia0
        q1_aar = ia1 * (ar_q1 - be0 * ar_q0 - m2)
        q1_aq1 = ia1 * (q1_q1 - be0 * q1_q0 - ar_q1)
        q2_q2 = m2 + 2.0 * be1 * ar_q1 + be1 * be1 * q1_q1
        ar_q2 = m2 + be1 * ar_q1
        q2_aq2 = m3 + 2.0 * be1 * q1_aar + be1 * be1 * q1_aq1
        a2 = rr2 / (m1 + be1 * r_q1)
        rr3 = a2 * a2 * q2_q2 - rr2
        be2 = rr3 / rr2
        a3 = rr3 / (m1 - 2.0 * a2 * ar_q2 + a2 * a2 * q2_aq2 - be2 * rr3 / a2)

        def update_row(row, unused):
            for m in range(3):
                ar2, old = v1[m, row], q1[m, row]
                q2 = ar2 + be1 * old
                r3 = v0[m, row] - a2 * q2
                q3 = ar2 - a2 * (v2[m, row] + be1 * q0[m, row]) + be2 * q2
                d2 = v0[m, row] + be1 * d1[m, row]
                d3 = r3 + be2 * d2
                x[m, row] = x[m, row] + (a2 * d2 + a3 * d3)
                v0[m, row] = r3 - a3 * q3
                q1[m, row] = q3
                q0[m, row] = q2
                d1[m, row] = d3
            return unused

        by_rows(0, ROWS - 1, 6, update_row, 0)
        update_row(ROWS - 1, 0)
        pltpu.make_async_copy(rest, rest, all_send.at[parity]).wait()
        return be2, 1.0 / a3, 1.0 / a2, rr3

    none = jnp.zeros((1, 1), F32)
    lax.fori_loop(0, OUTER, outer, (none, none, none, none + 1.0))

    stores = [
        pltpu.make_async_copy(
            source.at[m, 1:18, i + 1 : i + 2], target.at[i, :, m : m + 1], out_sem.at[at, m, i]
        )
        for at, (source, target) in enumerate(((x, increment_hbm), (v0, residual_hbm)))
        for i in range(NODES_X)
        for m in range(3)
    ]
    for copy in stores:
        copy.start()
    for copy in stores:
        copy.wait()


def place_kernel(increment_in, residual_in, increment_out, residual_out, sem):
    copies = [
        pltpu.make_async_copy(increment_in, increment_out, sem.at[0]),
        pltpu.make_async_copy(residual_in, residual_out, sem.at[1]),
    ]
    for copy in copies:
        copy.start()
    for copy in copies:
        copy.wait()


def solution(mesh):
    size_x, size_y = mesh.shape["gx"], mesh.shape["gy"]
    peers = size_x * size_y
    field = jax.ShapeDtypeStruct((NODES_X, NODES_Y, 3, NZ), F32)

    def vmem(*shape, dtype=F32):
        return pltpu.VMEM(shape, dtype)

    def node(*lead):
        return vmem(*lead, ROWS, SUB, NZ)

    dma = pltpu.SemaphoreType.DMA
    scratch = [
        vmem(1, SLOTS, dtype=jnp.int32), vmem(1, 1, dtype=jnp.int32), vmem(6, HID), vmem(42, HID),
        node(3), node(3), node(), node(), node(3), vmem(BY, SUB, NZ), vmem(HIDDEN_LAYERS, HID, HID),
        vmem(6, BY, SUB, NZ), vmem(12 * COLUMNS, NZ), vmem(NZ, SLOTS, dtype=BF16), vmem(SLOTS, NZ, dtype=BF16),
        vmem(COLUMNS, SLOTS, dtype=BF16), vmem(SLOTS, 128, dtype=BF16),
        vmem(128, SLOTS), vmem(32, SLOTS), vmem(2 * GROUP * COLUMNS, SLOTS, dtype=BF16),
        vmem(GROUP, BY, SUB, NZ),
        vmem(N_PAIRS, BY + 2, SUB, NZ),
        node(3), node(3), node(3), node(3), node(3), node(3), node(3),
        node(2, 3, 3), node(2, 3), vmem(2, peers, 1, 128),
        dma((10, 5)), dma((2, 3, 5)), dma((8,)), dma((8,)), dma((3, 8)), dma((3, 8)),
        dma((2, 8)), dma((2, 8)), dma((2, 8)), dma((2, 8)), dma((2,)), dma((2,)),
    ]

    def body(u_now, load, mass, modulus, plastic_ids, plastic_count, w_in, w_hidden, w_head):
        hbm = pl.BlockSpec(memory_space=pl.ANY)
        increment, residual = pl.pallas_call(
            lambda *refs: kernel(size_x, size_y, *refs),
            out_shape=(field, field),
            in_specs=[hbm] * 9,
            out_specs=(hbm, hbm),
            scratch_shapes=scratch,
            compiler_params=pltpu.CompilerParams(
                collective_id=0, has_side_effects=True, vmem_limit_bytes=60 * 2**20
            ),
        )(
            u_now.transpose(1, 2, 0, 3), load.transpose(1, 2, 0, 3), mass, modulus,
            plastic_ids.reshape(1, SLOTS), plastic_count, w_in, w_hidden, w_head.T,
        )
        increment, residual = pl.pallas_call(
            place_kernel,
            out_shape=(field, field),
            in_specs=[pl.BlockSpec(memory_space=pltpu.VMEM)] * 2,
            out_specs=(hbm, hbm),
            scratch_shapes=[dma((2,))],
        )(increment, residual)
        return increment.transpose(2, 0, 1, 3), residual.transpose(2, 0, 1, 3)

    split_field = P(None, "gx", "gy", None)
    split_block = P("gx", "gy", None)
    return jax.shard_map(
        body,
        mesh=mesh,
        in_specs=(
            split_field, split_field, split_block, split_block, split_block, P("gx", "gy"), P(), P(), P(),
        ),
        out_specs=(split_field, split_field),
        check_vma=False,
    )
```

```python
import jax
import jax.numpy as jnp
from jax import lax
from jax.experimental import pallas as pl
from jax.experimental.pallas import tpu as pltpu
from jax.sharding import PartitionSpec as P

MESH = pl.DeviceIdType.MESH
F32, BF16, F8 = jnp.float32, jnp.bfloat16, jnp.float8_e4m3fn
HIGH_SCALE, LOW_SCALE = 16.0, 16.0 * 512.0
LAME_FIRST = 0.3 / (1.3 * 0.4)
LAME_SECOND = 1.0 / 2.6

BX, BY, NZ = 4, 16, 256
NODES_X, NODES_Y = BX + 1, BY + 1
ROWS = BY + 3
SUB = 8
SLOTS, HID, HIDDEN_LAYERS = 1024, 512, 3
COLUMNS = BY * BX
OUTER = 3
GROUP = 7
RINGS = 4

PAIRS = [(a, b) for a in range(6) for b in range(a, 6)]
PAIR_OF = {}
for _at, (_a, _b) in enumerate(PAIRS):
    PAIR_OF[_a, _b] = PAIR_OF[_b, _a] = _at
N_PAIRS = len(PAIRS)
N_SCATTER = 28
LIVE, FIRST_PAIR = 6, 7

DIRECTIONS = [(dx, dy) for dx in (-1, 1) for dy in (-1, 1)] + [(0, -1), (0, 1), (-1, 0), (1, 0)]
FACES = 2


def iso(a, b):
    if a < 3 and b < 3:
        return LAME_FIRST + (2.0 * LAME_SECOND if a == b else 0.0)
    return LAME_SECOND if a == b else 0.0


def z_next(values):
    edge = lax.broadcasted_iota(jnp.int32, (values.shape[0], 128), 1) == 127
    low, high = [pltpu.roll(values[:, at : at + 128], 127, 1) for at in (0, 128)]
    return jnp.concatenate([jnp.where(edge, high, low), jnp.where(edge, 0.0, high)], axis=1)


def z_prev(values):
    edge = lax.broadcasted_iota(jnp.int32, (values.shape[0], 128), 1) == 0
    low, high = [pltpu.roll(values[:, at : at + 128], 1, 1) for at in (0, 128)]
    return jnp.concatenate([jnp.where(edge, 0.0, low), jnp.where(edge, low, high)], axis=1)


def x_pairs(values):
    upper = pltpu.roll(values, SUB - 1, 0)
    return upper + values, upper - values


def strain_row(low, high):
    a = [low[m][1] + high[m][1] for m in range(3)]
    b = [high[m][0] - low[m][0] for m in range(3)]
    c = [high[m][0] + low[m][0] for m in range(3)]
    yz, xz, xy = c[1] + b[2], c[0] + a[2], b[0] + a[1]
    return [
        z_next(a[0]) + a[0],
        z_next(b[1]) + b[1],
        z_next(c[2]) - c[2],
        z_next(yz) + (b[2] - c[1]),
        z_next(xz) + (a[2] - c[0]),
        z_next(xy) + xy,
    ]


def force_parts(stress):
    before = [z_prev(s) for s in stress]
    total = {n: stress[n] + before[n] for n in (0, 1, 3, 4, 5)}
    differ = {n: before[n] - stress[n] for n in (2, 3, 4)}
    parts = []
    for along_x, along_y, along_z in ((0, 5, 4), (5, 1, 3), (4, 3, 2)):
        parts.append(
            (
                total[along_x],
                differ[along_z] - total[along_y],
                differ[along_z] + total[along_y],
            )
        )
    return parts


def force_of(along_x, other):
    return pltpu.roll(along_x + other, 1, 0) + (other - along_x)


def split(values):
    high = values.astype(BF16)
    return high, (values - high.astype(F32)).astype(BF16)


def mm(a, b):
    return jnp.dot(a, b, preferred_element_type=F32)


def face(dx, dy, depth):
    if depth == 2:
        sx = {-1: slice(1, 3), 0: slice(1, 6), 1: slice(4, 6)}[dx]
        tx = {-1: slice(5, 7), 0: slice(1, 6), 1: slice(0, 2)}[dx]
        sy = {-1: slice(1, 3), 0: slice(1, 18), 1: slice(16, 18)}[dy]
        ty = {-1: slice(17, 19), 0: slice(1, 18), 1: slice(0, 2)}[dy]
    else:
        sx = {-1: slice(2, 3), 0: slice(1, 6), 1: slice(4, 5)}[dx]
        tx = {-1: slice(6, 7), 0: slice(1, 6), 1: slice(0, 1)}[dx]
        sy = {-1: slice(2, 3), 0: slice(1, 18), 1: slice(16, 17)}[dy]
        ty = {-1: slice(18, 19), 0: slice(1, 18), 1: slice(0, 1)}[dy]
    return sy, sx, ty, tx


def element_face(dx, dy):
    sx = {-1: slice(1, 2), 0: slice(1, 5), 1: slice(4, 5)}[dx]
    tx = {-1: slice(5, 6), 0: slice(1, 5), 1: slice(0, 1)}[dx]
    sy = {-1: slice(1, 2), 0: slice(1, 17), 1: slice(16, 17)}[dy]
    ty = {-1: slice(17, 18), 0: slice(1, 17), 1: slice(0, 1)}[dy]
    return sy, sx, ty, tx


def all_offsets(size_x, size_y):
    offsets = [
        (z, core, x, y)
        for z in range(size_x // 2)
        for core in range(2)
        for x in range(size_y // RINGS)
        for y in range(RINGS)
    ][1:]

    def hops(offset):
        z, core, x, y = offset
        return sum(min(d, RINGS - d) for d in (z, x, y)) * 2 + core

    return sorted(offsets, key=hops, reverse=True)


def by_rows(first, last, width, body, carry):
    assert (last - first) % width == 0

    def block(at, carry):
        for n in range(width):
            carry = body(first + at * width + n, carry)
        return carry

    return lax.fori_loop(0, (last - first) // width, block, carry)


def kernel(
    size_x, size_y,
    u_hbm, load_hbm, mass_hbm, modulus_hbm, ids_hbm, count_hbm, w_in_hbm, w_hidden_hbm, w_head_hbm,
    increment_hbm, residual_hbm,
    ids_ref, count_ref, w_in_ref, w_head_ref, ux, lx, mass_part, mass_full, mass_rx, modulus, weights,
    strain_now, packed, onehot_k, onehot_kt, onehot_r, inputs_t, out_t, values, lhs, scattered,
    tangent,
    v0, v1, v2, q1, q0, d1, x, sum_rx, copy_rx, gathered,
    load_sem, out_sem, mass_send, mass_recv, tan_send, tan_recv,
    sum_send, sum_recv, copy_send, copy_recv, all_send, all_recv,
):
    index_x, index_y = lax.axis_index("gx"), lax.axis_index("gy")
    me = index_x * size_y + index_y
    peers = size_x * size_y
    neighbours = [
        (lax.rem(index_x + dx + size_x, size_x), lax.rem(index_y + dy + size_y, size_y))
        for dx, dy in DIRECTIONS
    ]

    ring_x, ring_y = index_y // RINGS, lax.rem(index_y, RINGS)
    ring_z, core = index_x // 2, lax.rem(index_x, 2)
    at_z = [lax.rem(ring_z + d, RINGS) * 2 for d in range(size_x // 2)]
    at_core = [core, 1 - core]
    at_ring_x = [lax.rem(ring_x + d, RINGS) * RINGS for d in range(size_y // RINGS)]
    at_ring_y = [lax.rem(ring_y + d, RINGS) for d in range(RINGS)]
    along_gx = [[z + c for c in at_core] for z in at_z]
    along_gy = [[a + b for b in at_ring_y] for a in at_ring_x]
    others = [
        (along_gx[z][c], along_gy[a][b]) for z, c, a, b in all_offsets(size_x, size_y)
    ]

    for ref in (mass_part, modulus):
        ref[...] = jnp.zeros_like(ref)
    small = ((ids_hbm, ids_ref), (count_hbm, count_ref), (w_in_hbm, w_in_ref), (w_head_hbm, w_head_ref))
    small_loads = [
        pltpu.make_async_copy(source, target, load_sem.at[9, at])
        for at, (source, target) in enumerate(small)
    ]
    u_loads, modulus_loads, mass_loads, load_loads, weight_loads = [], [], [], [], []
    for i in range(NODES_X):
        for m in range(3):
            u_loads.append(pltpu.make_async_copy(u_hbm.at[i, :, m : m + 1], ux.at[m, 1:18, i + 1 : i + 2], load_sem.at[m, i]))
    for layer in range(HIDDEN_LAYERS):
        weight_loads.append(pltpu.make_async_copy(w_hidden_hbm.at[layer], weights.at[layer], load_sem.at[8, layer]))
    for i in range(BX):
        modulus_loads.append(pltpu.make_async_copy(modulus_hbm.at[i], modulus.at[:, i + 1], load_sem.at[6, i]))
    for i in range(NODES_X):
        mass_loads.append(pltpu.make_async_copy(mass_hbm.at[i], mass_part.at[1:18, i + 1], load_sem.at[7, i]))
        for m in range(3):
            load_loads.append(pltpu.make_async_copy(load_hbm.at[i, :, m : m + 1], lx.at[m, 1:18, i + 1 : i + 2], load_sem.at[3 + m, i]))
    loads = small_loads + u_loads + weight_loads + modulus_loads + mass_loads + load_loads
    for copy in loads:
        copy.start()

    barrier = pltpu.get_barrier_semaphore()
    for device in others:
        pl.semaphore_signal(barrier, inc=1, device_id=device, device_id_type=MESH)
    for copy in small_loads:
        copy.wait()

    ids = ids_ref[...]
    slot = lax.broadcasted_iota(jnp.int32, (1, SLOTS), 1)
    live = jnp.where(slot < count_ref[...], 1.0, 0.0)
    at_k = ids & (NZ - 1)
    at_j = (ids >> 8) & (BY - 1)
    at_i = ids >> 12
    onehot_k[...] = jnp.where(
        lax.broadcasted_iota(jnp.int32, (NZ, SLOTS), 0) == at_k, 1.0, 0.0
    ).astype(BF16)
    onehot_r[...] = jnp.where(
        lax.broadcasted_iota(jnp.int32, (COLUMNS, SLOTS), 0) == at_j * BX + at_i, live, 0.0
    ).astype(BF16)
    k_column = jnp.broadcast_to(at_k.astype(F32), (128, SLOTS)).T
    lane_k = lax.broadcasted_iota(jnp.int32, (SLOTS, 128), 1).astype(F32)
    onehot_kt[:, 0:128] = jnp.where(k_column == lane_k, 1.0, 0.0).astype(BF16)
    onehot_kt[:, 128:256] = jnp.where(k_column == lane_k + 128.0, 1.0, 0.0).astype(BF16)

    sub = lax.broadcasted_iota(jnp.int32, (SUB, NZ), 0)
    own_elements = (sub >= 1) & (sub <= BX)
    for copy in u_loads:
        copy.wait()

    def pairs_of(ref, row):
        return [x_pairs(ref[m, row]) for m in range(3)]

    def strain_step(row, low):
        high = pairs_of(ux, row + 1)
        for n, value in enumerate(strain_row(low, high)):
            strain_now[n, row - 1] = jnp.where(own_elements, 0.25 * value, 0.0)
        return high

    by_rows(1, 1 + BY, 8, strain_step, pairs_of(ux, 1))

    picked = []
    for n in range(6):
        for g in range(BY // 2):
            pair = jnp.where(
                sub < BX,
                pltpu.roll(strain_now[n, 2 * g], SUB - 1, 0),
                pltpu.roll(strain_now[n, 2 * g + 1], BX - 1, 0),
            )
            high = pair.astype(BF16).astype(F32)
            packed[n * COLUMNS + g * SUB : n * COLUMNS + (g + 1) * SUB] = high
            packed[(6 + n) * COLUMNS + g * SUB : (6 + n) * COLUMNS + (g + 1) * SUB] = pair - high
    at_slots = mm(packed[...].astype(BF16), onehot_k[...])
    for n in range(6):
        rows = at_slots[n * COLUMNS : (n + 1) * COLUMNS] + at_slots[(6 + n) * COLUMNS : (7 + n) * COLUMNS]
        picked.append(jnp.sum(rows * onehot_r[...].astype(F32), axis=0, keepdims=True))
    eps = jnp.concatenate(picked + [jnp.zeros((2, SLOTS), F32)], axis=0)
    eps_high = eps.astype(BF16).astype(F32)
    stacked = jnp.concatenate(
        [eps_high, eps - eps_high, eps_high, jnp.zeros((104, SLOTS), F32)], axis=0
    )
    inputs_t[...] = stacked.T.astype(BF16)

    w_in = jnp.concatenate([w_in_ref[...], jnp.zeros((2, HID), F32)], axis=0)
    w_in_high = w_in.astype(BF16).astype(F32)
    w_first = jnp.concatenate(
        [w_in_high, w_in_high, w_in - w_in_high, jnp.zeros((104, HID), F32)], axis=0
    ).astype(BF16)
    to_row = lax.broadcasted_iota(jnp.int32, (128, 42), 0)
    from_out = lax.broadcasted_iota(jnp.int32, (128, 42), 1)
    place = jnp.where(
        (from_out == (to_row // 8) * 6 + to_row % 8) & (to_row % 8 < 6) & (to_row < 56), 1.0, 0.0
    ).astype(BF16)
    head_high, head_low = split(w_head_ref[...])
    head = (mm(place, head_high) + mm(place, head_low)).T
    def product(hidden, parts):
        high, mixed_weight = parts
        hidden_high = hidden.astype(BF16)
        low = hidden - hidden_high.astype(F32)
        mixed = jnp.concatenate([(low * LOW_SCALE).astype(F8), (hidden * HIGH_SCALE).astype(F8)], axis=1)
        return mm(hidden_high, high) + mm(mixed, mixed_weight) * (1.0 / (HIGH_SCALE * LOW_SCALE))

    def narrow(weight):
        high = weight.astype(BF16)
        low = weight - high.astype(F32)
        return high, jnp.concatenate(
            [(weight * HIGH_SCALE).astype(F8), (low * LOW_SCALE).astype(F8)], axis=0
        )

    halves = []
    for layer in range(HIDDEN_LAYERS):
        weight_loads[layer].wait()
        halves.append(narrow(weights[layer]))

    half = SLOTS // 2
    left, right = mm(inputs_t[0:half], w_first), mm(inputs_t[half:SLOTS], w_first)
    for parts in halves + [narrow(head)]:
        left = product(jnp.tanh(left), parts)
        right = product(jnp.tanh(right), parts)
    out_t[:, 0:half] = left.T
    out_t[:, half:SLOTS] = right.T

    for copy in mass_loads:
        copy.wait()
    pl.semaphore_wait(barrier, peers - 1)
    mass_copies = []
    for q, ((dx, dy), device) in enumerate(zip(DIRECTIONS, neighbours)):
        sy, sx, ty, tx = face(dx, dy, 2)
        kind = 0 if dy == 0 else (1 if dx == 0 else 2)
        copy = pltpu.make_async_remote_copy(
            mass_part.at[sy, sx], mass_rx.at[kind, ty, tx], mass_send.at[q], mass_recv.at[q],
            device_id=device, device_id_type=MESH,
        )
        copy.start()
        mass_copies.append(copy)

    values[0:6] = out_t[0:6]
    values[LIVE : LIVE + 1] = jnp.ones((1, SLOTS), F32)
    factor = [out_t[8 * (a + 1) : 8 * (a + 2)] for a in range(6)]
    for at, (a, b) in enumerate(PAIRS):
        values[FIRST_PAIR + at : FIRST_PAIR + at + 1] = jnp.sum(
            factor[a] * factor[b], axis=0, keepdims=True
        ) * (1.0 / 6.0)

    def spread_ready(at):
        for n in range(GROUP):
            high, low = split(values[at * GROUP + n : at * GROUP + n + 1])
            rows = onehot_r[...]
            lhs[at, n * COLUMNS : (n + 1) * COLUMNS] = rows * high
            lhs[at, (GROUP + n) * COLUMNS : (GROUP + n + 1) * COLUMNS] = rows * low

    def spread_group(at):
        if at < N_SCATTER // GROUP - 1:
            spread_ready(at + 1)
        spread = mm(lhs[at], onehot_kt[...])
        return spread[: GROUP * COLUMNS] + spread[GROUP * COLUMNS :]

    def element_rows(spread, n, g):
        start = n * COLUMNS + g * SUB
        both = spread[start : start + SUB]
        return pltpu.roll(both, 1, 0), pltpu.roll(both, 5, 0)

    def sum_copies(parity):
        copies = []
        for q, ((dx, dy), device) in enumerate(zip(DIRECTIONS, neighbours)):
            sy, sx, ty, tx = face(dx, dy, 2)
            kind = 0 if dy == 0 else (1 if dx == 0 else 2)
            copies.append(
                pltpu.make_async_remote_copy(
                    v2.at[:, sy, sx], sum_rx.at[parity, kind, :, ty, tx],
                    sum_send.at[parity, q], sum_recv.at[parity, q],
                    device_id=device, device_id_type=MESH,
                )
            )
        return copies

    def exact_copies(parity):
        copies = []
        for q, ((dx, dy), device) in enumerate(zip(DIRECTIONS, neighbours)):
            sy, sx, ty, tx = face(dx, dy, 1)
            copies.append(
                pltpu.make_async_remote_copy(
                    v1.at[:, sy, sx], copy_rx.at[parity, :, ty, tx],
                    copy_send.at[parity, q], copy_recv.at[parity, q],
                    device_id=device, device_id_type=MESH,
                )
            )
        return copies

    global_x = index_x * BX + sub - 1
    keep_x = jnp.where(
        (global_x >= 0) & (global_x < size_x * BX) & (sub < SUB - 1), 1.0, 0.0
    )
    own_planes = (sub >= 1) & (sub <= NODES_X)
    rim_planes = ((sub <= 1) & (index_x > 0)) | ((sub >= NODES_X) & (sub <= NODES_X + 1))
    halo_planes = (sub == 0) | (sub == NODES_X + 1)
    flank_low, corner_low = own_planes & (index_y > 0), rim_planes & (index_y > 0)
    valid_elements = (sub <= BX + 1) & ((sub >= 1) | (index_x > 0))

    def keep_of(row):
        global_y = index_y * BY + row - 1
        inside = jnp.where((global_y >= 0) & (global_y < size_y * BY), 1.0, 0.0)
        return keep_x * inside

    def assembled(part, received, row):
        at_rim = isinstance(row, int)
        total = jnp.zeros((SUB, NZ), F32)
        if not at_rim or 1 <= row <= NODES_Y:
            total = part + jnp.where(rim_planes, received(0), 0.0)
        if at_rim:
            flank, corner = (flank_low, corner_low) if row <= 1 else (own_planes, rim_planes)
            total = total + jnp.where(flank, received(1), 0.0) + jnp.where(corner, received(2), 0.0)
        return total

    def all_rows(body):
        for row in (0, 1, NODES_Y, NODES_Y + 1):
            body(row)

        def inner(row, carry):
            body(row)
            return carry

        by_rows(2, NODES_Y, 5, inner, 0)

    def stress_now(row):
        scale = 0.25 * modulus[row]
        base = scale * (1.0 - 0.75 * scattered[LIVE, row])
        eps_row = [strain_now[n, row] for n in range(6)]
        trace = LAME_FIRST * (eps_row[0] + eps_row[1] + eps_row[2])
        elastic = [trace + 2.0 * LAME_SECOND * eps_row[n] for n in range(3)]
        elastic += [LAME_SECOND * eps_row[n] for n in range(3, 6)]
        return [base * elastic[n] + scale * scattered[n, row] for n in range(6)]

    zero = jnp.zeros((SUB, NZ), F32)
    no_parts = [(zero, zero)] * 3

    def residual_step(row, before):
        parts = force_parts(stress_now(row - 1))
        for m in range(3):
            force = force_of(parts[m][0] + before[m][0], parts[m][1] + before[m][1])
            v2[m, row] = jnp.where(own_planes, lx[m, row] - force, 0.0)
        return [(parts[m][0], parts[m][2]) for m in range(3)]

    spread_ready(0)
    spread = spread_group(0)
    for n in range(GROUP):
        for g in range(BY // 2):
            for odd, entry in enumerate(element_rows(spread, n, g)):
                scattered[n, 2 * g + odd] = jnp.where(own_elements, entry, 0.0)
    for copy in modulus_loads + load_loads:
        copy.wait()
    last = by_rows(1, 1 + BY, 8, residual_step, no_parts)
    for m in range(3):
        v2[m, NODES_Y] = jnp.where(own_planes, lx[m, NODES_Y] - force_of(*last[m]), 0.0)

    first_copies = sum_copies(0)
    for copy in first_copies:
        copy.start()

    tangent_copies = []
    planes = slice(1, 1 + BX)
    for group in range(N_PAIRS // GROUP):
        spread = spread_group(group + 1)
        for g in range(BY // 2):
            scales = [modulus[2 * g + odd] * (1.0 / 16.0) for odd in range(2)]
            bases = [scales[odd] * (1.0 - 0.75 * scattered[LIVE, 2 * g + odd]) for odd in range(2)]
            for n in range(GROUP):
                at = group * GROUP + n
                for odd, entry in enumerate(element_rows(spread, n, g)):
                    entry = scales[odd] * entry
                    if iso(*PAIRS[at]):
                        entry = entry + bases[odd] * iso(*PAIRS[at])
                    tangent[at, 2 * g + odd + 1, planes] = entry[planes]
        entries = pl.ds(group * GROUP, GROUP)
        for q, ((dx, dy), device) in enumerate(zip(DIRECTIONS, neighbours)):
            sy, sx, ty, tx = element_face(dx, dy)
            copy = pltpu.make_async_remote_copy(
                tangent.at[entries, sy, sx], tangent.at[entries, ty, tx],
                tan_send.at[group, q], tan_recv.at[group, q],
                device_id=device, device_id_type=MESH,
            )
            copy.start()
            tangent_copies.append(copy)

    for ref in (q1, q0, d1, x):
        ref[...] = jnp.zeros_like(ref)
    for copy in mass_copies:
        copy.wait()

    def mass_row(row):
        mass_full[row] = assembled(mass_part[row], lambda kind: mass_rx[kind, row], row)

    all_rows(mass_row)
    for copy in first_copies:
        copy.wait()

    def start_row(row):
        keep = keep_of(row)
        for m in range(3):
            part = None if isinstance(row, int) and row in (0, NODES_Y + 1) else v2[m, row]
            v0[m, row] = keep * assembled(part, lambda kind: sum_rx[0, kind, m, row], row)

    all_rows(start_row)
    for copy in tangent_copies:
        copy.wait()

    def stress_row(row, strain, present):
        entries = [tangent[at, row] for at in range(N_PAIRS)]
        result = []
        for a in range(6):
            total = entries[PAIR_OF[a, 0]] * strain[0]
            for b in range(1, 6):
                total = total + entries[PAIR_OF[a, b]] * strain[b]
            result.append(jnp.where(present, total, 0.0))
        return result

    def first_image(row, carry):
        low, before = carry
        high = pairs_of(v0, row + 1)
        present = valid_elements & (row + index_y > 0)
        parts = force_parts(stress_row(row, strain_row(low, high), present))
        keep = keep_of(row)
        for m in range(3):
            force = force_of(parts[m][0] + before[m][0], parts[m][1] + before[m][1])
            v1[m, row] = keep * (force + mass_full[row] * v0[m, row])
        return high, [(parts[m][0], parts[m][2]) for m in range(3)]

    def second_image(row, carry):
        low, before, sums = carry
        high = pairs_of(v1, row + 1)
        parts = force_parts(stress_row(row, strain_row(low, high), own_elements))
        rr, r_ar, ar_ar, ar_aar = sums
        for m in range(3):
            here, image = v0[m, row], v1[m, row]
            force = force_of(parts[m][0] + before[m][0], parts[m][1] + before[m][1])
            force = force + mass_part[row] * image
            v2[m, row] = force
            rr = rr + here * here
            r_ar = r_ar + here * image
            ar_ar = ar_ar + image * image
            ar_aar = ar_aar + image * force
        return high, [(parts[m][0], parts[m][2]) for m in range(3)], (rr, r_ar, ar_ar, ar_aar)

    lane = lax.broadcasted_iota(jnp.int32, (1, 128), 1)

    def outer(step, carry):
        be0, ia1, ia0, rr_before = carry
        parity = lax.rem(step, 2)
        sum_parity = lax.rem(step + 1, 2)
        by_rows(0, BY + 2, 6, first_image, (pairs_of(v0, 0), no_parts))
        exact = exact_copies(parity)
        for copy in exact:
            copy.start()
        _, before, sums = by_rows(
            1, 1 + BY, 8, second_image, (pairs_of(v1, 1), no_parts, (zero,) * 4)
        )
        ar_aar = sums[3]
        for m in range(3):
            image = v1[m, NODES_Y]
            force = force_of(*before[m]) + mass_part[NODES_Y] * image
            v2[m, NODES_Y] = force
            ar_aar = ar_aar + jnp.where(own_planes, image * force, 0.0)
        summed = sum_copies(sum_parity)
        for copy in summed[:-FACES]:
            copy.start()

        message = jnp.zeros((1, 128), F32)
        for at, (value, mask) in enumerate(
            ((sums[0], own_elements), (sums[1], own_elements), (sums[2], own_elements), (ar_aar, own_planes))
        ):
            total = jnp.sum(jnp.where(mask, value, 0.0), axis=0, keepdims=True)
            total = jnp.sum(total, axis=1, keepdims=True)
            message = message + jnp.where(lane == at, total, 0.0)
        gathered[parity, me] = message

        for device in others:
            pltpu.make_async_remote_copy(
                gathered.at[parity, me], gathered.at[parity, me],
                all_send.at[parity], all_recv.at[parity],
                device_id=device, device_id_type=MESH,
            ).start()
        for copy in summed[-FACES:]:
            copy.start()
        for copy in exact + summed:
            copy.wait()

        def image_row(row):
            keep = keep_of(row)
            outside = isinstance(row, int) and row in (0, NODES_Y + 1)
            for m in range(3):
                rim = copy_rx[parity, m, row]
                if outside:
                    ar2 = jnp.where(sub <= NODES_X + 1, rim, 0.0)
                else:
                    ar2 = jnp.where(halo_planes, rim, v1[m, row])
                ar2 = keep * ar2
                part = None if outside else v2[m, row]
                v2[m, row] = keep * assembled(part, lambda kind: sum_rx[sum_parity, kind, m, row], row)
                v1[m, row] = ar2
                q0[m, row] = (q1[m, row] - be0 * q0[m, row] - ar2) * ia1

        all_rows(image_row)
        rest = gathered.at[parity, 0 : peers - 1]
        pltpu.make_async_copy(rest, rest, all_recv.at[parity]).wait()
        totals = [jnp.sum(gathered[parity, at : at + 16], axis=0) for at in range(0, peers, 16)]
        while len(totals) > 1:
            totals = [a + b for a, b in zip(totals[0::2], totals[1::2])]
        totals = totals[0]
        rr2, m1, m2, m3 = [
            jnp.sum(jnp.where(lane == at, totals, 0.0), axis=1, keepdims=True) for at in range(4)
        ]
        be1 = jnp.where(step == 0, 0.0, rr2 / rr_before)
        r_q1 = -rr2 * ia1
        ar_q1 = (r_q1 - m1) * ia1
        q1_q1 = (rr_before + rr2) * ia1 * ia1
        ar_q0 = rr2 * ia1 * ia0
        q1_q0 = -rr_before * ia1 * ia0
        q1_aar = ia1 * (ar_q1 - be0 * ar_q0 - m2)
        q1_aq1 = ia1 * (q1_q1 - be0 * q1_q0 - ar_q1)
        q2_q2 = m2 + 2.0 * be1 * ar_q1 + be1 * be1 * q1_q1
        ar_q2 = m2 + be1 * ar_q1
        q2_aq2 = m3 + 2.0 * be1 * q1_aar + be1 * be1 * q1_aq1
        a2 = rr2 / (m1 + be1 * r_q1)
        rr3 = a2 * a2 * q2_q2 - rr2
        be2 = rr3 / rr2
        a3 = rr3 / (m1 - 2.0 * a2 * ar_q2 + a2 * a2 * q2_aq2 - be2 * rr3 / a2)

        def update_row(row, unused):
            for m in range(3):
                ar2, old = v1[m, row], q1[m, row]
                q2 = ar2 + be1 * old
                r3 = v0[m, row] - a2 * q2
                q3 = ar2 - a2 * (v2[m, row] + be1 * q0[m, row]) + be2 * q2
                d2 = v0[m, row] + be1 * d1[m, row]
                d3 = r3 + be2 * d2
                x[m, row] = x[m, row] + (a2 * d2 + a3 * d3)
                v0[m, row] = r3 - a3 * q3
                q1[m, row] = q3
                q0[m, row] = q2
                d1[m, row] = d3
            return unused

        by_rows(0, ROWS - 1, 6, update_row, 0)
        update_row(ROWS - 1, 0)
        pltpu.make_async_copy(rest, rest, all_send.at[parity]).wait()
        return be2, 1.0 / a3, 1.0 / a2, rr3

    none = jnp.zeros((1, 1), F32)
    lax.fori_loop(0, OUTER, outer, (none, none, none, none + 1.0))

    stores = [
        pltpu.make_async_copy(
            source.at[m, 1:18, i + 1 : i + 2], target.at[i, :, m : m + 1], out_sem.at[at, m, i]
        )
        for at, (source, target) in enumerate(((x, increment_hbm), (v0, residual_hbm)))
        for i in range(NODES_X)
        for m in range(3)
    ]
    for copy in stores:
        copy.start()
    for copy in stores:
        copy.wait()


def place_kernel(increment_in, residual_in, increment_out, residual_out, sem):
    copies = [
        pltpu.make_async_copy(increment_in, increment_out, sem.at[0]),
        pltpu.make_async_copy(residual_in, residual_out, sem.at[1]),
    ]
    for copy in copies:
        copy.start()
    for copy in copies:
        copy.wait()


def solution(mesh):
    size_x, size_y = mesh.shape["gx"], mesh.shape["gy"]
    peers = size_x * size_y
    field = jax.ShapeDtypeStruct((NODES_X, NODES_Y, 3, NZ), F32)

    def vmem(*shape, dtype=F32):
        return pltpu.VMEM(shape, dtype)

    def node(*lead):
        return vmem(*lead, ROWS, SUB, NZ)

    dma = pltpu.SemaphoreType.DMA
    scratch = [
        vmem(1, SLOTS, dtype=jnp.int32), vmem(1, 1, dtype=jnp.int32), vmem(6, HID), vmem(42, HID),
        node(3), node(3), node(), node(), node(3), vmem(BY, SUB, NZ), vmem(HIDDEN_LAYERS, HID, HID),
        vmem(6, BY, SUB, NZ), vmem(12 * COLUMNS, NZ), vmem(NZ, SLOTS, dtype=BF16), vmem(SLOTS, NZ, dtype=BF16),
        vmem(COLUMNS, SLOTS, dtype=BF16), vmem(SLOTS, 128, dtype=BF16),
        vmem(128, SLOTS), vmem(32, SLOTS), vmem(N_SCATTER // GROUP, 2 * GROUP * COLUMNS, SLOTS, dtype=BF16),
        vmem(GROUP, BY, SUB, NZ),
        vmem(N_PAIRS, BY + 2, SUB, NZ),
        node(3), node(3), node(3), node(3), node(3), node(3), node(3),
        node(2, 3, 3), node(2, 3), vmem(2, peers, 1, 128),
        dma((10, 5)), dma((2, 3, 5)), dma((8,)), dma((8,)), dma((3, 8)), dma((3, 8)),
        dma((2, 8)), dma((2, 8)), dma((2, 8)), dma((2, 8)), dma((2,)), dma((2,)),
    ]

    def body(u_now, load, mass, modulus, plastic_ids, plastic_count, w_in, w_hidden, w_head):
        hbm = pl.BlockSpec(memory_space=pl.ANY)
        increment, residual = pl.pallas_call(
            lambda *refs: kernel(size_x, size_y, *refs),
            out_shape=(field, field),
            in_specs=[hbm] * 9,
            out_specs=(hbm, hbm),
            scratch_shapes=scratch,
            compiler_params=pltpu.CompilerParams(
                collective_id=0, has_side_effects=True, vmem_limit_bytes=60 * 2**20
            ),
        )(
            u_now.transpose(1, 2, 0, 3), load.transpose(1, 2, 0, 3), mass, modulus,
            plastic_ids.reshape(1, SLOTS), plastic_count, w_in, w_hidden, w_head.T,
        )
        increment, residual = pl.pallas_call(
            place_kernel,
            out_shape=(field, field),
            in_specs=[pl.BlockSpec(memory_space=pltpu.VMEM)] * 2,
            out_specs=(hbm, hbm),
            scratch_shapes=[dma((2,))],
        )(increment, residual)
        return increment.transpose(2, 0, 1, 3), residual.transpose(2, 0, 1, 3)

    split_field = P(None, "gx", "gy", None)
    split_block = P("gx", "gy", None)
    return jax.shard_map(
        body,
        mesh=mesh,
        in_specs=(
            split_field, split_field, split_block, split_block, split_block, P("gx", "gy"), P(), P(), P(),
        ),
        out_specs=(split_field, split_field),
        check_vma=False,
    )
```

```python
import jax
import jax.numpy as jnp
from jax import lax
from jax.experimental import pallas as pl
from jax.experimental.pallas import tpu as pltpu
from jax.sharding import PartitionSpec as P

MESH = pl.DeviceIdType.MESH
F32, BF16, F8 = jnp.float32, jnp.bfloat16, jnp.float8_e4m3fn
HIGH_SCALE, LOW_SCALE = 16.0, 16.0 * 512.0
LAME_FIRST = 0.3 / (1.3 * 0.4)
LAME_SECOND = 1.0 / 2.6

BX, BY, NZ = 4, 16, 256
NODES_X, NODES_Y = BX + 1, BY + 1
ROWS = BY + 3
SUB = 8
SLOTS, HID, HIDDEN_LAYERS = 1024, 512, 3
COLUMNS = BY * BX
OUTER = 3
GROUP = 7
RINGS = 4

PAIRS = [(a, b) for a in range(6) for b in range(a, 6)]
PAIR_OF = {}
for _at, (_a, _b) in enumerate(PAIRS):
    PAIR_OF[_a, _b] = PAIR_OF[_b, _a] = _at
N_PAIRS = len(PAIRS)
N_SCATTER = 28
LIVE, FIRST_PAIR = 6, 7

DIRECTIONS = [(dx, dy) for dx in (-1, 1) for dy in (-1, 1)] + [(0, -1), (0, 1), (-1, 0), (1, 0)]
FACES = 2


def iso(a, b):
    if a < 3 and b < 3:
        return LAME_FIRST + (2.0 * LAME_SECOND if a == b else 0.0)
    return LAME_SECOND if a == b else 0.0


def z_next(values):
    edge = lax.broadcasted_iota(jnp.int32, (values.shape[0], 128), 1) == 127
    low, high = [pltpu.roll(values[:, at : at + 128], 127, 1) for at in (0, 128)]
    return jnp.concatenate([jnp.where(edge, high, low), jnp.where(edge, 0.0, high)], axis=1)


def z_prev(values):
    edge = lax.broadcasted_iota(jnp.int32, (values.shape[0], 128), 1) == 0
    low, high = [pltpu.roll(values[:, at : at + 128], 1, 1) for at in (0, 128)]
    return jnp.concatenate([jnp.where(edge, 0.0, low), jnp.where(edge, low, high)], axis=1)


def x_pairs(values):
    upper = pltpu.roll(values, SUB - 1, 0)
    return upper + values, upper - values


def strain_row(low, high):
    a = [low[m][1] + high[m][1] for m in range(3)]
    b = [high[m][0] - low[m][0] for m in range(3)]
    c = [high[m][0] + low[m][0] for m in range(3)]
    yz, xz, xy = c[1] + b[2], c[0] + a[2], b[0] + a[1]
    return [
        z_next(a[0]) + a[0],
        z_next(b[1]) + b[1],
        z_next(c[2]) - c[2],
        z_next(yz) + (b[2] - c[1]),
        z_next(xz) + (a[2] - c[0]),
        z_next(xy) + xy,
    ]


def force_parts(stress):
    before = [z_prev(s) for s in stress]
    total = {n: stress[n] + before[n] for n in (0, 1, 3, 4, 5)}
    differ = {n: before[n] - stress[n] for n in (2, 3, 4)}
    parts = []
    for along_x, along_y, along_z in ((0, 5, 4), (5, 1, 3), (4, 3, 2)):
        parts.append(
            (
                total[along_x],
                differ[along_z] - total[along_y],
                differ[along_z] + total[along_y],
            )
        )
    return parts


def force_of(along_x, other):
    return pltpu.roll(along_x + other, 1, 0) + (other - along_x)


def split(values):
    high = values.astype(BF16)
    return high, (values - high.astype(F32)).astype(BF16)


def mm(a, b):
    return jnp.dot(a, b, preferred_element_type=F32)


def face(dx, dy, depth):
    if depth == 2:
        sx = {-1: slice(1, 3), 0: slice(1, 6), 1: slice(4, 6)}[dx]
        tx = {-1: slice(5, 7), 0: slice(1, 6), 1: slice(0, 2)}[dx]
        sy = {-1: slice(1, 3), 0: slice(1, 18), 1: slice(16, 18)}[dy]
        ty = {-1: slice(17, 19), 0: slice(1, 18), 1: slice(0, 2)}[dy]
    else:
        sx = {-1: slice(2, 3), 0: slice(1, 6), 1: slice(4, 5)}[dx]
        tx = {-1: slice(6, 7), 0: slice(1, 6), 1: slice(0, 1)}[dx]
        sy = {-1: slice(2, 3), 0: slice(1, 18), 1: slice(16, 17)}[dy]
        ty = {-1: slice(18, 19), 0: slice(1, 18), 1: slice(0, 1)}[dy]
    return sy, sx, ty, tx


def element_face(dx, dy):
    sx = {-1: slice(1, 2), 0: slice(1, 5), 1: slice(4, 5)}[dx]
    tx = {-1: slice(5, 6), 0: slice(1, 5), 1: slice(0, 1)}[dx]
    sy = {-1: slice(1, 2), 0: slice(1, 17), 1: slice(16, 17)}[dy]
    ty = {-1: slice(17, 18), 0: slice(1, 17), 1: slice(0, 1)}[dy]
    return sy, sx, ty, tx


def all_offsets(size_x, size_y):
    offsets = [
        (z, core, x, y)
        for z in range(size_x // 2)
        for core in range(2)
        for x in range(size_y // RINGS)
        for y in range(RINGS)
    ][1:]

    def hops(offset):
        z, core, x, y = offset
        return sum(min(d, RINGS - d) for d in (z, x, y)) * 2 + core

    return sorted(offsets, key=hops, reverse=True)


def by_rows(first, last, width, body, carry):
    assert (last - first) % width == 0

    def block(at, carry):
        for n in range(width):
            carry = body(first + at * width + n, carry)
        return carry

    return lax.fori_loop(0, (last - first) // width, block, carry)


def kernel(
    size_x, size_y,
    u_hbm, load_hbm, mass_hbm, modulus_hbm, ids_hbm, count_hbm, w_in_hbm, w_hidden_hbm, w_head_hbm,
    increment_hbm, residual_hbm,
    ids_ref, count_ref, w_in_ref, w_head_ref, ux, lx, mass_part, mass_full, mass_rx, modulus, weights,
    strain_now, packed, onehot_k, onehot_kt, onehot_r, inputs_t, out_t, values, lhs, scattered,
    tangent,
    v0, v1, v2, q1, q0, d1, x, sum_rx, copy_rx, gathered,
    load_sem, out_sem, mass_send, mass_recv, tan_send, tan_recv,
    sum_send, sum_recv, copy_send, copy_recv, all_send, all_recv,
):
    index_x, index_y = lax.axis_index("gx"), lax.axis_index("gy")
    me = index_x * size_y + index_y
    peers = size_x * size_y
    neighbours = [
        (lax.rem(index_x + dx + size_x, size_x), lax.rem(index_y + dy + size_y, size_y))
        for dx, dy in DIRECTIONS
    ]

    ring_x, ring_y = index_y // RINGS, lax.rem(index_y, RINGS)
    ring_z, core = index_x // 2, lax.rem(index_x, 2)
    at_z = [lax.rem(ring_z + d, RINGS) * 2 for d in range(size_x // 2)]
    at_core = [core, 1 - core]
    at_ring_x = [lax.rem(ring_x + d, RINGS) * RINGS for d in range(size_y // RINGS)]
    at_ring_y = [lax.rem(ring_y + d, RINGS) for d in range(RINGS)]
    along_gx = [[z + c for c in at_core] for z in at_z]
    along_gy = [[a + b for b in at_ring_y] for a in at_ring_x]
    others = [
        (along_gx[z][c], along_gy[a][b]) for z, c, a, b in all_offsets(size_x, size_y)
    ]

    for ref in (mass_part, modulus):
        ref[...] = jnp.zeros_like(ref)
    small = ((ids_hbm, ids_ref), (count_hbm, count_ref), (w_in_hbm, w_in_ref), (w_head_hbm, w_head_ref))
    small_loads = [
        pltpu.make_async_copy(source, target, load_sem.at[9, at])
        for at, (source, target) in enumerate(small)
    ]
    u_loads, modulus_loads, mass_loads, load_loads, weight_loads = [], [], [], [], []
    for i in range(NODES_X):
        for m in range(3):
            u_loads.append(pltpu.make_async_copy(u_hbm.at[i, :, m : m + 1], ux.at[m, 1:18, i + 1 : i + 2], load_sem.at[m, i]))
    for layer in range(HIDDEN_LAYERS):
        weight_loads.append(pltpu.make_async_copy(w_hidden_hbm.at[layer], weights.at[layer], load_sem.at[8, layer]))
    for i in range(BX):
        modulus_loads.append(pltpu.make_async_copy(modulus_hbm.at[i], modulus.at[:, i + 1], load_sem.at[6, i]))
    for i in range(NODES_X):
        mass_loads.append(pltpu.make_async_copy(mass_hbm.at[i], mass_part.at[1:18, i + 1], load_sem.at[7, i]))
        for m in range(3):
            load_loads.append(pltpu.make_async_copy(load_hbm.at[i, :, m : m + 1], lx.at[m, 1:18, i + 1 : i + 2], load_sem.at[3 + m, i]))
    loads = small_loads + u_loads + weight_loads + modulus_loads + mass_loads + load_loads
    for copy in loads:
        copy.start()

    barrier = pltpu.get_barrier_semaphore()
    for device in others:
        pl.semaphore_signal(barrier, inc=1, device_id=device, device_id_type=MESH)
    for copy in small_loads:
        copy.wait()

    ids = ids_ref[...]
    slot = lax.broadcasted_iota(jnp.int32, (1, SLOTS), 1)
    live = jnp.where(slot < count_ref[...], 1.0, 0.0)
    at_k = ids & (NZ - 1)
    at_j = (ids >> 8) & (BY - 1)
    at_i = ids >> 12
    onehot_k[...] = jnp.where(
        lax.broadcasted_iota(jnp.int32, (NZ, SLOTS), 0) == at_k, 1.0, 0.0
    ).astype(BF16)
    onehot_r[...] = jnp.where(
        lax.broadcasted_iota(jnp.int32, (COLUMNS, SLOTS), 0) == at_j * BX + at_i, live, 0.0
    ).astype(BF16)
    k_column = jnp.broadcast_to(at_k.astype(F32), (128, SLOTS)).T
    lane_k = lax.broadcasted_iota(jnp.int32, (SLOTS, 128), 1).astype(F32)
    onehot_kt[:, 0:128] = jnp.where(k_column == lane_k, 1.0, 0.0).astype(BF16)
    onehot_kt[:, 128:256] = jnp.where(k_column == lane_k + 128.0, 1.0, 0.0).astype(BF16)

    sub = lax.broadcasted_iota(jnp.int32, (SUB, NZ), 0)
    own_elements = (sub >= 1) & (sub <= BX)
    for copy in u_loads:
        copy.wait()

    def pairs_of(ref, row):
        return [x_pairs(ref[m, row]) for m in range(3)]

    def strain_step(row, low):
        high = pairs_of(ux, row + 1)
        for n, value in enumerate(strain_row(low, high)):
            strain_now[n, row - 1] = jnp.where(own_elements, 0.25 * value, 0.0)
        return high

    by_rows(1, 1 + BY, 8, strain_step, pairs_of(ux, 1))

    picked = []
    for n in range(6):
        for g in range(BY // 2):
            pair = jnp.where(
                sub < BX,
                pltpu.roll(strain_now[n, 2 * g], SUB - 1, 0),
                pltpu.roll(strain_now[n, 2 * g + 1], BX - 1, 0),
            )
            high = pair.astype(BF16).astype(F32)
            packed[n * COLUMNS + g * SUB : n * COLUMNS + (g + 1) * SUB] = high
            packed[(6 + n) * COLUMNS + g * SUB : (6 + n) * COLUMNS + (g + 1) * SUB] = pair - high
    at_slots = mm(packed[...].astype(BF16), onehot_k[...])
    for n in range(6):
        rows = at_slots[n * COLUMNS : (n + 1) * COLUMNS] + at_slots[(6 + n) * COLUMNS : (7 + n) * COLUMNS]
        picked.append(jnp.sum(rows * onehot_r[...].astype(F32), axis=0, keepdims=True))
    eps = jnp.concatenate(picked + [jnp.zeros((2, SLOTS), F32)], axis=0)
    eps_high = eps.astype(BF16).astype(F32)
    stacked = jnp.concatenate(
        [eps_high, eps - eps_high, eps_high, jnp.zeros((104, SLOTS), F32)], axis=0
    )
    inputs_t[...] = stacked.T.astype(BF16)

    w_in = jnp.concatenate([w_in_ref[...], jnp.zeros((2, HID), F32)], axis=0)
    w_in_high = w_in.astype(BF16).astype(F32)
    w_first = jnp.concatenate(
        [w_in_high, w_in_high, w_in - w_in_high, jnp.zeros((104, HID), F32)], axis=0
    ).astype(BF16)
    to_row = lax.broadcasted_iota(jnp.int32, (128, 42), 0)
    from_out = lax.broadcasted_iota(jnp.int32, (128, 42), 1)
    place = jnp.where(
        (from_out == (to_row // 8) * 6 + to_row % 8) & (to_row % 8 < 6) & (to_row < 56), 1.0, 0.0
    ).astype(BF16)
    head_high, head_low = split(w_head_ref[...])
    head = (mm(place, head_high) + mm(place, head_low)).T
    def product(hidden, parts):
        high, mixed_weight = parts
        hidden_high = hidden.astype(BF16)
        low = hidden - hidden_high.astype(F32)
        mixed = jnp.concatenate([(low * (LOW_SCALE / HIGH_SCALE)).astype(F8), hidden.astype(F8)], axis=1)
        return mm(hidden_high, high) + mm(mixed, mixed_weight) * (1.0 / LOW_SCALE)

    def narrow(weight):
        high = weight.astype(BF16)
        low = weight - high.astype(F32)
        return high, jnp.concatenate(
            [(weight * HIGH_SCALE).astype(F8), (low * LOW_SCALE).astype(F8)], axis=0
        )

    halves = []
    for layer in range(HIDDEN_LAYERS):
        weight_loads[layer].wait()
        halves.append(narrow(weights[layer]))

    half = SLOTS // 2
    left, right = mm(inputs_t[0:half], w_first), mm(inputs_t[half:SLOTS], w_first)
    for parts in halves + [narrow(head)]:
        left = product(jnp.tanh(left), parts)
        right = product(jnp.tanh(right), parts)
    out_t[:, 0:half] = left.T
    out_t[:, half:SLOTS] = right.T

    for copy in mass_loads:
        copy.wait()
    pl.semaphore_wait(barrier, peers - 1)
    mass_copies = []
    for q, ((dx, dy), device) in enumerate(zip(DIRECTIONS, neighbours)):
        sy, sx, ty, tx = face(dx, dy, 2)
        kind = 0 if dy == 0 else (1 if dx == 0 else 2)
        copy = pltpu.make_async_remote_copy(
            mass_part.at[sy, sx], mass_rx.at[kind, ty, tx], mass_send.at[q], mass_recv.at[q],
            device_id=device, device_id_type=MESH,
        )
        copy.start()
        mass_copies.append(copy)

    values[0:6] = out_t[0:6]
    values[LIVE : LIVE + 1] = jnp.ones((1, SLOTS), F32)
    factor = [out_t[8 * (a + 1) : 8 * (a + 2)] for a in range(6)]
    for at, (a, b) in enumerate(PAIRS):
        values[FIRST_PAIR + at : FIRST_PAIR + at + 1] = jnp.sum(
            factor[a] * factor[b], axis=0, keepdims=True
        ) * (1.0 / 6.0)

    def spread_ready(at):
        for n in range(GROUP):
            high, low = split(values[at * GROUP + n : at * GROUP + n + 1])
            rows = onehot_r[...]
            lhs[at, n * COLUMNS : (n + 1) * COLUMNS] = rows * high
            lhs[at, (GROUP + n) * COLUMNS : (GROUP + n + 1) * COLUMNS] = rows * low

    def spread_group(at):
        if at < N_SCATTER // GROUP - 1:
            spread_ready(at + 1)
        spread = mm(lhs[at], onehot_kt[...])
        return spread[: GROUP * COLUMNS] + spread[GROUP * COLUMNS :]

    def element_rows(spread, n, g):
        start = n * COLUMNS + g * SUB
        both = spread[start : start + SUB]
        return pltpu.roll(both, 1, 0), pltpu.roll(both, 5, 0)

    def sum_copies(parity):
        copies = []
        for q, ((dx, dy), device) in enumerate(zip(DIRECTIONS, neighbours)):
            sy, sx, ty, tx = face(dx, dy, 2)
            kind = 0 if dy == 0 else (1 if dx == 0 else 2)
            copies.append(
                pltpu.make_async_remote_copy(
                    v2.at[:, sy, sx], sum_rx.at[parity, kind, :, ty, tx],
                    sum_send.at[parity, q], sum_recv.at[parity, q],
                    device_id=device, device_id_type=MESH,
                )
            )
        return copies

    def exact_copies(parity):
        copies = []
        for q, ((dx, dy), device) in enumerate(zip(DIRECTIONS, neighbours)):
            sy, sx, ty, tx = face(dx, dy, 1)
            copies.append(
                pltpu.make_async_remote_copy(
                    v1.at[:, sy, sx], copy_rx.at[parity, :, ty, tx],
                    copy_send.at[parity, q], copy_recv.at[parity, q],
                    device_id=device, device_id_type=MESH,
                )
            )
        return copies

    global_x = index_x * BX + sub - 1
    keep_x = jnp.where(
        (global_x >= 0) & (global_x < size_x * BX) & (sub < SUB - 1), 1.0, 0.0
    )
    own_planes = (sub >= 1) & (sub <= NODES_X)
    rim_planes = ((sub <= 1) & (index_x > 0)) | ((sub >= NODES_X) & (sub <= NODES_X + 1))
    halo_planes = (sub == 0) | (sub == NODES_X + 1)
    flank_low, corner_low = own_planes & (index_y > 0), rim_planes & (index_y > 0)
    valid_elements = (sub <= BX + 1) & ((sub >= 1) | (index_x > 0))

    def keep_of(row):
        global_y = index_y * BY + row - 1
        inside = jnp.where((global_y >= 0) & (global_y < size_y * BY), 1.0, 0.0)
        return keep_x * inside

    def assembled(part, received, row):
        at_rim = isinstance(row, int)
        total = jnp.zeros((SUB, NZ), F32)
        if not at_rim or 1 <= row <= NODES_Y:
            total = part + jnp.where(rim_planes, received(0), 0.0)
        if at_rim:
            flank, corner = (flank_low, corner_low) if row <= 1 else (own_planes, rim_planes)
            total = total + jnp.where(flank, received(1), 0.0) + jnp.where(corner, received(2), 0.0)
        return total

    def all_rows(body):
        for row in (0, 1, NODES_Y, NODES_Y + 1):
            body(row)

        def inner(row, carry):
            body(row)
            return carry

        by_rows(2, NODES_Y, 3, inner, 0)

    def stress_now(row):
        scale = 0.25 * modulus[row]
        base = scale * (1.0 - 0.75 * scattered[LIVE, row])
        eps_row = [strain_now[n, row] for n in range(6)]
        trace = LAME_FIRST * (eps_row[0] + eps_row[1] + eps_row[2])
        elastic = [trace + 2.0 * LAME_SECOND * eps_row[n] for n in range(3)]
        elastic += [LAME_SECOND * eps_row[n] for n in range(3, 6)]
        return [base * elastic[n] + scale * scattered[n, row] for n in range(6)]

    zero = jnp.zeros((SUB, NZ), F32)
    no_parts = [(zero, zero)] * 3

    def residual_step(row, before):
        parts = force_parts(stress_now(row - 1))
        for m in range(3):
            force = force_of(parts[m][0] + before[m][0], parts[m][1] + before[m][1])
            v2[m, row] = jnp.where(own_planes, lx[m, row] - force, 0.0)
        return [(parts[m][0], parts[m][2]) for m in range(3)]

    spread_ready(0)
    spread = spread_group(0)
    for n in range(GROUP):
        for g in range(BY // 2):
            for odd, entry in enumerate(element_rows(spread, n, g)):
                scattered[n, 2 * g + odd] = jnp.where(own_elements, entry, 0.0)
    for copy in modulus_loads + load_loads:
        copy.wait()
    last = by_rows(1, 1 + BY, 8, residual_step, no_parts)
    for m in range(3):
        v2[m, NODES_Y] = jnp.where(own_planes, lx[m, NODES_Y] - force_of(*last[m]), 0.0)

    first_copies = sum_copies(0)
    for copy in first_copies:
        copy.start()

    tangent_copies = []
    planes = slice(1, 1 + BX)
    for group in range(N_PAIRS // GROUP):
        spread = spread_group(group + 1)
        for g in range(BY // 2):
            scales = [modulus[2 * g + odd] * (1.0 / 16.0) for odd in range(2)]
            bases = [scales[odd] * (1.0 - 0.75 * scattered[LIVE, 2 * g + odd]) for odd in range(2)]
            for n in range(GROUP):
                at = group * GROUP + n
                for odd, entry in enumerate(element_rows(spread, n, g)):
                    entry = scales[odd] * entry
                    if iso(*PAIRS[at]):
                        entry = entry + bases[odd] * iso(*PAIRS[at])
                    tangent[at, 2 * g + odd + 1, planes] = entry[planes]
        entries = pl.ds(group * GROUP, GROUP)
        for q, ((dx, dy), device) in enumerate(zip(DIRECTIONS, neighbours)):
            sy, sx, ty, tx = element_face(dx, dy)
            copy = pltpu.make_async_remote_copy(
                tangent.at[entries, sy, sx], tangent.at[entries, ty, tx],
                tan_send.at[group, q], tan_recv.at[group, q],
                device_id=device, device_id_type=MESH,
            )
            copy.start()
            tangent_copies.append(copy)

    for ref in (q1, q0, d1, x):
        ref[...] = jnp.zeros_like(ref)
    for copy in mass_copies:
        copy.wait()

    def mass_row(row):
        mass_full[row] = assembled(mass_part[row], lambda kind: mass_rx[kind, row], row)

    all_rows(mass_row)
    for copy in first_copies:
        copy.wait()

    def start_row(row):
        keep = keep_of(row)
        for m in range(3):
            part = None if isinstance(row, int) and row in (0, NODES_Y + 1) else v2[m, row]
            v0[m, row] = keep * assembled(part, lambda kind: sum_rx[0, kind, m, row], row)

    all_rows(start_row)
    for copy in tangent_copies:
        copy.wait()

    def stress_row(row, strain, present):
        entries = [tangent[at, row] for at in range(N_PAIRS)]
        result = []
        for a in range(6):
            total = entries[PAIR_OF[a, 0]] * strain[0]
            for b in range(1, 6):
                total = total + entries[PAIR_OF[a, b]] * strain[b]
            result.append(jnp.where(present, total, 0.0))
        return result

    def first_image(row, carry):
        low, before = carry
        high = pairs_of(v0, row + 1)
        present = valid_elements & (row + index_y > 0)
        parts = force_parts(stress_row(row, strain_row(low, high), present))
        keep = keep_of(row)
        for m in range(3):
            force = force_of(parts[m][0] + before[m][0], parts[m][1] + before[m][1])
            v1[m, row] = keep * (force + mass_full[row] * v0[m, row])
        return high, [(parts[m][0], parts[m][2]) for m in range(3)]

    def second_image(row, carry):
        low, before, sums = carry
        high = pairs_of(v1, row + 1)
        parts = force_parts(stress_row(row, strain_row(low, high), own_elements))
        rr, r_ar, ar_ar, ar_aar = sums
        for m in range(3):
            here, image = v0[m, row], v1[m, row]
            force = force_of(parts[m][0] + before[m][0], parts[m][1] + before[m][1])
            force = force + mass_part[row] * image
            v2[m, row] = force
            rr = rr + here * here
            r_ar = r_ar + here * image
            ar_ar = ar_ar + image * image
            ar_aar = ar_aar + image * force
        return high, [(parts[m][0], parts[m][2]) for m in range(3)], (rr, r_ar, ar_ar, ar_aar)

    lane = lax.broadcasted_iota(jnp.int32, (1, 128), 1)

    def outer(step, carry):
        be0, ia1, ia0, rr_before = carry
        parity = lax.rem(step, 2)
        sum_parity = lax.rem(step + 1, 2)
        by_rows(0, BY + 2, 6, first_image, (pairs_of(v0, 0), no_parts))
        exact = exact_copies(parity)
        for copy in exact:
            copy.start()
        _, before, sums = by_rows(
            1, 1 + BY, 8, second_image, (pairs_of(v1, 1), no_parts, (zero,) * 4)
        )
        ar_aar = sums[3]
        for m in range(3):
            image = v1[m, NODES_Y]
            force = force_of(*before[m]) + mass_part[NODES_Y] * image
            v2[m, NODES_Y] = force
            ar_aar = ar_aar + jnp.where(own_planes, image * force, 0.0)
        summed = sum_copies(sum_parity)
        for copy in summed[:-FACES]:
            copy.start()

        message = jnp.zeros((1, 128), F32)
        for at, (value, mask) in enumerate(
            ((sums[0], own_elements), (sums[1], own_elements), (sums[2], own_elements), (ar_aar, own_planes))
        ):
            total = jnp.sum(jnp.where(mask, value, 0.0), axis=0, keepdims=True)
            total = jnp.sum(total, axis=1, keepdims=True)
            message = message + jnp.where(lane == at, total, 0.0)
        gathered[parity, me] = message

        for device in others:
            pltpu.make_async_remote_copy(
                gathered.at[parity, me], gathered.at[parity, me],
                all_send.at[parity], all_recv.at[parity],
                device_id=device, device_id_type=MESH,
            ).start()
        for copy in summed[-FACES:]:
            copy.start()
        for copy in exact + summed:
            copy.wait()

        def image_row(row):
            keep = keep_of(row)
            outside = isinstance(row, int) and row in (0, NODES_Y + 1)
            for m in range(3):
                rim = copy_rx[parity, m, row]
                if outside:
                    ar2 = jnp.where(sub <= NODES_X + 1, rim, 0.0)
                else:
                    ar2 = jnp.where(halo_planes, rim, v1[m, row])
                ar2 = keep * ar2
                part = None if outside else v2[m, row]
                v2[m, row] = keep * assembled(part, lambda kind: sum_rx[sum_parity, kind, m, row], row)
                v1[m, row] = ar2
                q0[m, row] = (q1[m, row] - be0 * q0[m, row] - ar2) * ia1

        all_rows(image_row)
        rest = gathered.at[parity, 0 : peers - 1]
        pltpu.make_async_copy(rest, rest, all_recv.at[parity]).wait()
        totals = [jnp.sum(gathered[parity, at : at + 16], axis=0) for at in range(0, peers, 16)]
        while len(totals) > 1:
            totals = [a + b for a, b in zip(totals[0::2], totals[1::2])]
        totals = totals[0]
        rr2, m1, m2, m3 = [
            jnp.sum(jnp.where(lane == at, totals, 0.0), axis=1, keepdims=True) for at in range(4)
        ]
        be1 = jnp.where(step == 0, 0.0, rr2 / rr_before)
        r_q1 = -rr2 * ia1
        ar_q1 = (r_q1 - m1) * ia1
        q1_q1 = (rr_before + rr2) * ia1 * ia1
        ar_q0 = rr2 * ia1 * ia0
        q1_q0 = -rr_before * ia1 * ia0
        q1_aar = ia1 * (ar_q1 - be0 * ar_q0 - m2)
        q1_aq1 = ia1 * (q1_q1 - be0 * q1_q0 - ar_q1)
        q2_q2 = m2 + 2.0 * be1 * ar_q1 + be1 * be1 * q1_q1
        ar_q2 = m2 + be1 * ar_q1
        q2_aq2 = m3 + 2.0 * be1 * q1_aar + be1 * be1 * q1_aq1
        a2 = rr2 / (m1 + be1 * r_q1)
        rr3 = a2 * a2 * q2_q2 - rr2
        be2 = rr3 / rr2
        a3 = rr3 / (m1 - 2.0 * a2 * ar_q2 + a2 * a2 * q2_aq2 - be2 * rr3 / a2)

        def update_row(row, unused):
            for m in range(3):
                ar2, old = v1[m, row], q1[m, row]
                q2 = ar2 + be1 * old
                r3 = v0[m, row] - a2 * q2
                q3 = ar2 - a2 * (v2[m, row] + be1 * q0[m, row]) + be2 * q2
                d2 = v0[m, row] + be1 * d1[m, row]
                d3 = r3 + be2 * d2
                x[m, row] = x[m, row] + (a2 * d2 + a3 * d3)
                v0[m, row] = r3 - a3 * q3
                q1[m, row] = q3
                q0[m, row] = q2
                d1[m, row] = d3
            return unused

        by_rows(0, ROWS - 1, 3, update_row, 0)
        update_row(ROWS - 1, 0)
        pltpu.make_async_copy(rest, rest, all_send.at[parity]).wait()
        return be2, 1.0 / a3, 1.0 / a2, rr3

    none = jnp.zeros((1, 1), F32)
    lax.fori_loop(0, OUTER, outer, (none, none, none, none + 1.0))

    stores = [
        pltpu.make_async_copy(
            source.at[m, 1:18, i + 1 : i + 2], target.at[i, :, m : m + 1], out_sem.at[at, m, i]
        )
        for at, (source, target) in enumerate(((x, increment_hbm), (v0, residual_hbm)))
        for i in range(NODES_X)
        for m in range(3)
    ]
    for copy in stores:
        copy.start()
    for copy in stores:
        copy.wait()


def place_kernel(increment_in, residual_in, increment_out, residual_out, sem):
    copies = [
        pltpu.make_async_copy(increment_in, increment_out, sem.at[0]),
        pltpu.make_async_copy(residual_in, residual_out, sem.at[1]),
    ]
    for copy in copies:
        copy.start()
    for copy in copies:
        copy.wait()


def solution(mesh):
    size_x, size_y = mesh.shape["gx"], mesh.shape["gy"]
    peers = size_x * size_y
    field = jax.ShapeDtypeStruct((NODES_X, NODES_Y, 3, NZ), F32)

    def vmem(*shape, dtype=F32):
        return pltpu.VMEM(shape, dtype)

    def node(*lead):
        return vmem(*lead, ROWS, SUB, NZ)

    dma = pltpu.SemaphoreType.DMA
    scratch = [
        vmem(1, SLOTS, dtype=jnp.int32), vmem(1, 1, dtype=jnp.int32), vmem(6, HID), vmem(42, HID),
        node(3), node(3), node(), node(), node(3), vmem(BY, SUB, NZ), vmem(HIDDEN_LAYERS, HID, HID),
        vmem(6, BY, SUB, NZ), vmem(12 * COLUMNS, NZ), vmem(NZ, SLOTS, dtype=BF16), vmem(SLOTS, NZ, dtype=BF16),
        vmem(COLUMNS, SLOTS, dtype=BF16), vmem(SLOTS, 128, dtype=BF16),
        vmem(128, SLOTS), vmem(32, SLOTS), vmem(N_SCATTER // GROUP, 2 * GROUP * COLUMNS, SLOTS, dtype=BF16),
        vmem(GROUP, BY, SUB, NZ),
        vmem(N_PAIRS, BY + 2, SUB, NZ),
        node(3), node(3), node(3), node(3), node(3), node(3), node(3),
        node(2, 3, 3), node(2, 3), vmem(2, peers, 1, 128),
        dma((10, 5)), dma((2, 3, 5)), dma((8,)), dma((8,)), dma((3, 8)), dma((3, 8)),
        dma((2, 8)), dma((2, 8)), dma((2, 8)), dma((2, 8)), dma((2,)), dma((2,)),
    ]

    def body(u_now, load, mass, modulus, plastic_ids, plastic_count, w_in, w_hidden, w_head):
        hbm = pl.BlockSpec(memory_space=pl.ANY)
        increment, residual = pl.pallas_call(
            lambda *refs: kernel(size_x, size_y, *refs),
            out_shape=(field, field),
            in_specs=[hbm] * 9,
            out_specs=(hbm, hbm),
            scratch_shapes=scratch,
            compiler_params=pltpu.CompilerParams(
                collective_id=0, has_side_effects=True, vmem_limit_bytes=60 * 2**20
            ),
        )(
            u_now.transpose(1, 2, 0, 3), load.transpose(1, 2, 0, 3), mass, modulus,
            plastic_ids.reshape(1, SLOTS), plastic_count, w_in, w_hidden, w_head.T,
        )
        increment, residual = pl.pallas_call(
            place_kernel,
            out_shape=(field, field),
            in_specs=[pl.BlockSpec(memory_space=pltpu.VMEM)] * 2,
            out_specs=(hbm, hbm),
            scratch_shapes=[dma((2,))],
        )(increment, residual)
        return increment.transpose(2, 0, 1, 3), residual.transpose(2, 0, 1, 3)

    split_field = P(None, "gx", "gy", None)
    split_block = P("gx", "gy", None)
    return jax.shard_map(
        body,
        mesh=mesh,
        in_specs=(
            split_field, split_field, split_block, split_block, split_block, P("gx", "gy"), P(), P(), P(),
        ),
        out_specs=(split_field, split_field),
        check_vma=False,
    )
```

```python
import jax
import jax.numpy as jnp
from jax import lax
from jax.experimental import pallas as pl
from jax.experimental.pallas import tpu as pltpu
from jax.sharding import PartitionSpec as P

MESH = pl.DeviceIdType.MESH
F32, BF16, F8 = jnp.float32, jnp.bfloat16, jnp.float8_e4m3fn
HIGH_SCALE, LOW_SCALE = 16.0, 16.0 * 512.0
LAME_FIRST = 0.3 / (1.3 * 0.4)
LAME_SECOND = 1.0 / 2.6

BX, BY, NZ = 4, 16, 256
NODES_X, NODES_Y = BX + 1, BY + 1
ROWS = BY + 3
SUB = 8
SLOTS, HID, HIDDEN_LAYERS = 1024, 512, 3
COLUMNS = BY * BX
OUTER = 3
GROUP = 7
RINGS = 4

PAIRS = [(a, b) for a in range(6) for b in range(a, 6)]
PAIR_OF = {}
for _at, (_a, _b) in enumerate(PAIRS):
    PAIR_OF[_a, _b] = PAIR_OF[_b, _a] = _at
N_PAIRS = len(PAIRS)
N_SCATTER = 28
LIVE, FIRST_PAIR = 6, 7

DIRECTIONS = [(dx, dy) for dx in (-1, 1) for dy in (-1, 1)] + [(0, -1), (0, 1), (-1, 0), (1, 0)]
FACES = 2


def iso(a, b):
    if a < 3 and b < 3:
        return LAME_FIRST + (2.0 * LAME_SECOND if a == b else 0.0)
    return LAME_SECOND if a == b else 0.0


def z_next(values):
    edge = lax.broadcasted_iota(jnp.int32, (values.shape[0], 128), 1) == 127
    low, high = [pltpu.roll(values[:, at : at + 128], 127, 1) for at in (0, 128)]
    return jnp.concatenate([jnp.where(edge, high, low), jnp.where(edge, 0.0, high)], axis=1)


def z_prev(values):
    edge = lax.broadcasted_iota(jnp.int32, (values.shape[0], 128), 1) == 0
    low, high = [pltpu.roll(values[:, at : at + 128], 1, 1) for at in (0, 128)]
    return jnp.concatenate([jnp.where(edge, 0.0, low), jnp.where(edge, low, high)], axis=1)


def x_pairs(values):
    upper = pltpu.roll(values, SUB - 1, 0)
    return upper + values, upper - values


def strain_row(low, high):
    a = [low[m][1] + high[m][1] for m in range(3)]
    b = [high[m][0] - low[m][0] for m in range(3)]
    c = [high[m][0] + low[m][0] for m in range(3)]
    yz, xz, xy = c[1] + b[2], c[0] + a[2], b[0] + a[1]
    return [
        z_next(a[0]) + a[0],
        z_next(b[1]) + b[1],
        z_next(c[2]) - c[2],
        z_next(yz) + (b[2] - c[1]),
        z_next(xz) + (a[2] - c[0]),
        z_next(xy) + xy,
    ]


def force_parts(stress):
    before = [z_prev(s) for s in stress]
    total = {n: stress[n] + before[n] for n in (0, 1, 3, 4, 5)}
    differ = {n: before[n] - stress[n] for n in (2, 3, 4)}
    parts = []
    for along_x, along_y, along_z in ((0, 5, 4), (5, 1, 3), (4, 3, 2)):
        parts.append(
            (
                total[along_x],
                differ[along_z] - total[along_y],
                differ[along_z] + total[along_y],
            )
        )
    return parts


def force_of(along_x, other):
    return pltpu.roll(along_x + other, 1, 0) + (other - along_x)


def split(values):
    high = values.astype(BF16)
    return high, (values - high.astype(F32)).astype(BF16)


def mm(a, b):
    return jnp.dot(a, b, preferred_element_type=F32)


def face(dx, dy, depth):
    if depth == 2:
        sx = {-1: slice(1, 3), 0: slice(1, 6), 1: slice(4, 6)}[dx]
        tx = {-1: slice(5, 7), 0: slice(1, 6), 1: slice(0, 2)}[dx]
        sy = {-1: slice(1, 3), 0: slice(1, 18), 1: slice(16, 18)}[dy]
        ty = {-1: slice(17, 19), 0: slice(1, 18), 1: slice(0, 2)}[dy]
    else:
        sx = {-1: slice(2, 3), 0: slice(1, 6), 1: slice(4, 5)}[dx]
        tx = {-1: slice(6, 7), 0: slice(1, 6), 1: slice(0, 1)}[dx]
        sy = {-1: slice(2, 3), 0: slice(1, 18), 1: slice(16, 17)}[dy]
        ty = {-1: slice(18, 19), 0: slice(1, 18), 1: slice(0, 1)}[dy]
    return sy, sx, ty, tx


def element_face(dx, dy):
    sx = {-1: slice(1, 2), 0: slice(1, 5), 1: slice(4, 5)}[dx]
    tx = {-1: slice(5, 6), 0: slice(1, 5), 1: slice(0, 1)}[dx]
    sy = {-1: slice(1, 2), 0: slice(1, 17), 1: slice(16, 17)}[dy]
    ty = {-1: slice(17, 18), 0: slice(1, 17), 1: slice(0, 1)}[dy]
    return sy, sx, ty, tx


def all_offsets(size_x, size_y):
    offsets = [
        (z, core, x, y)
        for z in range(size_x // 2)
        for core in range(2)
        for x in range(size_y // RINGS)
        for y in range(RINGS)
    ][1:]

    def hops(offset):
        z, core, x, y = offset
        return sum(min(d, RINGS - d) for d in (z, x, y)) * 2 + core

    return sorted(offsets, key=hops, reverse=True)


def by_rows(first, last, width, body, carry):
    assert (last - first) % width == 0

    def block(at, carry):
        for n in range(width):
            carry = body(first + at * width + n, carry)
        return carry

    return lax.fori_loop(0, (last - first) // width, block, carry)


def kernel(
    size_x, size_y,
    u_hbm, load_hbm, mass_hbm, modulus_hbm, ids_hbm, count_hbm, w_in_hbm, w_hidden_hbm, w_head_hbm,
    increment_hbm, residual_hbm,
    ids_ref, count_ref, w_in_ref, w_head_ref, ux, lx, mass_part, mass_full, mass_rx, modulus, weights,
    strain_now, packed, onehot_k, onehot_kt, onehot_r, inputs_t, out_t, values, lhs, scattered,
    tangent,
    v0, v1, v2, q1, q0, d1, x, sum_rx, copy_rx, gathered,
    load_sem, out_sem, mass_send, mass_recv, tan_send, tan_recv,
    sum_send, sum_recv, copy_send, copy_recv, all_send, all_recv,
):
    index_x, index_y = lax.axis_index("gx"), lax.axis_index("gy")
    me = index_x * size_y + index_y
    peers = size_x * size_y
    neighbours = [
        (lax.rem(index_x + dx + size_x, size_x), lax.rem(index_y + dy + size_y, size_y))
        for dx, dy in DIRECTIONS
    ]

    ring_x, ring_y = index_y // RINGS, lax.rem(index_y, RINGS)
    ring_z, core = index_x // 2, lax.rem(index_x, 2)
    at_z = [lax.rem(ring_z + d, RINGS) * 2 for d in range(size_x // 2)]
    at_core = [core, 1 - core]
    at_ring_x = [lax.rem(ring_x + d, RINGS) * RINGS for d in range(size_y // RINGS)]
    at_ring_y = [lax.rem(ring_y + d, RINGS) for d in range(RINGS)]
    along_gx = [[z + c for c in at_core] for z in at_z]
    along_gy = [[a + b for b in at_ring_y] for a in at_ring_x]
    others = [
        (along_gx[z][c], along_gy[a][b]) for z, c, a, b in all_offsets(size_x, size_y)
    ]

    for ref in (mass_part, modulus):
        ref[...] = jnp.zeros_like(ref)
    small = ((ids_hbm, ids_ref), (count_hbm, count_ref), (w_in_hbm, w_in_ref), (w_head_hbm, w_head_ref))
    small_loads = [
        pltpu.make_async_copy(source, target, load_sem.at[9, at])
        for at, (source, target) in enumerate(small)
    ]
    u_loads, modulus_loads, mass_loads, load_loads, weight_loads = [], [], [], [], []
    for i in range(NODES_X):
        for m in range(3):
            u_loads.append(pltpu.make_async_copy(u_hbm.at[i, :, m : m + 1], ux.at[m, 1:18, i + 1 : i + 2], load_sem.at[m, i]))
    for layer in range(HIDDEN_LAYERS):
        weight_loads.append(pltpu.make_async_copy(w_hidden_hbm.at[layer], weights.at[layer], load_sem.at[8, layer]))
    for i in range(BX):
        modulus_loads.append(pltpu.make_async_copy(modulus_hbm.at[i], modulus.at[:, i + 1], load_sem.at[6, i]))
    for i in range(NODES_X):
        mass_loads.append(pltpu.make_async_copy(mass_hbm.at[i], mass_part.at[1:18, i + 1], load_sem.at[7, i]))
        for m in range(3):
            load_loads.append(pltpu.make_async_copy(load_hbm.at[i, :, m : m + 1], lx.at[m, 1:18, i + 1 : i + 2], load_sem.at[3 + m, i]))
    loads = small_loads + u_loads + weight_loads + modulus_loads + mass_loads + load_loads
    for copy in loads:
        copy.start()

    barrier = pltpu.get_barrier_semaphore()
    for device in others:
        pl.semaphore_signal(barrier, inc=1, device_id=device, device_id_type=MESH)
    for copy in small_loads:
        copy.wait()

    ids = ids_ref[...]
    slot = lax.broadcasted_iota(jnp.int32, (1, SLOTS), 1)
    live = jnp.where(slot < count_ref[...], 1.0, 0.0)
    at_k = ids & (NZ - 1)
    at_j = (ids >> 8) & (BY - 1)
    at_i = ids >> 12
    onehot_k[...] = jnp.where(
        lax.broadcasted_iota(jnp.int32, (NZ, SLOTS), 0) == at_k, 1.0, 0.0
    ).astype(BF16)
    onehot_r[...] = jnp.where(
        lax.broadcasted_iota(jnp.int32, (COLUMNS, SLOTS), 0) == at_j * BX + at_i, live, 0.0
    ).astype(BF16)
    k_column = jnp.broadcast_to(at_k.astype(F32), (128, SLOTS)).T
    lane_k = lax.broadcasted_iota(jnp.int32, (SLOTS, 128), 1).astype(F32)
    onehot_kt[:, 0:128] = jnp.where(k_column == lane_k, 1.0, 0.0).astype(BF16)
    onehot_kt[:, 128:256] = jnp.where(k_column == lane_k + 128.0, 1.0, 0.0).astype(BF16)

    sub = lax.broadcasted_iota(jnp.int32, (SUB, NZ), 0)
    own_elements = (sub >= 1) & (sub <= BX)
    for copy in u_loads:
        copy.wait()

    def pairs_of(ref, row):
        return [x_pairs(ref[m, row]) for m in range(3)]

    def strain_step(row, low):
        high = pairs_of(ux, row + 1)
        for n, value in enumerate(strain_row(low, high)):
            strain_now[n, row - 1] = jnp.where(own_elements, 0.25 * value, 0.0)
        return high

    by_rows(1, 1 + BY, 8, strain_step, pairs_of(ux, 1))

    picked = []
    for n in range(6):
        for g in range(BY // 2):
            pair = jnp.where(
                sub < BX,
                pltpu.roll(strain_now[n, 2 * g], SUB - 1, 0),
                pltpu.roll(strain_now[n, 2 * g + 1], BX - 1, 0),
            )
            high = pair.astype(BF16).astype(F32)
            packed[n * COLUMNS + g * SUB : n * COLUMNS + (g + 1) * SUB] = high
            packed[(6 + n) * COLUMNS + g * SUB : (6 + n) * COLUMNS + (g + 1) * SUB] = pair - high
    at_slots = mm(packed[...].astype(BF16), onehot_k[...])
    for n in range(6):
        rows = at_slots[n * COLUMNS : (n + 1) * COLUMNS] + at_slots[(6 + n) * COLUMNS : (7 + n) * COLUMNS]
        picked.append(jnp.sum(rows * onehot_r[...].astype(F32), axis=0, keepdims=True))
    eps = jnp.concatenate(picked + [jnp.zeros((2, SLOTS), F32)], axis=0)
    eps_high = eps.astype(BF16).astype(F32)
    stacked = jnp.concatenate(
        [eps_high, eps - eps_high, eps_high, jnp.zeros((104, SLOTS), F32)], axis=0
    )
    inputs_t[...] = stacked.T.astype(BF16)

    w_in = jnp.concatenate([w_in_ref[...], jnp.zeros((2, HID), F32)], axis=0)
    w_in_high = w_in.astype(BF16).astype(F32)
    w_first = jnp.concatenate(
        [w_in_high, w_in_high, w_in - w_in_high, jnp.zeros((104, HID), F32)], axis=0
    ).astype(BF16)
    to_row = lax.broadcasted_iota(jnp.int32, (128, 42), 0)
    from_out = lax.broadcasted_iota(jnp.int32, (128, 42), 1)
    place = jnp.where(
        (from_out == (to_row // 8) * 6 + to_row % 8) & (to_row % 8 < 6) & (to_row < 56), 1.0, 0.0
    ).astype(BF16)
    head_high, head_low = split(w_head_ref[...])
    head = (mm(place, head_high) + mm(place, head_low)).T
    def product(hidden, parts):
        high, mixed_weight = parts
        hidden_high = hidden.astype(BF16)
        low = hidden - hidden_high.astype(F32)
        mixed = jnp.concatenate([(low * (LOW_SCALE / HIGH_SCALE)).astype(F8), hidden.astype(F8)], axis=1)
        return mm(hidden_high, high) + mm(mixed, mixed_weight) * (1.0 / LOW_SCALE)

    def narrow(weight):
        high = weight.astype(BF16)
        low = weight - high.astype(F32)
        return high, jnp.concatenate(
            [(weight * HIGH_SCALE).astype(F8), (low * LOW_SCALE).astype(F8)], axis=0
        )

    halves = []
    for layer in range(HIDDEN_LAYERS):
        weight_loads[layer].wait()
        halves.append(narrow(weights[layer]))

    half = SLOTS // 2
    left, right = mm(inputs_t[0:half], w_first), mm(inputs_t[half:SLOTS], w_first)
    for parts in halves + [narrow(head)]:
        left = product(jnp.tanh(left), parts)
        right = product(jnp.tanh(right), parts)
    out_t[:, 0:half] = left.T
    out_t[:, half:SLOTS] = right.T

    for copy in mass_loads:
        copy.wait()
    pl.semaphore_wait(barrier, peers - 1)
    mass_copies = []
    for q, ((dx, dy), device) in enumerate(zip(DIRECTIONS, neighbours)):
        sy, sx, ty, tx = face(dx, dy, 2)
        kind = 0 if dy == 0 else (1 if dx == 0 else 2)
        copy = pltpu.make_async_remote_copy(
            mass_part.at[sy, sx], mass_rx.at[kind, ty, tx], mass_send.at[q], mass_recv.at[q],
            device_id=device, device_id_type=MESH,
        )
        copy.start()
        mass_copies.append(copy)

    values[0:6] = out_t[0:6]
    values[LIVE : LIVE + 1] = jnp.ones((1, SLOTS), F32)
    factor = [out_t[8 * (a + 1) : 8 * (a + 2)] for a in range(6)]
    for at, (a, b) in enumerate(PAIRS):
        values[FIRST_PAIR + at : FIRST_PAIR + at + 1] = jnp.sum(
            factor[a] * factor[b], axis=0, keepdims=True
        ) * (1.0 / 6.0)

    def spread_ready(at):
        for n in range(GROUP):
            high, low = split(values[at * GROUP + n : at * GROUP + n + 1])
            rows = onehot_r[...]
            lhs[at, n * COLUMNS : (n + 1) * COLUMNS] = rows * high
            lhs[at, (GROUP + n) * COLUMNS : (GROUP + n + 1) * COLUMNS] = rows * low

    def spread_group(at):
        if at < N_SCATTER // GROUP - 1:
            spread_ready(at + 1)
        spread = mm(lhs[at], onehot_kt[...])
        return spread[: GROUP * COLUMNS] + spread[GROUP * COLUMNS :]

    def element_rows(spread, n, g):
        start = n * COLUMNS + g * SUB
        both = spread[start : start + SUB]
        return pltpu.roll(both, 1, 0), pltpu.roll(both, 5, 0)

    def sum_copies(parity):
        copies = []
        for q, ((dx, dy), device) in enumerate(zip(DIRECTIONS, neighbours)):
            sy, sx, ty, tx = face(dx, dy, 2)
            kind = 0 if dy == 0 else (1 if dx == 0 else 2)
            copies.append(
                pltpu.make_async_remote_copy(
                    v2.at[:, sy, sx], sum_rx.at[parity, kind, :, ty, tx],
                    sum_send.at[parity, q], sum_recv.at[parity, q],
                    device_id=device, device_id_type=MESH,
                )
            )
        return copies

    def exact_copies(parity):
        copies = []
        for q, ((dx, dy), device) in enumerate(zip(DIRECTIONS, neighbours)):
            sy, sx, ty, tx = face(dx, dy, 1)
            copies.append(
                pltpu.make_async_remote_copy(
                    v1.at[:, sy, sx], copy_rx.at[parity, :, ty, tx],
                    copy_send.at[parity, q], copy_recv.at[parity, q],
                    device_id=device, device_id_type=MESH,
                )
            )
        return copies

    global_x = index_x * BX + sub - 1
    keep_x = jnp.where(
        (global_x >= 0) & (global_x < size_x * BX) & (sub < SUB - 1), 1.0, 0.0
    )
    own_planes = (sub >= 1) & (sub <= NODES_X)
    rim_planes = ((sub <= 1) & (index_x > 0)) | ((sub >= NODES_X) & (sub <= NODES_X + 1))
    halo_planes = (sub == 0) | (sub == NODES_X + 1)
    flank_low, corner_low = own_planes & (index_y > 0), rim_planes & (index_y > 0)
    valid_elements = (sub <= BX + 1) & ((sub >= 1) | (index_x > 0))

    def keep_of(row):
        global_y = index_y * BY + row - 1
        inside = jnp.where((global_y >= 0) & (global_y < size_y * BY), 1.0, 0.0)
        return keep_x * inside

    def assembled(part, received, row):
        at_rim = isinstance(row, int)
        total = jnp.zeros((SUB, NZ), F32)
        if not at_rim or 1 <= row <= NODES_Y:
            total = part + jnp.where(rim_planes, received(0), 0.0)
        if at_rim:
            flank, corner = (flank_low, corner_low) if row <= 1 else (own_planes, rim_planes)
            total = total + jnp.where(flank, received(1), 0.0) + jnp.where(corner, received(2), 0.0)
        return total

    def all_rows(body):
        for row in (0, 1, NODES_Y, NODES_Y + 1):
            body(row)

        def inner(row, carry):
            body(row)
            return carry

        by_rows(2, NODES_Y, 3, inner, 0)

    def stress_now(row):
        scale = 0.25 * modulus[row]
        base = scale * (1.0 - 0.75 * scattered[LIVE, row])
        eps_row = [strain_now[n, row] for n in range(6)]
        trace = LAME_FIRST * (eps_row[0] + eps_row[1] + eps_row[2])
        elastic = [trace + 2.0 * LAME_SECOND * eps_row[n] for n in range(3)]
        elastic += [LAME_SECOND * eps_row[n] for n in range(3, 6)]
        return [base * elastic[n] + scale * scattered[n, row] for n in range(6)]

    zero = jnp.zeros((SUB, NZ), F32)
    no_parts = [(zero, zero)] * 3

    def residual_step(row, before):
        parts = force_parts(stress_now(row - 1))
        for m in range(3):
            force = force_of(parts[m][0] + before[m][0], parts[m][1] + before[m][1])
            v2[m, row] = jnp.where(own_planes, lx[m, row] - force, 0.0)
        return [(parts[m][0], parts[m][2]) for m in range(3)]

    spread_ready(0)
    spread = spread_group(0)
    for n in range(GROUP):
        for g in range(BY // 2):
            for odd, entry in enumerate(element_rows(spread, n, g)):
                scattered[n, 2 * g + odd] = jnp.where(own_elements, entry, 0.0)
    for copy in modulus_loads + load_loads:
        copy.wait()
    last = by_rows(1, 1 + BY, 8, residual_step, no_parts)
    for m in range(3):
        v2[m, NODES_Y] = jnp.where(own_planes, lx[m, NODES_Y] - force_of(*last[m]), 0.0)

    first_copies = sum_copies(0)
    for copy in first_copies:
        copy.start()

    tangent_copies = []
    planes = slice(1, 1 + BX)
    for group in range(N_PAIRS // GROUP):
        spread = spread_group(group + 1)
        for g in range(BY // 2):
            scales = [modulus[2 * g + odd] * (1.0 / 16.0) for odd in range(2)]
            bases = [scales[odd] * (1.0 - 0.75 * scattered[LIVE, 2 * g + odd]) for odd in range(2)]
            for n in range(GROUP):
                at = group * GROUP + n
                for odd, entry in enumerate(element_rows(spread, n, g)):
                    entry = scales[odd] * entry
                    if iso(*PAIRS[at]):
                        entry = entry + bases[odd] * iso(*PAIRS[at])
                    tangent[at, 2 * g + odd + 1, planes] = entry[planes]
        entries = pl.ds(group * GROUP, GROUP)
        for q, ((dx, dy), device) in enumerate(zip(DIRECTIONS, neighbours)):
            sy, sx, ty, tx = element_face(dx, dy)
            copy = pltpu.make_async_remote_copy(
                tangent.at[entries, sy, sx], tangent.at[entries, ty, tx],
                tan_send.at[group, q], tan_recv.at[group, q],
                device_id=device, device_id_type=MESH,
            )
            copy.start()
            tangent_copies.append(copy)

    for ref in (q1, q0, d1, x):
        ref[...] = jnp.zeros_like(ref)
    for copy in mass_copies:
        copy.wait()

    def mass_row(row):
        mass_full[row] = assembled(mass_part[row], lambda kind: mass_rx[kind, row], row)

    all_rows(mass_row)
    for copy in first_copies:
        copy.wait()

    def start_row(row):
        keep = keep_of(row)
        for m in range(3):
            part = None if isinstance(row, int) and row in (0, NODES_Y + 1) else v2[m, row]
            v0[m, row] = keep * assembled(part, lambda kind: sum_rx[0, kind, m, row], row)

    all_rows(start_row)
    for copy in tangent_copies:
        copy.wait()

    def stress_row(row, strain, present):
        entries = [tangent[at, row] for at in range(N_PAIRS)]
        result = []
        for a in range(6):
            total = entries[PAIR_OF[a, 0]] * strain[0]
            for b in range(1, 6):
                total = total + entries[PAIR_OF[a, b]] * strain[b]
            result.append(jnp.where(present, total, 0.0))
        return result

    def first_image(row, carry):
        low, before = carry
        high = pairs_of(v0, row + 1)
        present = valid_elements & (row + index_y > 0)
        parts = force_parts(stress_row(row, strain_row(low, high), present))
        keep = keep_of(row)
        for m in range(3):
            force = force_of(parts[m][0] + before[m][0], parts[m][1] + before[m][1])
            v1[m, row] = keep * (force + mass_full[row] * v0[m, row])
        return high, [(parts[m][0], parts[m][2]) for m in range(3)]

    def second_image(row, carry):
        low, before, sums = carry
        high = pairs_of(v1, row + 1)
        parts = force_parts(stress_row(row, strain_row(low, high), own_elements))
        rr, r_ar, ar_ar, ar_aar = sums
        for m in range(3):
            here, image = v0[m, row], v1[m, row]
            force = force_of(parts[m][0] + before[m][0], parts[m][1] + before[m][1])
            force = force + mass_part[row] * image
            v2[m, row] = force
            rr = rr + here * here
            r_ar = r_ar + here * image
            ar_ar = ar_ar + image * image
            ar_aar = ar_aar + image * force
        return high, [(parts[m][0], parts[m][2]) for m in range(3)], (rr, r_ar, ar_ar, ar_aar)

    lane = lax.broadcasted_iota(jnp.int32, (1, 128), 1)

    def outer(step, carry):
        be0, ia1, ia0, rr_before = carry
        parity = lax.rem(step, 2)
        sum_parity = lax.rem(step + 1, 2)
        by_rows(0, BY + 2, 6, first_image, (pairs_of(v0, 0), no_parts))
        exact = exact_copies(parity)
        for copy in exact:
            copy.start()
        _, before, sums = by_rows(
            1, 1 + BY, 8, second_image, (pairs_of(v1, 1), no_parts, (zero,) * 4)
        )
        ar_aar = sums[3]
        for m in range(3):
            image = v1[m, NODES_Y]
            force = force_of(*before[m]) + mass_part[NODES_Y] * image
            v2[m, NODES_Y] = force
            ar_aar = ar_aar + jnp.where(own_planes, image * force, 0.0)
        summed = sum_copies(sum_parity)
        for copy in summed[:-FACES]:
            copy.start()

        message = jnp.zeros((1, 128), F32)
        for at, (value, mask) in enumerate(
            ((sums[0], own_elements), (sums[1], own_elements), (sums[2], own_elements), (ar_aar, own_planes))
        ):
            total = jnp.sum(jnp.where(mask, value, 0.0), axis=0, keepdims=True)
            total = jnp.sum(total, axis=1, keepdims=True)
            message = message + jnp.where(lane == at, total, 0.0)
        gathered[parity, me] = message

        for device in others:
            pltpu.make_async_remote_copy(
                gathered.at[parity, me], gathered.at[parity, me],
                all_send.at[parity], all_recv.at[parity],
                device_id=device, device_id_type=MESH,
            ).start()
        for copy in summed[-FACES:]:
            copy.start()
        for copy in exact + summed:
            copy.wait()

        def image_row(row):
            keep = keep_of(row)
            outside = isinstance(row, int) and row in (0, NODES_Y + 1)
            for m in range(3):
                rim = copy_rx[parity, m, row]
                if outside:
                    ar2 = jnp.where(sub <= NODES_X + 1, rim, 0.0)
                else:
                    ar2 = jnp.where(halo_planes, rim, v1[m, row])
                ar2 = keep * ar2
                part = None if outside else v2[m, row]
                v2[m, row] = keep * assembled(part, lambda kind: sum_rx[sum_parity, kind, m, row], row)
                v1[m, row] = ar2
                q0[m, row] = (q1[m, row] - be0 * q0[m, row] - ar2) * ia1

        all_rows(image_row)
        rest = gathered.at[parity, 0 : peers - 1]
        pltpu.make_async_copy(rest, rest, all_recv.at[parity]).wait()
        totals = [jnp.sum(gathered[parity, at : at + 16], axis=0) for at in range(0, peers, 16)]
        while len(totals) > 1:
            totals = [a + b for a, b in zip(totals[0::2], totals[1::2])]
        totals = totals[0]
        rr2, m1, m2, m3 = [
            jnp.sum(jnp.where(lane == at, totals, 0.0), axis=1, keepdims=True) for at in range(4)
        ]
        be1 = jnp.where(step == 0, 0.0, rr2 / rr_before)
        r_q1 = -rr2 * ia1
        ar_q1 = (r_q1 - m1) * ia1
        q1_q1 = (rr_before + rr2) * ia1 * ia1
        ar_q0 = rr2 * ia1 * ia0
        q1_q0 = -rr_before * ia1 * ia0
        q1_aar = ia1 * (ar_q1 - be0 * ar_q0 - m2)
        q1_aq1 = ia1 * (q1_q1 - be0 * q1_q0 - ar_q1)
        q2_q2 = m2 + 2.0 * be1 * ar_q1 + be1 * be1 * q1_q1
        ar_q2 = m2 + be1 * ar_q1
        q2_aq2 = m3 + 2.0 * be1 * q1_aar + be1 * be1 * q1_aq1
        a2 = rr2 / (m1 + be1 * r_q1)
        rr3 = a2 * a2 * q2_q2 - rr2
        be2 = rr3 / rr2
        a3 = rr3 / (m1 - 2.0 * a2 * ar_q2 + a2 * a2 * q2_aq2 - be2 * rr3 / a2)

        def update_row(row, unused):
            for m in range(3):
                ar2, old = v1[m, row], q1[m, row]
                q2 = ar2 + be1 * old
                r3 = v0[m, row] - a2 * q2
                q3 = ar2 - a2 * (v2[m, row] + be1 * q0[m, row]) + be2 * q2
                d2 = v0[m, row] + be1 * d1[m, row]
                d3 = r3 + be2 * d2
                x[m, row] = x[m, row] + (a2 * d2 + a3 * d3)
                v0[m, row] = r3 - a3 * q3
                q1[m, row] = q3
                q0[m, row] = q2
                d1[m, row] = d3
            return unused

        by_rows(0, ROWS - 1, 3, update_row, 0)
        update_row(ROWS - 1, 0)
        pltpu.make_async_copy(rest, rest, all_send.at[parity]).wait()
        return be2, 1.0 / a3, 1.0 / a2, rr3

    none = jnp.zeros((1, 1), F32)
    lax.fori_loop(0, OUTER, outer, (none, none, none, none + 1.0))

    stores = [
        pltpu.make_async_copy(
            source.at[m, 1:18, i + 1 : i + 2], target.at[i, :, m : m + 1], out_sem.at[at, m, i]
        )
        for at, (source, target) in enumerate(((x, increment_hbm), (v0, residual_hbm)))
        for i in range(NODES_X)
        for m in range(3)
    ]
    for copy in stores:
        copy.start()
    for copy in stores:
        copy.wait()


def place_kernel(increment_in, residual_in, increment_out, residual_out, held, load_sem, store_sem):
    pieces = [
        (source.at[i], held.at[at, i], target.at[i], load_sem.at[at, i], store_sem.at[at, i])
        for at, (source, target) in enumerate(((increment_in, increment_out), (residual_in, residual_out)))
        for i in range(NODES_X)
    ]
    loads = [pltpu.make_async_copy(source, slot, arrived) for source, slot, _, arrived, _ in pieces]
    stores = [pltpu.make_async_copy(slot, target, left) for _, slot, target, _, left in pieces]
    for load in loads:
        load.start()
    for load, store in zip(loads, stores):
        load.wait()
        store.start()
    for store in stores:
        store.wait()


def solution(mesh):
    size_x, size_y = mesh.shape["gx"], mesh.shape["gy"]
    peers = size_x * size_y
    field = jax.ShapeDtypeStruct((NODES_X, NODES_Y, 3, NZ), F32)

    def vmem(*shape, dtype=F32):
        return pltpu.VMEM(shape, dtype)

    def node(*lead):
        return vmem(*lead, ROWS, SUB, NZ)

    dma = pltpu.SemaphoreType.DMA
    scratch = [
        vmem(1, SLOTS, dtype=jnp.int32), vmem(1, 1, dtype=jnp.int32), vmem(6, HID), vmem(42, HID),
        node(3), node(3), node(), node(), node(3), vmem(BY, SUB, NZ), vmem(HIDDEN_LAYERS, HID, HID),
        vmem(6, BY, SUB, NZ), vmem(12 * COLUMNS, NZ), vmem(NZ, SLOTS, dtype=BF16), vmem(SLOTS, NZ, dtype=BF16),
        vmem(COLUMNS, SLOTS, dtype=BF16), vmem(SLOTS, 128, dtype=BF16),
        vmem(128, SLOTS), vmem(32, SLOTS), vmem(N_SCATTER // GROUP, 2 * GROUP * COLUMNS, SLOTS, dtype=BF16),
        vmem(GROUP, BY, SUB, NZ),
        vmem(N_PAIRS, BY + 2, SUB, NZ),
        node(3), node(3), node(3), node(3), node(3), node(3), node(3),
        node(2, 3, 3), node(2, 3), vmem(2, peers, 1, 128),
        dma((10, 5)), dma((2, 3, 5)), dma((8,)), dma((8,)), dma((3, 8)), dma((3, 8)),
        dma((2, 8)), dma((2, 8)), dma((2, 8)), dma((2, 8)), dma((2,)), dma((2,)),
    ]

    def body(u_now, load, mass, modulus, plastic_ids, plastic_count, w_in, w_hidden, w_head):
        hbm = pl.BlockSpec(memory_space=pl.ANY)
        increment, residual = pl.pallas_call(
            lambda *refs: kernel(size_x, size_y, *refs),
            out_shape=(field, field),
            in_specs=[hbm] * 9,
            out_specs=(hbm, hbm),
            scratch_shapes=scratch,
            compiler_params=pltpu.CompilerParams(
                collective_id=0, has_side_effects=True, vmem_limit_bytes=60 * 2**20
            ),
        )(
            u_now.transpose(1, 2, 0, 3), load.transpose(1, 2, 0, 3), mass, modulus,
            plastic_ids.reshape(1, SLOTS), plastic_count, w_in, w_hidden, w_head.T,
        )
        increment, residual = pl.pallas_call(
            place_kernel,
            out_shape=(field, field),
            in_specs=[hbm, hbm],
            out_specs=(hbm, hbm),
            scratch_shapes=[vmem(2, NODES_X, NODES_Y, 3, NZ), dma((2, NODES_X)), dma((2, NODES_X))],
        )(increment, residual)
        return increment.transpose(2, 0, 1, 3), residual.transpose(2, 0, 1, 3)

    split_field = P(None, "gx", "gy", None)
    split_block = P("gx", "gy", None)
    return jax.shard_map(
        body,
        mesh=mesh,
        in_specs=(
            split_field, split_field, split_block, split_block, split_block, P("gx", "gy"), P(), P(), P(),
        ),
        out_specs=(split_field, split_field),
        check_vma=False,
    )
```
